128 devices in a mesh: row: 8 (over x, y_lo), col: 16 (over y_hi, z, core).
Axes of the slice: x: 4, y: 4 (y_hi: 2, y_lo: 2; y = y_hi * 2 + y_lo), z: 4, core: 2. Of those that a mesh axis runs over, the one named last changes fastest.
Arguments:
- a_blocks: bfloat16 [8, 160, 8, 128, 128], P('row', 'col'), may hold values from -6 to 6
- a_cols: int32 [8, 160, 8], P('row', 'col'), may hold values from 0 to 19, as said below
- a_count: int32 [8, 160], P('row', 'col'), may hold values from 4 to 8
- b_blocks: bfloat16 [16, 160, 8, 128, 128], P('col', 'row'), may hold values from -0.25 to 0.25
- b_cols: int32 [16, 160, 8], P('col', 'row'), may hold values from 0 to 19, as said below
- b_count: int32 [16, 160], P('col', 'row'), may hold values from 4 to 8
- c_cols: int32 [8, 160, 12], P('row', 'col'), may hold values from 0 to 19, as said below
- c_owner: int32 [8, 1920, 1], P('row', 'col'), may hold values from 0 to 127; in each aligned block of 120 rows (0 to 119, 120 to 239, ..., all dimensions but the last counted through in order) at most 2 rows name the same one
Outputs:
- owned: bfloat16 [128, 128, 2, 128, 128], P(('row', 'col'))
The draws below stay inside these ranges and needn't reach their ends.
Inputs may be any that keep to these rules, and one draw needn't show every extreme that they name: `a_cols`: within each block row the 8 entries are distinct. `b_cols`: within each block row the 8 entries are distinct. `c_cols`: within each block row the 12 entries are distinct. `c_owner`: among the 120 entries of one device no owner appears more than 2 times, and some owner appears exactly 2 times.
All inputs are finite; a program needn't handle non-finite values.
Results may differ from the reference program's by a relative error of at most 0.001.
Values may be sent and summed in bfloat16 or wider, within the bound.
No kernel may reach another device: no remote copies, remote signals or barrier semaphores. Data moves between devices by JAX's collectives and lax.ppermute only.
A program may use at most 128 MiB of HBM per device.

```python
import math
import jax
import jax.numpy as jnp
import numpy as np
from jax import lax

BS = 128
RB = 10
SA = 8
SB = 8
FC = 12
STOPS = 2
KB = 20
NBLK = 160
PER = 2
N_ROW = 8
N_COL = 16
DEVICES = 128


def distinct_rows(key, row_total, choices_total, taken):
    scores = jax.random.randint(key, (row_total, choices_total), 0, 1 << 20) * choices_total + jnp.arange(choices_total, dtype=jnp.int32)[None, :]
    ordering = jnp.argsort(scores, axis=1, stable=True)
    return ordering[:, :taken].astype(jnp.int32)


def draw_a_cols(key, part):
    key = jax.random.fold_in(key, 11)
    return distinct_rows(key, N_ROW * NBLK, KB, SA).reshape(N_ROW, NBLK, SA)


def draw_b_cols(key, part):
    key = jax.random.fold_in(key, 23)
    return distinct_rows(key, N_COL * N_ROW * KB, KB, SB).reshape(N_COL, N_ROW * KB, SB)


def draw_c_cols(key, part):
    key = jax.random.fold_in(key, 37)
    return distinct_rows(key, N_ROW * NBLK, KB, FC).reshape(N_ROW, NBLK, FC)


def with_ends(values, own_key, low, largest):
    extent = values.shape
    spot = [jax.random.randint(jax.random.fold_in(own_key, axis), (), 0, extent[axis]) for axis in range(len(extent))]
    values = values.at[tuple(spot)].set(low)
    longest = extent.index(max(extent))
    spot[longest] = (spot[longest] + 1) % extent[longest]
    return values.at[tuple(spot)].set(largest)


def block_levels(own_key, extent, cuts, low, top_value):
    factor_of, own = 1.0, jax.random.fold_in(own_key, 6)
    for position, blocks in cuts:
        steps = jnp.exp(jax.random.uniform(jax.random.fold_in(own, position), (blocks,), jnp.float32, low / len(cuts), top_value / len(cuts)))
        factor_of = factor_of * jnp.repeat(steps, extent[position] // blocks).reshape([-1 if axis == position else 1 for axis in range(len(extent))])
    return factor_of


def assign_block(rng, own, number, rows, amount, top, most, lean):
    ranking = jax.random.permutation(rng, amount)
    crowded, common = portions_of(amount, rows * top, most, lean, True), portions_of(amount, rows * top, most, lean, False)
    places = jnp.arange(amount)

    def named(sizes, turn):
        used = int((sizes > 0).sum())
        fixed = max(1, used // 4)
        passed = fixed + (places - fixed + turn * (used - fixed)) % max(1, amount - fixed)
        return jnp.zeros((amount,), jnp.int32).at[ranking[jnp.where(places < fixed, places, passed)]].set(jnp.asarray(sizes, jnp.int32))

    sizes = jnp.where(number % 4 == 0, named(crowded, number // 4), named(common, number - number // 4 - 1))
    mixed = jax.random.permutation(jax.random.fold_in(own, 3), amount)
    source_of, receiver = mixed[0:amount // 2 * 2:2], mixed[1:amount // 2 * 2:2]
    margin = jnp.minimum(sizes[source_of] - 1, most - sizes[receiver]) // 2
    margin = jnp.where((source_of == ranking[0]) | (receiver == ranking[0]) | (sizes[receiver] == 0), 0, jnp.maximum(margin, 0))
    passed = jax.random.randint(jax.random.fold_in(own, 4), (amount // 2,), 0, 1 << 20) % (margin + 1)
    sizes = sizes.at[source_of].add(-passed).at[receiver].add(passed)
    labels = jnp.searchsorted(jnp.cumsum(sizes), jnp.arange(rows * top), side="right").astype(jnp.int32)
    listing = labels.reshape(top, rows).T
    listing = listing[jax.random.permutation(jax.random.fold_in(own, 1), rows)]
    turn = jax.random.randint(jax.random.fold_in(own, 2), (rows, 1), 0, top)
    return jnp.take_along_axis(listing, (jnp.arange(top)[None, :] + turn) % top, axis=1)


def portions_of(amount, total, reach, skew, full):
    loads = [(1 << 20) // math.isqrt(grade ** skew) + 1 for grade in range(1, amount + 1)]
    largest = reach if full else min(reach, max(-(-total // amount), total * loads[0] // sum(loads)))
    least = 1 if total - largest >= amount - 1 else 0
    given, rest = [largest] + [least] * (amount - 1), total - largest - least * (amount - 1)
    while rest > 0:
        free = [i for i in range(1, amount) if given[i] < largest] or [i for i in range(1, amount) if given[i] < reach]
        whole, budget = sum([loads[i] for i in free]), rest
        for i in free:
            more = min(reach - given[i], max(1, budget * loads[i] // whole), rest)
            given[i] = given[i] + more
            rest = rest - more
    return np.array(given)


def scatter_about(key, extent, width, bound, cuts=(), kind=jnp.bfloat16):
    result = width * jax.random.normal(key, extent, jnp.float32)
    if cuts:
        result = result * block_levels(key, extent, cuts, -0.22, 0.18)
    return jnp.clip(result, -bound, bound).astype(kind)


def setup_inputs(seed: int = 0) -> dict:
    keys = jax.random.split(jax.random.key(seed), 9)
    a_blocks = scatter_about(keys[0], (N_ROW, NBLK, SA, BS, BS), 1.0, 6.0, ((0, 8), (1, 16)))
    a_cols = draw_a_cols(jax.random.fold_in(keys[8], 71), 0)
    a_count = with_ends(jax.random.randint(keys[2], (N_ROW, NBLK), SA // 2, SA + 1), jax.random.fold_in(keys[2], 1), SA // 2, SA).astype(jnp.int32)
    b_blocks = scatter_about(keys[3], (N_COL, N_ROW * KB, SB, BS, BS), (4 * BS) ** -0.5, 0.25, ((0, 16), (1, 8)))
    b_cols = draw_b_cols(jax.random.fold_in(keys[8], 71), 0)
    b_count = with_ends(jax.random.randint(keys[5], (N_COL, N_ROW * KB), SB // 2, SB + 1), jax.random.fold_in(keys[5], 1), SB // 2, SB).astype(jnp.int32)
    c_cols = draw_c_cols(jax.random.fold_in(keys[8], 71), 0)
    c_owner_keys = jax.random.split(jax.random.fold_in(keys[7], 1), N_ROW * (NBLK * FC) // (RB * FC))
    c_owner_turns = jax.random.permutation(jax.random.fold_in(keys[7], 3), N_ROW * (NBLK * FC) // (RB * FC))
    c_owner = jax.vmap(lambda own, number: assign_block(jax.random.fold_in(keys[7], 2), own, number, RB * FC, DEVICES, 1, PER, 1))(c_owner_keys, c_owner_turns).reshape((N_ROW, NBLK * FC, 1))
    return dict(a_blocks=a_blocks, a_cols=a_cols, a_count=a_count, b_blocks=b_blocks, b_cols=b_cols, b_count=b_count, c_cols=c_cols, c_owner=c_owner)


def choose_index(first_columns, first_counts, second_columns, second_counts, filter_columns):
    slots_first = first_columns.shape[1]
    slots_second = second_columns.shape[1]
    panel_rows = second_columns.shape[0]
    lookup = (first_columns[:, :, None] == jnp.arange(panel_rows, dtype=jnp.int32)[None, None, :]).astype(jnp.int32)
    stored = jnp.sum(lookup[:, :, :, None] * second_columns[None, None, :, :], axis=2, dtype=jnp.int32)
    stored_counts = jnp.sum(lookup * second_counts[None, None, :], axis=2, dtype=jnp.int32)
    live_first = jnp.arange(slots_first, dtype=jnp.int32)[None, :] < first_counts[:, None]
    live_second = jnp.arange(slots_second, dtype=jnp.int32)[None, None, :] < stored_counts[:, :, None]
    matches = (stored[:, :, :, None] == filter_columns[:, None, None, :]) & live_second[:, :, :, None] & live_first[:, :, None, None]
    flat_index = first_columns[:, :, None] * slots_second + jnp.arange(slots_second, dtype=jnp.int32)[None, None, :]
    picked = jnp.sum(jnp.where(matches, flat_index[:, :, :, None], 0), axis=2, dtype=jnp.int32)
    return jnp.where(jnp.any(matches, axis=2), picked, panel_rows * slots_second).astype(jnp.int32)


def stop_product(first_blocks, first_columns, first_counts, second_blocks, second_columns, second_counts, filter_columns):
    index = choose_index(first_columns, first_counts, second_columns, second_counts, filter_columns)
    side = second_blocks.shape[2]
    flat_blocks = jnp.concatenate([second_blocks.reshape(-1, side, side), jnp.zeros((1, side, side), second_blocks.dtype)], axis=0)
    chosen = flat_blocks[index].astype(jnp.float32)
    return jnp.einsum("iapq,iafqr->ifpr", first_blocks.astype(jnp.float32), chosen)


def slot_sources(owners, devices, per_owner):
    length = owners.shape[0]
    positions = jnp.arange(length, dtype=jnp.int32)
    earlier = (owners[:, None] == owners[None, :]) & (positions[None, :] < positions[:, None])
    ranks = jnp.sum(earlier, axis=1, dtype=jnp.int32)
    slots = (owners * per_owner + ranks).astype(jnp.int32)
    return jnp.full((devices * per_owner,), length, jnp.int32).at[slots].set(positions)


def pick_panel(array, major, start, length):
    whole = lax.dynamic_index_in_dim(array, major, 0, keepdims=False)
    return lax.dynamic_slice_in_dim(whole, start, length, 0)


def reference(a_blocks, a_cols, a_count, b_blocks, b_cols, b_count, c_cols, c_owner):
    def one_device(device):
        grid_row = (device // N_COL).astype(jnp.int32)
        grid_col = (device % N_COL).astype(jnp.int32)
        first_start = (grid_col * RB).astype(jnp.int32)
        second_start = (grid_row * KB).astype(jnp.int32)
        filter_columns = pick_panel(c_cols, grid_row, first_start, RB)
        total = jnp.zeros((RB, FC, BS, BS), jnp.float32)
        for stop in range(STOPS):
            first_major = ((grid_row + stop) % N_ROW).astype(jnp.int32)
            second_major = ((grid_col + stop) % N_COL).astype(jnp.int32)
            total = total + stop_product(
                pick_panel(a_blocks, first_major, first_start, RB),
                pick_panel(a_cols, first_major, first_start, RB),
                pick_panel(a_count, first_major, first_start, RB),
                pick_panel(b_blocks, second_major, second_start, KB),
                pick_panel(b_cols, second_major, second_start, KB),
                pick_panel(b_count, second_major, second_start, KB),
                filter_columns)
        product = total.astype(jnp.bfloat16).reshape(RB * FC, BS, BS)
        owners = pick_panel(c_owner, grid_row, (grid_col * RB * FC).astype(jnp.int32), RB * FC)[:, 0]
        sources = slot_sources(owners, DEVICES, PER)
        padded = jnp.concatenate([product, jnp.zeros((1, BS, BS), jnp.bfloat16)], axis=0)
        return padded[sources].reshape(DEVICES, PER, BS, BS)

    sent = lax.map(one_device, jnp.arange(DEVICES, dtype=jnp.int32))
    return jnp.swapaxes(sent, 0, 1)
```

```python
import functools

import jax
import jax.numpy as jnp
from jax import lax
from jax.experimental import pallas as pl
from jax.experimental.pallas import tpu as pltpu
from jax.sharding import PartitionSpec as P

VMEM_LIMIT = 40 * 1024 * 1024
TABLE_ROWS = 20


def move(value, chosen):
    rows, cols = lax.axis_size("row"), lax.axis_size("col")
    pairs = []
    for r in range(rows):
        for c in range(cols):
            to = chosen(r, c)
            if to is not None:
                pairs.append((r * cols + c, (to[0] % rows) * cols + to[1] % cols))
    return lax.ppermute(value, ("row", "col"), pairs)


def flat_meta(columns, counts):
    return jnp.concatenate([columns.reshape(-1), counts])


def fill_table(table, meta, slots, width):
    panel_rows = meta.shape[0] // (slots + 1)
    blank = panel_rows * slots

    def clear(n, carry):
        table[n] = blank
        return carry

    lax.fori_loop(0, table.shape[0], clear, 0, unroll=width)
    for k in range(panel_rows):
        count = meta[blank + k]
        for b in range(slots):
            block = k * slots + b
            table[k * width + meta[block]] = jnp.where(b < count, block, blank)


def load_second(second, held, sem):
    total = second.shape[0]
    copy = pltpu.make_async_copy(second, held.at[pl.ds(0, total)], sem)
    copy.start()
    held[total] = jnp.zeros(held.shape[1:], held.dtype)
    return copy


def row_starts(meta, i, slots, width):
    row_total = meta.shape[0] // (slots + 1)
    count = meta[row_total * slots + i]
    return [
        jnp.where(a < count, meta[i * slots + a] * width, TABLE_ROWS * width) for a in range(slots)
    ]


def pair_product(starts, table, columns, first, held):
    slots = first.shape[1]
    row = jnp.concatenate([first[0, a] for a in range(slots)], axis=1)
    picked = [
        jnp.concatenate([held[table[start + column]] for start in starts], axis=0)
        for column in columns
    ]
    return jnp.dot(row, jnp.concatenate(picked, axis=1), preferred_element_type=jnp.float32)


def first_stop_kernel(
    first_meta, second_meta, kept_columns, first, second,
    total, blank, table, held, zeros, held_sem, blank_sem,
):
    i = pl.program_id(0)
    kept, side = total.shape[1], total.shape[2]
    slots = first.shape[1]
    width = table.shape[0] // (TABLE_ROWS + 1)
    part = zeros.shape[0]

    @pl.when(i == 0)
    def _():
        copy = load_second(second, held, held_sem)
        zeros[...] = jnp.zeros(zeros.shape, zeros.dtype)
        for j in range(blank.shape[0] // part):
            pltpu.make_async_copy(zeros, blank.at[pl.ds(j * part, part)], blank_sem).start()
        fill_table(table, second_meta, slots, width)
        copy.wait()

    starts = row_starts(first_meta, i, slots, width)
    for f in range(0, kept, 2):
        columns = [kept_columns[i * kept + f + g] for g in range(2)]
        both = pair_product(starts, table, columns, first, held)
        total[0, f] = both[:, :side]
        total[0, f + 1] = both[:, side:]

    @pl.when(i == pl.num_programs(0) - 1)
    def _():
        pltpu.make_async_copy(blank, blank, blank_sem).wait()


def last_stop_kernel(
    first_meta, second_meta, kept_columns, owner, place,
    early, late, before, second, part_a, part_b, part_c, blank,
    out, table, used, held, rows, product, held_sem, row_sem, out_sem,
):
    del blank
    i = pl.program_id(0)
    kept, side = before.shape[1], before.shape[2]
    width = table.shape[0] // (TABLE_ROWS + 1)
    per_owner = out.shape[0] // used.shape[0]
    row_total, slots = rows.shape[0], rows.shape[1]
    total = held.shape[0] - 1

    @pl.when(i == 0)
    def _():
        whole = held.at[pl.ds(0, total)]

        @pl.when(place[0] == 0)
        def _():
            pltpu.make_async_copy(second, whole, held_sem).start()

        @pl.when(place[0] != 0)
        def _():
            at = 0
            for part in (part_a, part_b, part_c):
                span = pl.ds(at, part.shape[0])
                pltpu.make_async_copy(part, held.at[span], held_sem).start()
                at += part.shape[0]

        @pl.when(place[1] == 0)
        def _():
            for j in range(row_total):
                pltpu.make_async_copy(early.at[j], rows.at[j], row_sem.at[j]).start()

        @pl.when(place[1] != 0)
        def _():
            for j in range(row_total):
                pltpu.make_async_copy(late.at[j], rows.at[j], row_sem.at[j]).start()

        held[total] = jnp.zeros(held.shape[1:], held.dtype)

        def clear(n, carry):
            used[n] = 0
            return carry

        lax.fori_loop(0, used.shape[0], clear, 0, unroll=16)
        fill_table(table, second_meta, slots, width)
        pltpu.make_async_copy(whole, whole, held_sem).wait()

    pltpu.make_async_copy(rows.at[i], rows.at[i], row_sem.at[i]).wait()
    first = rows.at[pl.ds(i, 1)]
    starts = row_starts(first_meta, i, slots, width)
    for f in range(0, kept, 2):
        columns = [kept_columns[i * kept + f + g] for g in range(2)]
        both = pair_product(starts, table, columns, first, held)
        for g in range(2):
            l = i * kept + f + g
            value = both[:, g * side:(g + 1) * side] + before[0, f + g]
            product[l] = value.astype(product.dtype)
            rank = used[owner[l]]
            used[owner[l]] = rank + 1
            slot = owner[l] * per_owner + rank
            pltpu.make_async_copy(product.at[l], out.at[slot], out_sem).start()

    @pl.when(i == pl.num_programs(0) - 1)
    def _():
        pltpu.make_async_copy(product, out.at[pl.ds(0, product.shape[0])], out_sem).wait()


def first_stop(first_meta, second_meta, kept_columns, first, second, outgoing):
    rows, slots, side, _ = first.shape
    kept = kept_columns.shape[0] // rows
    second_total = second.shape[0]
    part = 16
    return pl.pallas_call(
        first_stop_kernel,
        grid_spec=pltpu.PrefetchScalarGridSpec(
            num_scalar_prefetch=3,
            grid=(rows,),
            in_specs=[
                pl.BlockSpec((1, slots, side, side), lambda i, *_: (i, 0, 0, 0)),
                pl.BlockSpec(memory_space=pl.ANY),
            ],
            out_specs=[
                pl.BlockSpec((1, kept, side, side), lambda i, *_: (i, 0, 0, 0)),
                pl.BlockSpec(memory_space=pl.ANY),
            ],
            scratch_shapes=[
                pltpu.SMEM(((TABLE_ROWS + 1) * TABLE_ROWS,), jnp.int32),
                pltpu.VMEM((second_total + 1, side, side), second.dtype),
                pltpu.VMEM((part, side, side), second.dtype),
                pltpu.SemaphoreType.DMA,
                pltpu.SemaphoreType.DMA,
            ],
        ),
        out_shape=[
            jax.ShapeDtypeStruct((rows, kept, side, side), jnp.float32),
            jax.ShapeDtypeStruct((outgoing, side, side), second.dtype),
        ],
        compiler_params=pltpu.CompilerParams(vmem_limit_bytes=62 * 1024 * 1024),
        cost_estimate=pl.CostEstimate(
            flops=4 * rows * slots * kept * side**3,
            bytes_accessed=2 * (rows * (slots * 2 + kept * 4) + 2 * second_total) * side**2,
            transcendentals=0,
        ),
    )(first_meta, second_meta, kept_columns, first, second)


def last_stop(
    first_meta, second_meta, kept_columns, owner, place,
    early, late, before, second, part_a, part_b, part_c, blank, owners,
):
    rows, slots, side, _ = early.shape
    kept = before.shape[1]
    second_total = second.shape[0]
    return pl.pallas_call(
        last_stop_kernel,
        grid_spec=pltpu.PrefetchScalarGridSpec(
            num_scalar_prefetch=5,
            grid=(rows,),
            in_specs=[
                pl.BlockSpec(memory_space=pl.ANY),
                pl.BlockSpec(memory_space=pl.ANY),
                pl.BlockSpec((1, kept, side, side), lambda i, *_: (i, 0, 0, 0)),
                pl.BlockSpec(memory_space=pl.ANY),
                pl.BlockSpec(memory_space=pl.ANY),
                pl.BlockSpec(memory_space=pl.ANY),
                pl.BlockSpec(memory_space=pl.ANY),
                pl.BlockSpec(memory_space=pl.ANY),
            ],
            out_specs=pl.BlockSpec(memory_space=pl.ANY),
            scratch_shapes=[
                pltpu.SMEM(((TABLE_ROWS + 1) * TABLE_ROWS,), jnp.int32),
                pltpu.SMEM((owners,), jnp.int32),
                pltpu.VMEM((second_total + 1, side, side), second.dtype),
                pltpu.VMEM(early.shape, early.dtype),
                pltpu.VMEM((rows * kept, side, side), second.dtype),
                pltpu.SemaphoreType.DMA,
                pltpu.SemaphoreType.DMA((rows,)),
                pltpu.SemaphoreType.DMA,
            ],
        ),
        out_shape=jax.ShapeDtypeStruct(blank.shape, blank.dtype),
        input_output_aliases={12: 0},
        compiler_params=pltpu.CompilerParams(vmem_limit_bytes=VMEM_LIMIT),
        cost_estimate=pl.CostEstimate(flops=1024, bytes_accessed=1024, transcendentals=0),
    )(
        first_meta, second_meta, kept_columns, owner, place,
        early, late, before, second, part_a, part_b, part_c, blank,
    )


def cut_kernel(place, source, *rest):
    targets, sem = rest[:-1], rest[-1]

    @pl.when(place[0] != 0)
    def _():
        copies, at = [], 0
        for n, target in enumerate(targets):
            piece = source.at[pl.ds(at, target.shape[0])]
            copies.append(pltpu.make_async_copy(piece, target, sem.at[n]))
            at += target.shape[0]
        for copy in copies:
            copy.start()
        for copy in copies:
            copy.wait()


def cut(place, value, sizes):
    return pl.pallas_call(
        cut_kernel,
        in_specs=[pl.BlockSpec(memory_space=pltpu.SMEM), pl.BlockSpec(memory_space=pl.ANY)],
        out_specs=[pl.BlockSpec(memory_space=pl.ANY)] * len(sizes),
        out_shape=[jax.ShapeDtypeStruct((size,) + value.shape[1:], value.dtype) for size in sizes],
        scratch_shapes=[pltpu.SemaphoreType.DMA((len(sizes),))],
        compiler_params=pltpu.CompilerParams(vmem_limit_bytes=VMEM_LIMIT),
        cost_estimate=pl.CostEstimate(flops=1024, bytes_accessed=1024, transcendentals=0),
    )(place, value)


def copy_kernel(parts, source, target, sem):
    size = source.shape[0] // parts
    for j in range(parts):
        piece = pl.ds(j * size, size)
        pltpu.make_async_copy(source.at[piece], target.at[piece], sem).start()
    pltpu.make_async_copy(source, target, sem).wait()


def hand_over(value):
    return pl.pallas_call(
        functools.partial(copy_kernel, 16),
        in_specs=[pl.BlockSpec(memory_space=pl.ANY)],
        out_specs=pl.BlockSpec(memory_space=pl.ANY),
        out_shape=jax.ShapeDtypeStruct(value.shape, value.dtype),
        scratch_shapes=[pltpu.SemaphoreType.DMA],
        compiler_params=pltpu.CompilerParams(vmem_limit_bytes=VMEM_LIMIT),
    )(value)


def on_device(a_blocks, a_cols, a_count, b_blocks, b_cols, b_count, c_cols, c_owner):
    devices = lax.axis_size("row") * lax.axis_size("col")
    span = lax.axis_size("col") // 2
    rows, kept = c_cols.shape[1], c_cols.shape[2]
    side = a_blocks.shape[3]
    per_owner = max(2, 3 * rows * kept // (2 * devices))
    first = a_blocks[0]
    second = b_blocks[0].reshape(-1, side, side)
    total = second.shape[0]
    large = total * 9 // 20
    spot = lax.axis_index("col") % span
    crossing = (spot == 0).astype(jnp.int32)[None]

    def near(r, c):
        return r ^ 1, c

    def far(r, c):
        return r ^ 1, c + span

    def to_last(r, c):
        return r, c + span - 1

    def at(place, step):
        return lambda r, c: step(r, c) if c % span == place else None

    part_a, part_b, part_c = cut(crossing, second, (large, large, total - 2 * large))
    part_a = move(part_a, at(0, near))
    part_b = move(part_b, at(0, to_last))
    part_c = move(part_c, at(0, lambda r, c: (r, c - 1)))
    early = move(first, lambda r, c: (r - 1, c) if c % span > 1 else None)
    second_next = move(second, lambda r, c: (r, c - 1) if c % span else None)

    own_first_meta = flat_meta(a_cols[0], a_count[0])
    own_second_meta = flat_meta(b_cols[0], b_count[0])
    kept_columns = c_cols[0].reshape(-1)
    owner = c_owner[0, :, 0]
    before, blank = first_stop(
        own_first_meta, own_second_meta, kept_columns, first, second, devices * per_owner
    )

    part_a, part_b, part_c, first, before, blank = lax.optimization_barrier(
        (part_a, part_b, part_c, first, before, blank)
    )
    late = move(first, lambda r, c: (r - 1, c) if c % span < 2 else None)
    part_a = move(part_a, at(0, far))
    part_b = move(part_b, at(span - 1, far))

    part_a, part_b, early, second_next, first_meta, second_meta = lax.optimization_barrier(
        (part_a, part_b, early, second_next, own_first_meta, own_second_meta)
    )
    part_a = move(part_a, at(0, to_last))
    part_b = move(part_b, at(span - 1, near))
    first_meta = move(first_meta, lambda r, c: (r - 1, c))
    second_meta = move(second_meta, lambda r, c: (r, c - 1))

    place = jnp.stack([spot == span - 1, spot < 2]).astype(jnp.int32)
    outgoing = last_stop(
        first_meta, second_meta, kept_columns, owner, place,
        early, late, before, second_next, part_a, part_b, part_c, blank, devices,
    )
    arrived = lax.all_to_all(
        outgoing.reshape(devices, per_owner, side, side),
        ("row", "col"),
        split_axis=0,
        concat_axis=0,
        tiled=True,
    )
    return hand_over(arrived).reshape(1, devices, per_owner, side, side)


def solution(mesh):
    return jax.shard_map(
        on_device,
        mesh=mesh,
        in_specs=(
            P("row", "col", None, None, None),
            P("row", "col", None),
            P("row", "col"),
            P("col", "row", None, None, None),
            P("col", "row", None),
            P("col", "row"),
            P("row", "col", None),
            P("row", "col", None),
        ),
        out_specs=P(("row", "col"), None, None, None, None),
        check_vma=False,
    )
```

```python
import functools

import jax
import jax.numpy as jnp
from jax import lax
from jax.experimental import pallas as pl
from jax.experimental.pallas import tpu as pltpu
from jax.sharding import PartitionSpec as P

VMEM_LIMIT = 40 * 1024 * 1024
LARGE_VMEM_LIMIT = 62 * 1024 * 1024
TABLE_ROWS = 20


def move(value, chosen):
    rows, cols = lax.axis_size("row"), lax.axis_size("col")
    pairs = []
    for r in range(rows):
        for c in range(cols):
            to = chosen(r, c)
            if to is not None:
                pairs.append((r * cols + c, (to[0] % rows) * cols + to[1] % cols))
    return lax.ppermute(value, ("row", "col"), pairs)


def flat_meta(columns, counts):
    return jnp.concatenate([columns.reshape(-1), counts])


def fill_table(table, meta, slots, width):
    panel_rows = meta.shape[0] // (slots + 1)
    blank = panel_rows * slots

    def clear(n, carry):
        table[n] = blank
        return carry

    lax.fori_loop(0, table.shape[0], clear, 0, unroll=width)
    for k in range(panel_rows):
        count = meta[blank + k]
        for b in range(slots):
            block = k * slots + b
            table[k * width + meta[block]] = jnp.where(b < count, block, blank)


def load_second(second, held, sem):
    total = second.shape[0]
    copy = pltpu.make_async_copy(second, held.at[pl.ds(0, total)], sem)
    copy.start()
    held[total] = jnp.zeros(held.shape[1:], held.dtype)
    return copy


def row_starts(meta, i, slots, width):
    row_total = meta.shape[0] // (slots + 1)
    count = meta[row_total * slots + i]
    return [
        jnp.where(a < count, meta[i * slots + a] * width, TABLE_ROWS * width) for a in range(slots)
    ]


def pair_product(starts, table, columns, first, held):
    slots = first.shape[1]
    row = jnp.concatenate([first[0, a] for a in range(slots)], axis=1)
    picked = [
        jnp.concatenate([held[table[start + column]] for start in starts], axis=0)
        for column in columns
    ]
    return jnp.dot(row, jnp.concatenate(picked, axis=1), preferred_element_type=jnp.float32)


def first_stop_kernel(
    first_meta, second_meta, kept_columns, first, second,
    total, blank, table, held, zeros, held_sem, blank_sem,
):
    i = pl.program_id(0)
    kept, side = total.shape[1], total.shape[2]
    slots = first.shape[1]
    width = table.shape[0] // (TABLE_ROWS + 1)
    part = zeros.shape[0]

    @pl.when(i == 0)
    def _():
        copy = load_second(second, held, held_sem)
        zeros[...] = jnp.zeros(zeros.shape, zeros.dtype)
        for j in range(blank.shape[0] // part):
            pltpu.make_async_copy(zeros, blank.at[pl.ds(j * part, part)], blank_sem).start()
        fill_table(table, second_meta, slots, width)
        copy.wait()

    starts = row_starts(first_meta, i, slots, width)
    for f in range(0, kept, 2):
        columns = [kept_columns[i * kept + f + g] for g in range(2)]
        both = pair_product(starts, table, columns, first, held)
        total[0, f] = both[:, :side]
        total[0, f + 1] = both[:, side:]

    @pl.when(i == pl.num_programs(0) - 1)
    def _():
        pltpu.make_async_copy(blank, blank, blank_sem).wait()


def last_stop_kernel(
    first_meta, second_meta, kept_columns, owner, place,
    early, late, before, second, part_a, part_b, part_c, blank,
    out, table, used, held, rows, product, held_sem, row_sem, out_sem,
):
    del blank
    i = pl.program_id(0)
    kept, side = before.shape[1], before.shape[2]
    width = table.shape[0] // (TABLE_ROWS + 1)
    per_owner = out.shape[0] // used.shape[0]
    row_total, slots = rows.shape[0], rows.shape[1]
    total = held.shape[0] - 1

    @pl.when(i == 0)
    def _():
        whole = held.at[pl.ds(0, total)]

        @pl.when(place[0] == 0)
        def _():
            pltpu.make_async_copy(second, whole, held_sem).start()

        @pl.when(place[0] != 0)
        def _():
            at = 0
            for part in (part_a, part_b, part_c):
                span = pl.ds(at, part.shape[0])
                pltpu.make_async_copy(part, held.at[span], held_sem).start()
                at += part.shape[0]

        @pl.when(place[1] == 0)
        def _():
            for j in range(row_total):
                pltpu.make_async_copy(early.at[j], rows.at[j], row_sem.at[j]).start()

        @pl.when(place[1] != 0)
        def _():
            for j in range(row_total):
                pltpu.make_async_copy(late.at[j], rows.at[j], row_sem.at[j]).start()

        held[total] = jnp.zeros(held.shape[1:], held.dtype)

        def clear(n, carry):
            used[n] = 0
            return carry

        lax.fori_loop(0, used.shape[0], clear, 0, unroll=16)
        fill_table(table, second_meta, slots, width)
        pltpu.make_async_copy(whole, whole, held_sem).wait()

    pltpu.make_async_copy(rows.at[i], rows.at[i], row_sem.at[i]).wait()
    first = rows.at[pl.ds(i, 1)]
    starts = row_starts(first_meta, i, slots, width)
    for f in range(0, kept, 2):
        columns = [kept_columns[i * kept + f + g] for g in range(2)]
        both = pair_product(starts, table, columns, first, held)
        for g in range(2):
            l = i * kept + f + g
            value = both[:, g * side:(g + 1) * side] + before[0, f + g]
            product[l] = value.astype(product.dtype)
            rank = used[owner[l]]
            used[owner[l]] = rank + 1
            slot = owner[l] * per_owner + rank
            pltpu.make_async_copy(product.at[l], out.at[slot], out_sem).start()

    @pl.when(i == pl.num_programs(0) - 1)
    def _():
        pltpu.make_async_copy(product, out.at[pl.ds(0, product.shape[0])], out_sem).wait()


def first_stop(first_meta, second_meta, kept_columns, first, second, outgoing):
    rows, slots, side, _ = first.shape
    kept = kept_columns.shape[0] // rows
    second_total = second.shape[0]
    part = 16
    return pl.pallas_call(
        first_stop_kernel,
        grid_spec=pltpu.PrefetchScalarGridSpec(
            num_scalar_prefetch=3,
            grid=(rows,),
            in_specs=[
                pl.BlockSpec((1, slots, side, side), lambda i, *_: (i, 0, 0, 0)),
                pl.BlockSpec(memory_space=pl.ANY),
            ],
            out_specs=[
                pl.BlockSpec((1, kept, side, side), lambda i, *_: (i, 0, 0, 0)),
                pl.BlockSpec(memory_space=pl.ANY),
            ],
            scratch_shapes=[
                pltpu.SMEM(((TABLE_ROWS + 1) * TABLE_ROWS,), jnp.int32),
                pltpu.VMEM((second_total + 1, side, side), second.dtype),
                pltpu.VMEM((part, side, side), second.dtype),
                pltpu.SemaphoreType.DMA,
                pltpu.SemaphoreType.DMA,
            ],
        ),
        out_shape=[
            jax.ShapeDtypeStruct((rows, kept, side, side), jnp.float32),
            jax.ShapeDtypeStruct((outgoing, side, side), second.dtype),
        ],
        compiler_params=pltpu.CompilerParams(vmem_limit_bytes=LARGE_VMEM_LIMIT),
        cost_estimate=pl.CostEstimate(
            flops=4 * rows * slots * kept * side**3,
            bytes_accessed=2 * (rows * (slots * 2 + kept * 4) + 2 * second_total) * side**2,
            transcendentals=0,
        ),
    )(first_meta, second_meta, kept_columns, first, second)


def last_stop(
    first_meta, second_meta, kept_columns, owner, place,
    early, late, before, second, part_a, part_b, part_c, blank, owners,
):
    rows, slots, side, _ = early.shape
    kept = before.shape[1]
    second_total = second.shape[0]
    return pl.pallas_call(
        last_stop_kernel,
        grid_spec=pltpu.PrefetchScalarGridSpec(
            num_scalar_prefetch=5,
            grid=(rows,),
            in_specs=[
                pl.BlockSpec(memory_space=pl.ANY),
                pl.BlockSpec(memory_space=pl.ANY),
                pl.BlockSpec((1, kept, side, side), lambda i, *_: (i, 0, 0, 0)),
                pl.BlockSpec(memory_space=pl.ANY),
                pl.BlockSpec(memory_space=pl.ANY),
                pl.BlockSpec(memory_space=pl.ANY),
                pl.BlockSpec(memory_space=pl.ANY),
                pl.BlockSpec(memory_space=pl.ANY),
            ],
            out_specs=pl.BlockSpec(memory_space=pl.ANY),
            scratch_shapes=[
                pltpu.SMEM(((TABLE_ROWS + 1) * TABLE_ROWS,), jnp.int32),
                pltpu.SMEM((owners,), jnp.int32),
                pltpu.VMEM((second_total + 1, side, side), second.dtype),
                pltpu.VMEM(early.shape, early.dtype),
                pltpu.VMEM((rows * kept, side, side), second.dtype),
                pltpu.SemaphoreType.DMA,
                pltpu.SemaphoreType.DMA((rows,)),
                pltpu.SemaphoreType.DMA,
            ],
        ),
        out_shape=jax.ShapeDtypeStruct(blank.shape, blank.dtype),
        input_output_aliases={12: 0},
        compiler_params=pltpu.CompilerParams(vmem_limit_bytes=VMEM_LIMIT),
        cost_estimate=pl.CostEstimate(flops=1024, bytes_accessed=1024, transcendentals=0),
    )(
        first_meta, second_meta, kept_columns, owner, place,
        early, late, before, second, part_a, part_b, part_c, blank,
    )


def cut_kernel(place, source, *rest):
    held, in_sem, out_sem = rest[-3:]
    targets = rest[:-3]

    @pl.when(place[0] != 0)
    def _():
        loads, stores, at = [], [], 0
        for n, target in enumerate(targets):
            piece = pl.ds(at, target.shape[0])
            loads.append(pltpu.make_async_copy(source.at[piece], held.at[piece], in_sem.at[n]))
            stores.append(pltpu.make_async_copy(held.at[piece], target, out_sem.at[n]))
            at += target.shape[0]
        for load in loads:
            load.start()
        for load, store in zip(loads, stores):
            load.wait()
            store.start()
        for store in stores:
            store.wait()


def cut(place, value, sizes):
    return pl.pallas_call(
        cut_kernel,
        in_specs=[pl.BlockSpec(memory_space=pltpu.SMEM), pl.BlockSpec(memory_space=pl.ANY)],
        out_specs=[pl.BlockSpec(memory_space=pl.ANY)] * len(sizes),
        out_shape=[jax.ShapeDtypeStruct((size,) + value.shape[1:], value.dtype) for size in sizes],
        scratch_shapes=[
            pltpu.VMEM(value.shape, value.dtype),
            pltpu.SemaphoreType.DMA((len(sizes),)),
            pltpu.SemaphoreType.DMA((len(sizes),)),
        ],
        compiler_params=pltpu.CompilerParams(vmem_limit_bytes=LARGE_VMEM_LIMIT),
        cost_estimate=pl.CostEstimate(flops=1024, bytes_accessed=1024, transcendentals=0),
    )(place, value)


def copy_kernel(parts, source, target, sem):
    size = source.shape[0] // parts
    for j in range(parts):
        piece = pl.ds(j * size, size)
        pltpu.make_async_copy(source.at[piece], target.at[piece], sem).start()
    pltpu.make_async_copy(source, target, sem).wait()


def hand_over(value):
    return pl.pallas_call(
        functools.partial(copy_kernel, 16),
        in_specs=[pl.BlockSpec(memory_space=pl.ANY)],
        out_specs=pl.BlockSpec(memory_space=pl.ANY),
        out_shape=jax.ShapeDtypeStruct(value.shape, value.dtype),
        scratch_shapes=[pltpu.SemaphoreType.DMA],
        compiler_params=pltpu.CompilerParams(vmem_limit_bytes=VMEM_LIMIT),
    )(value)


def on_device(a_blocks, a_cols, a_count, b_blocks, b_cols, b_count, c_cols, c_owner):
    devices = lax.axis_size("row") * lax.axis_size("col")
    span = lax.axis_size("col") // 2
    rows, kept = c_cols.shape[1], c_cols.shape[2]
    side = a_blocks.shape[3]
    per_owner = max(2, 3 * rows * kept // (2 * devices))
    first = a_blocks[0]
    second = b_blocks[0].reshape(-1, side, side)
    total = second.shape[0]
    large = total * 17 // 40
    spot = lax.axis_index("col") % span
    crossing = (spot == 0).astype(jnp.int32)[None]

    def near(r, c):
        return r ^ 1, c

    def far(r, c):
        return r ^ 1, c + span

    def to_last(r, c):
        return r, c + span - 1

    middle = span - 3

    def at(place, step):
        return lambda r, c: step(r, c) if c % span == place else None

    part_a, part_b, part_c = cut(crossing, second, (large, large, total - 2 * large))
    part_a = move(part_a, at(0, near))
    part_b = move(part_b, at(0, to_last))
    part_c = move(part_c, at(0, lambda r, c: far(r, c + middle)))
    early = move(first, lambda r, c: (r - 1, c) if c % span > 1 else None)
    second_next = move(second, lambda r, c: (r, c - 1) if c % span else None)

    own_first_meta = flat_meta(a_cols[0], a_count[0])
    own_second_meta = flat_meta(b_cols[0], b_count[0])
    kept_columns = c_cols[0].reshape(-1)
    owner = c_owner[0, :, 0]
    before, blank = first_stop(
        own_first_meta, own_second_meta, kept_columns, first, second, devices * per_owner
    )

    part_a, part_b, part_c, first, before, blank = lax.optimization_barrier(
        (part_a, part_b, part_c, first, before, blank)
    )
    late = move(first, lambda r, c: (r - 1, c) if c % span < 2 else None)
    part_a = move(part_a, at(0, far))
    part_b = move(part_b, at(span - 1, far))

    part_a, part_b, part_c, early, second_next, first_meta = lax.optimization_barrier(
        (part_a, part_b, part_c, early, second_next, own_first_meta)
    )
    part_a = move(part_a, at(0, to_last))
    part_b = move(part_b, at(span - 1, near))
    part_c = move(part_c, at(middle, near))
    first_meta = move(first_meta, lambda r, c: (r - 1, c))

    part_c, second_meta = lax.optimization_barrier((part_c, own_second_meta))
    part_c = move(part_c, at(middle, lambda r, c: (r, c + 2)))
    second_meta = move(second_meta, lambda r, c: (r, c - 1))

    place = jnp.stack([spot == span - 1, spot < 2]).astype(jnp.int32)
    outgoing = last_stop(
        first_meta, second_meta, kept_columns, owner, place,
        early, late, before, second_next, part_a, part_b, part_c, blank, devices,
    )
    arrived = lax.all_to_all(
        outgoing.reshape(devices, per_owner, side, side),
        ("row", "col"),
        split_axis=0,
        concat_axis=0,
        tiled=True,
    )
    return hand_over(arrived).reshape(1, devices, per_owner, side, side)


def solution(mesh):
    return jax.shard_map(
        on_device,
        mesh=mesh,
        in_specs=(
            P("row", "col", None, None, None),
            P("row", "col", None),
            P("row", "col"),
            P("col", "row", None, None, None),
            P("col", "row", None),
            P("col", "row"),
            P("row", "col", None),
            P("row", "col", None),
        ),
        out_specs=P(("row", "col"), None, None, None, None),
        check_vma=False,
    )
```

```python
import functools

import jax
import jax.numpy as jnp
from jax import lax
from jax.experimental import pallas as pl
from jax.experimental.pallas import tpu as pltpu
from jax.sharding import PartitionSpec as P

VMEM_LIMIT = 40 * 1024 * 1024
LARGE_VMEM_LIMIT = 62 * 1024 * 1024
TABLE_ROWS = 20


def move(value, chosen):
    rows, cols = lax.axis_size("row"), lax.axis_size("col")
    pairs = []
    for r in range(rows):
        for c in range(cols):
            to = chosen(r, c)
            if to is not None:
                pairs.append((r * cols + c, (to[0] % rows) * cols + to[1] % cols))
    return lax.ppermute(value, ("row", "col"), pairs)


def flat_meta(columns, counts):
    return jnp.concatenate([columns.reshape(-1), counts])


def fill_table(table, meta, slots, width):
    panel_rows = meta.shape[0] // (slots + 1)
    blank = panel_rows * slots

    def clear(n, carry):
        table[n] = blank
        return carry

    lax.fori_loop(0, table.shape[0], clear, 0, unroll=width)
    for k in range(panel_rows):
        count = meta[blank + k]
        for b in range(slots):
            block = k * slots + b
            table[k * width + meta[block]] = jnp.where(b < count, block, blank)


def load_second(second, held, sem):
    total = second.shape[0]
    copy = pltpu.make_async_copy(second, held.at[pl.ds(0, total)], sem)
    copy.start()
    held[total] = jnp.zeros(held.shape[1:], held.dtype)
    return copy


def row_starts(meta, i, slots, width):
    row_total = meta.shape[0] // (slots + 1)
    count = meta[row_total * slots + i]
    return [
        jnp.where(a < count, meta[i * slots + a] * width, TABLE_ROWS * width) for a in range(slots)
    ]


def pair_product(starts, table, columns, first, held):
    slots = first.shape[1]
    row = jnp.concatenate([first[0, a] for a in range(slots)], axis=1)
    picked = [
        jnp.concatenate([held[table[start + column]] for start in starts], axis=0)
        for column in columns
    ]
    return jnp.dot(row, jnp.concatenate(picked, axis=1), preferred_element_type=jnp.float32)


def first_stop_kernel(
    first_meta, second_meta, kept_columns, first, second,
    total, blank, table, held, zeros, held_sem, blank_sem,
):
    i = pl.program_id(0)
    kept, side = total.shape[1], total.shape[2]
    slots = first.shape[1]
    width = table.shape[0] // (TABLE_ROWS + 1)
    part = zeros.shape[0]

    @pl.when(i == 0)
    def _():
        copy = load_second(second, held, held_sem)
        zeros[...] = jnp.zeros(zeros.shape, zeros.dtype)
        for j in range(blank.shape[0] // part):
            pltpu.make_async_copy(zeros, blank.at[pl.ds(j * part, part)], blank_sem).start()
        fill_table(table, second_meta, slots, width)
        copy.wait()

    starts = row_starts(first_meta, i, slots, width)
    for f in range(0, kept, 2):
        columns = [kept_columns[i * kept + f + g] for g in range(2)]
        both = pair_product(starts, table, columns, first, held)
        total[0, f] = both[:, :side]
        total[0, f + 1] = both[:, side:]

    @pl.when(i == pl.num_programs(0) - 1)
    def _():
        pltpu.make_async_copy(blank, blank, blank_sem).wait()


def last_stop_kernel(
    first_meta, second_meta, kept_columns, owner, place,
    early, late, before, second, part_a, part_b, part_c, blank,
    out, table, used, held, rows, product, held_sem, row_sem, out_sem,
):
    del blank
    i = pl.program_id(0)
    kept, side = before.shape[1], before.shape[2]
    width = table.shape[0] // (TABLE_ROWS + 1)
    per_owner = out.shape[0] // used.shape[0]
    row_total, slots = rows.shape[0], rows.shape[1]
    total = held.shape[0] - 1

    @pl.when(i == 0)
    def _():
        whole = held.at[pl.ds(0, total)]

        @pl.when(place[0] == 0)
        def _():
            pltpu.make_async_copy(second, whole, held_sem).start()

        @pl.when(place[0] != 0)
        def _():
            at = 0
            for part in (part_a, part_b, part_c):
                span = pl.ds(at, part.shape[0])
                pltpu.make_async_copy(part, held.at[span], held_sem).start()
                at += part.shape[0]

        @pl.when(place[1] == 0)
        def _():
            for j in range(row_total):
                pltpu.make_async_copy(early.at[j], rows.at[j], row_sem.at[j]).start()

        @pl.when(place[1] != 0)
        def _():
            for j in range(row_total):
                pltpu.make_async_copy(late.at[j], rows.at[j], row_sem.at[j]).start()

        held[total] = jnp.zeros(held.shape[1:], held.dtype)

        def clear(n, carry):
            used[n] = 0
            return carry

        lax.fori_loop(0, used.shape[0], clear, 0, unroll=16)
        fill_table(table, second_meta, slots, width)
        pltpu.make_async_copy(whole, whole, held_sem).wait()

    pltpu.make_async_copy(rows.at[i], rows.at[i], row_sem.at[i]).wait()
    first = rows.at[pl.ds(i, 1)]
    starts = row_starts(first_meta, i, slots, width)
    for f in range(0, kept, 2):
        columns = [kept_columns[i * kept + f + g] for g in range(2)]
        both = pair_product(starts, table, columns, first, held)
        for g in range(2):
            l = i * kept + f + g
            value = both[:, g * side:(g + 1) * side] + before[0, f + g]
            product[l] = value.astype(product.dtype)
            rank = used[owner[l]]
            used[owner[l]] = rank + 1
            slot = owner[l] * per_owner + rank
            pltpu.make_async_copy(product.at[l], out.at[slot], out_sem).start()

    @pl.when(i == pl.num_programs(0) - 1)
    def _():
        pltpu.make_async_copy(product, out.at[pl.ds(0, product.shape[0])], out_sem).wait()


def first_stop(first_meta, second_meta, kept_columns, first, second, outgoing):
    rows, slots, side, _ = first.shape
    kept = kept_columns.shape[0] // rows
    second_total = second.shape[0]
    part = 16
    return pl.pallas_call(
        first_stop_kernel,
        grid_spec=pltpu.PrefetchScalarGridSpec(
            num_scalar_prefetch=3,
            grid=(rows,),
            in_specs=[
                pl.BlockSpec((1, slots, side, side), lambda i, *_: (i, 0, 0, 0)),
                pl.BlockSpec(memory_space=pl.ANY),
            ],
            out_specs=[
                pl.BlockSpec((1, kept, side, side), lambda i, *_: (i, 0, 0, 0)),
                pl.BlockSpec(memory_space=pl.ANY),
            ],
            scratch_shapes=[
                pltpu.SMEM(((TABLE_ROWS + 1) * TABLE_ROWS,), jnp.int32),
                pltpu.VMEM((second_total + 1, side, side), second.dtype),
                pltpu.VMEM((part, side, side), second.dtype),
                pltpu.SemaphoreType.DMA,
                pltpu.SemaphoreType.DMA,
            ],
        ),
        out_shape=[
            jax.ShapeDtypeStruct((rows, kept, side, side), jnp.float32),
            jax.ShapeDtypeStruct((outgoing, side, side), second.dtype),
        ],
        compiler_params=pltpu.CompilerParams(vmem_limit_bytes=LARGE_VMEM_LIMIT),
        cost_estimate=pl.CostEstimate(
            flops=4 * rows * slots * kept * side**3,
            bytes_accessed=2 * (rows * (slots * 2 + kept * 4) + 2 * second_total) * side**2,
            transcendentals=0,
        ),
    )(first_meta, second_meta, kept_columns, first, second)


def last_stop(
    first_meta, second_meta, kept_columns, owner, place,
    early, late, before, second, part_a, part_b, part_c, blank, owners,
):
    rows, slots, side, _ = early.shape
    kept = before.shape[1]
    second_total = second.shape[0]
    return pl.pallas_call(
        last_stop_kernel,
        grid_spec=pltpu.PrefetchScalarGridSpec(
            num_scalar_prefetch=5,
            grid=(rows,),
            in_specs=[
                pl.BlockSpec(memory_space=pl.ANY),
                pl.BlockSpec(memory_space=pl.ANY),
                pl.BlockSpec((1, kept, side, side), lambda i, *_: (i, 0, 0, 0)),
                pl.BlockSpec(memory_space=pl.ANY),
                pl.BlockSpec(memory_space=pl.ANY),
                pl.BlockSpec(memory_space=pl.ANY),
                pl.BlockSpec(memory_space=pl.ANY),
                pl.BlockSpec(memory_space=pl.ANY),
            ],
            out_specs=pl.BlockSpec(memory_space=pl.ANY),
            scratch_shapes=[
                pltpu.SMEM(((TABLE_ROWS + 1) * TABLE_ROWS,), jnp.int32),
                pltpu.SMEM((owners,), jnp.int32),
                pltpu.VMEM((second_total + 1, side, side), second.dtype),
                pltpu.VMEM(early.shape, early.dtype),
                pltpu.VMEM((rows * kept, side, side), second.dtype),
                pltpu.SemaphoreType.DMA,
                pltpu.SemaphoreType.DMA((rows,)),
                pltpu.SemaphoreType.DMA,
            ],
        ),
        out_shape=jax.ShapeDtypeStruct(blank.shape, blank.dtype),
        input_output_aliases={12: 0},
        compiler_params=pltpu.CompilerParams(vmem_limit_bytes=VMEM_LIMIT),
        cost_estimate=pl.CostEstimate(flops=1024, bytes_accessed=1024, transcendentals=0),
    )(
        first_meta, second_meta, kept_columns, owner, place,
        early, late, before, second, part_a, part_b, part_c, blank,
    )


def cut_kernel(place, source, *rest):
    held, in_sem, out_sem = rest[-3:]
    targets = rest[:-3]

    @pl.when(place[0] != 0)
    def _():
        loads, stores, at = [], [], 0
        for n, target in enumerate(targets):
            piece = pl.ds(at, target.shape[0])
            loads.append(pltpu.make_async_copy(source.at[piece], held.at[piece], in_sem.at[n]))
            stores.append(pltpu.make_async_copy(held.at[piece], target, out_sem.at[n]))
            at += target.shape[0]
        for load in loads:
            load.start()
        for load, store in zip(loads, stores):
            load.wait()
            store.start()
        for store in stores:
            store.wait()


def cut(place, value, sizes):
    return pl.pallas_call(
        cut_kernel,
        in_specs=[pl.BlockSpec(memory_space=pltpu.SMEM), pl.BlockSpec(memory_space=pl.ANY)],
        out_specs=[pl.BlockSpec(memory_space=pl.ANY)] * len(sizes),
        out_shape=[jax.ShapeDtypeStruct((size,) + value.shape[1:], value.dtype) for size in sizes],
        scratch_shapes=[
            pltpu.VMEM(value.shape, value.dtype),
            pltpu.SemaphoreType.DMA((len(sizes),)),
            pltpu.SemaphoreType.DMA((len(sizes),)),
        ],
        compiler_params=pltpu.CompilerParams(vmem_limit_bytes=LARGE_VMEM_LIMIT),
        cost_estimate=pl.CostEstimate(flops=1024, bytes_accessed=1024, transcendentals=0),
    )(place, value)


def copy_kernel(parts, source, target, sem):
    size = source.shape[0] // parts
    for j in range(parts):
        piece = pl.ds(j * size, size)
        pltpu.make_async_copy(source.at[piece], target.at[piece], sem).start()
    pltpu.make_async_copy(source, target, sem).wait()


def hand_over(value):
    return pl.pallas_call(
        functools.partial(copy_kernel, 16),
        in_specs=[pl.BlockSpec(memory_space=pl.ANY)],
        out_specs=pl.BlockSpec(memory_space=pl.ANY),
        out_shape=jax.ShapeDtypeStruct(value.shape, value.dtype),
        scratch_shapes=[pltpu.SemaphoreType.DMA],
        compiler_params=pltpu.CompilerParams(vmem_limit_bytes=VMEM_LIMIT),
    )(value)


def on_device(a_blocks, a_cols, a_count, b_blocks, b_cols, b_count, c_cols, c_owner):
    devices = lax.axis_size("row") * lax.axis_size("col")
    span = lax.axis_size("col") // 2
    rows, kept = c_cols.shape[1], c_cols.shape[2]
    side = a_blocks.shape[3]
    per_owner = max(2, 3 * rows * kept // (2 * devices))
    first = a_blocks[0]
    second = b_blocks[0].reshape(-1, side, side)
    total = second.shape[0]
    large = total * 17 // 40
    spot = lax.axis_index("col") % span
    crossing = (spot == 0).astype(jnp.int32)[None]

    last, middle = span - 1, span - 3

    def near(r, c):
        return r ^ 1, c

    def far(r, c):
        return r ^ 1, c + span

    def at(place, step):
        return lambda r, c: step(r, c) if c % span == place else None

    part_a, part_b, part_c = cut(crossing, second, (large, large, total - 2 * large))
    part_a = move(part_a, at(0, near))
    part_b = move(part_b, at(0, lambda r, c: far(r, c + last)))
    part_c = move(part_c, at(0, lambda r, c: far(r, c + middle)))
    early = move(first, lambda r, c: (r - 1, c) if c % span > 1 else None)
    second_next = move(second, lambda r, c: (r, c - 1) if c % span else None)

    own_first_meta = flat_meta(a_cols[0], a_count[0])
    own_second_meta = flat_meta(b_cols[0], b_count[0])
    kept_columns = c_cols[0].reshape(-1)
    owner = c_owner[0, :, 0]
    before, blank = first_stop(
        own_first_meta, own_second_meta, kept_columns, first, second, devices * per_owner
    )

    part_a, part_b, part_c, first, before, blank = lax.optimization_barrier(
        (part_a, part_b, part_c, first, before, blank)
    )
    late = move(first, lambda r, c: (r - 1, c) if c % span < 2 else None)
    part_a = move(part_a, at(0, lambda r, c: far(r, c + last)))
    part_b = move(part_b, at(last, near))

    part_a, part_c, early, second_next, first_meta = lax.optimization_barrier(
        (part_a, part_c, early, second_next, own_first_meta)
    )
    part_c = move(part_c, at(middle, near))
    first_meta = move(first_meta, lambda r, c: (r - 1, c))

    part_c, second_meta = lax.optimization_barrier((part_c, own_second_meta))
    part_c = move(part_c, at(middle, lambda r, c: (r, c + last - middle)))
    second_meta = move(second_meta, lambda r, c: (r, c - 1))

    place = jnp.stack([spot == span - 1, spot < 2]).astype(jnp.int32)
    outgoing = last_stop(
        first_meta, second_meta, kept_columns, owner, place,
        early, late, before, second_next, part_a, part_b, part_c, blank, devices,
    )
    arrived = lax.all_to_all(
        outgoing.reshape(devices, per_owner, side, side),
        ("row", "col"),
        split_axis=0,
        concat_axis=0,
        tiled=True,
    )
    return hand_over(arrived).reshape(1, devices, per_owner, side, side)


def solution(mesh):
    return jax.shard_map(
        on_device,
        mesh=mesh,
        in_specs=(
            P("row", "col", None, None, None),
            P("row", "col", None),
            P("row", "col"),
            P("col", "row", None, None, None),
            P("col", "row", None),
            P("col", "row"),
            P("row", "col", None),
            P("row", "col", None),
        ),
        out_specs=P(("row", "col"), None, None, None, None),
        check_vma=False,
    )
```

```python
import functools

import jax
import jax.numpy as jnp
from jax import lax
from jax.experimental import pallas as pl
from jax.experimental.pallas import tpu as pltpu
from jax.sharding import PartitionSpec as P

VMEM_LIMIT = 40 * 1024 * 1024
LARGE_VMEM_LIMIT = 62 * 1024 * 1024
TABLE_ROWS = 20
SHORT = 4
STRIDE = 13
SHIFT = 8
PIECE = 8


def move(value, chosen):
    rows, cols = lax.axis_size("row"), lax.axis_size("col")
    pairs = []
    for r in range(rows):
        for c in range(cols):
            to = chosen(r, c)
            if to is not None:
                pairs.append((r * cols + c, (to[0] % rows) * cols + to[1] % cols))
    return lax.ppermute(value, ("row", "col"), pairs)


def flat_meta(columns, counts):
    return jnp.concatenate([columns.reshape(-1), counts])


def fill_table(table, meta, slots, width):
    panel_rows = meta.shape[0] // (slots + 1)
    blank = panel_rows * slots

    def clear(n, carry):
        table[n] = blank
        return carry

    lax.fori_loop(0, table.shape[0], clear, 0, unroll=width)
    for k in range(panel_rows):
        count = meta[blank + k]
        for b in range(slots):
            block = k * slots + b
            table[k * width + meta[block]] = jnp.where(b < count, block, blank)


def list_matches(matches, crowded, table, meta, kept_columns, slots, width):
    row_total = meta.shape[0] // (slots + 1)
    kept = kept_columns.shape[0] // row_total
    blank = TABLE_ROWS * slots

    def one_row(i, carry):
        count = meta[row_total * slots + i]
        starts = [
            jnp.where(a < count, meta[i * slots + a] * width, TABLE_ROWS * width)
            for a in range(slots)
        ]
        firsts = [(i * slots + a) << SHIFT for a in range(slots)]
        most = jnp.int32(0)
        for f in range(kept):
            l = i * kept + f
            column = kept_columns[l]
            found = jnp.int32(0)
            for start, first in zip(starts, firsts):
                block = table[start + column]
                matches[l * STRIDE + found] = first + block
                found += (block != blank).astype(jnp.int32)
            for n in range(slots - SHORT):
                matches[l * STRIDE + found + n] = blank
            matches[l * STRIDE + STRIDE - 1] = found
            most = jnp.maximum(most, found)
        crowded[i] = (most > SHORT).astype(jnp.int32)
        return carry

    lax.fori_loop(0, row_total, one_row, 0)


def load_pieces(source, target, sem):
    total = source.shape[0]
    for at in range(0, total, PIECE):
        piece = pl.ds(at, min(PIECE, total - at))
        pltpu.make_async_copy(source.at[piece], target.at[piece], sem).start()


def matched_product(matches, l, terms, rows, held):
    codes = [matches[l * STRIDE + n] for n in range(terms)]
    left = jnp.concatenate([rows[code >> SHIFT] for code in codes], axis=1)
    right = jnp.concatenate([held[code & ((1 << SHIFT) - 1)] for code in codes], axis=0)
    return jnp.dot(left, right, preferred_element_type=jnp.float32)


def row_products(matches, crowded, i, slots, rows, held, kept, put):
    for f in range(kept):
        l = i * kept + f
        put(l, f, matched_product(matches, l, SHORT, rows, held))

    @pl.when(crowded[i] != 0)
    def _():
        def again(f, carry):
            l = i * kept + f

            @pl.when(matches[l * STRIDE + STRIDE - 1] > SHORT)
            def _():
                put(l, f, matched_product(matches, l, slots, rows, held))

            return carry

        lax.fori_loop(0, kept, again, 0)


def first_stop_kernel(
    first_meta, second_meta, kept_columns, first, second,
    total, blank, table, matches, crowded, held, rows, zeros, held_sem, row_sem, blank_sem,
):
    i = pl.program_id(0)
    kept = total.shape[1]
    row_total = pl.num_programs(0)
    slots = rows.shape[0] // (kept_columns.shape[0] // kept)
    width = table.shape[0] // (TABLE_ROWS + 1)
    part = zeros.shape[0]
    panel = held.at[pl.ds(0, second.shape[0])]

    @pl.when(i == 0)
    def _():
        load_pieces(second, panel, held_sem)
        load_pieces(first, rows, row_sem)
        held[second.shape[0]] = jnp.zeros(held.shape[1:], held.dtype)
        zeros[...] = jnp.zeros(zeros.shape, zeros.dtype)
        fill_table(table, second_meta, slots, width)
        list_matches(matches, crowded, table, first_meta, kept_columns, slots, width)
        pltpu.make_async_copy(rows, rows, row_sem).wait()
        pltpu.make_async_copy(panel, panel, held_sem).wait()
        for j in range(blank.shape[0] // part):
            pltpu.make_async_copy(zeros, blank.at[pl.ds(j * part, part)], blank_sem).start()

    def put(l, f, value):
        total[0, f] = value

    row_products(matches, crowded, i, slots, rows, held, kept, put)

    @pl.when(i == row_total - 1)
    def _():
        pltpu.make_async_copy(blank, blank, blank_sem).wait()


def last_stop_kernel(
    first_meta, second_meta, kept_columns, owner, place,
    early, late, before, second, part_a, part_b, part_c, blank,
    out, table, matches, crowded, used, held, rows, product, held_sem, row_sem, out_sem,
):
    del blank
    i = pl.program_id(0)
    kept = before.shape[1]
    slots = rows.shape[0] // (kept_columns.shape[0] // kept)
    width = table.shape[0] // (TABLE_ROWS + 1)
    per_owner = out.shape[0] // used.shape[0]
    total = held.shape[0] - 1
    panel = held.at[pl.ds(0, total)]

    @pl.when(i == 0)
    def _():
        @pl.when(place[0] == 0)
        def _():
            load_pieces(second, panel, held_sem)

        @pl.when(place[0] != 0)
        def _():
            at = 0
            for part in (part_a, part_b, part_c):
                load_pieces(part, held.at[pl.ds(at, part.shape[0])], held_sem)
                at += part.shape[0]

        @pl.when(place[1] == 0)
        def _():
            load_pieces(early, rows, row_sem)

        @pl.when(place[1] != 0)
        def _():
            load_pieces(late, rows, row_sem)

        held[total] = jnp.zeros(held.shape[1:], held.dtype)

        def clear(n, carry):
            used[n] = 0
            return carry

        lax.fori_loop(0, used.shape[0], clear, 0, unroll=16)
        fill_table(table, second_meta, slots, width)
        list_matches(matches, crowded, table, first_meta, kept_columns, slots, width)
        pltpu.make_async_copy(rows, rows, row_sem).wait()
        pltpu.make_async_copy(panel, panel, held_sem).wait()

    def put(l, f, value):
        product[l] = (value + before[0, f]).astype(product.dtype)

    row_products(matches, crowded, i, slots, rows, held, kept, put)
    for f in range(kept):
        l = i * kept + f
        rank = used[owner[l]]
        used[owner[l]] = rank + 1
        slot = owner[l] * per_owner + rank
        pltpu.make_async_copy(product.at[l], out.at[slot], out_sem).start()

    @pl.when(i == pl.num_programs(0) - 1)
    def _():
        pltpu.make_async_copy(product, out.at[pl.ds(0, product.shape[0])], out_sem).wait()


def list_scratch(kept_total, row_total):
    return [
        pltpu.SMEM(((TABLE_ROWS + 1) * TABLE_ROWS,), jnp.int32),
        pltpu.SMEM((kept_total * STRIDE,), jnp.int32),
        pltpu.SMEM((row_total,), jnp.int32),
    ]


def first_stop(first_meta, second_meta, kept_columns, first, second, outgoing):
    first_total, side, _ = first.shape
    rows = first_meta.shape[0] - first_total
    kept = kept_columns.shape[0] // rows
    second_total = second.shape[0]
    part = 16
    return pl.pallas_call(
        first_stop_kernel,
        grid_spec=pltpu.PrefetchScalarGridSpec(
            num_scalar_prefetch=3,
            grid=(rows,),
            in_specs=[pl.BlockSpec(memory_space=pl.ANY)] * 2,
            out_specs=[
                pl.BlockSpec((1, kept, side, side), lambda i, *_: (i, 0, 0, 0)),
                pl.BlockSpec(memory_space=pl.ANY),
            ],
            scratch_shapes=list_scratch(rows * kept, rows) + [
                pltpu.VMEM((second_total + 1, side, side), second.dtype),
                pltpu.VMEM(first.shape, first.dtype),
                pltpu.VMEM((part, side, side), second.dtype),
                pltpu.SemaphoreType.DMA,
                pltpu.SemaphoreType.DMA,
                pltpu.SemaphoreType.DMA,
            ],
        ),
        out_shape=[
            jax.ShapeDtypeStruct((rows, kept, side, side), jnp.float32),
            jax.ShapeDtypeStruct((outgoing, side, side), second.dtype),
        ],
        compiler_params=pltpu.CompilerParams(vmem_limit_bytes=LARGE_VMEM_LIMIT),
        cost_estimate=pl.CostEstimate(
            flops=4 * first_total * kept * side**3,
            bytes_accessed=2 * (first_total * 2 + rows * kept * 4 + 2 * second_total) * side**2,
            transcendentals=0,
        ),
    )(first_meta, second_meta, kept_columns, first, second)


def last_stop(
    first_meta, second_meta, kept_columns, owner, place,
    early, late, before, second, part_a, part_b, part_c, blank, owners,
):
    side = early.shape[1]
    rows, kept = before.shape[:2]
    second_total = second.shape[0]
    return pl.pallas_call(
        last_stop_kernel,
        grid_spec=pltpu.PrefetchScalarGridSpec(
            num_scalar_prefetch=5,
            grid=(rows,),
            in_specs=[
                pl.BlockSpec(memory_space=pl.ANY),
                pl.BlockSpec(memory_space=pl.ANY),
                pl.BlockSpec((1, kept, side, side), lambda i, *_: (i, 0, 0, 0)),
                pl.BlockSpec(memory_space=pl.ANY),
                pl.BlockSpec(memory_space=pl.ANY),
                pl.BlockSpec(memory_space=pl.ANY),
                pl.BlockSpec(memory_space=pl.ANY),
                pl.BlockSpec(memory_space=pl.ANY),
            ],
            out_specs=pl.BlockSpec(memory_space=pl.ANY),
            scratch_shapes=list_scratch(rows * kept, rows) + [
                pltpu.SMEM((owners,), jnp.int32),
                pltpu.VMEM((second_total + 1, side, side), second.dtype),
                pltpu.VMEM(early.shape, early.dtype),
                pltpu.VMEM((rows * kept, side, side), second.dtype),
                pltpu.SemaphoreType.DMA,
                pltpu.SemaphoreType.DMA,
                pltpu.SemaphoreType.DMA,
            ],
        ),
        out_shape=jax.ShapeDtypeStruct(blank.shape, blank.dtype),
        input_output_aliases={12: 0},
        compiler_params=pltpu.CompilerParams(vmem_limit_bytes=LARGE_VMEM_LIMIT),
        cost_estimate=pl.CostEstimate(flops=1024, bytes_accessed=1024, transcendentals=0),
    )(
        first_meta, second_meta, kept_columns, owner, place,
        early, late, before, second, part_a, part_b, part_c, blank,
    )


def cut_kernel(place, source, *rest):
    held, in_sem, out_sem = rest[-3:]
    targets = rest[:-3]

    @pl.when(place[0] != 0)
    def _():
        loads, stores, at = [], [], 0
        for n, target in enumerate(targets):
            piece = pl.ds(at, target.shape[0])
            loads.append(pltpu.make_async_copy(source.at[piece], held.at[piece], in_sem.at[n]))
            stores.append(pltpu.make_async_copy(held.at[piece], target, out_sem.at[n]))
            at += target.shape[0]
        for load in loads:
            load.start()
        for load, store in zip(loads, stores):
            load.wait()
            store.start()
        for store in stores:
            store.wait()


def cut(place, value, sizes):
    return pl.pallas_call(
        cut_kernel,
        in_specs=[pl.BlockSpec(memory_space=pltpu.SMEM), pl.BlockSpec(memory_space=pl.ANY)],
        out_specs=[pl.BlockSpec(memory_space=pl.ANY)] * len(sizes),
        out_shape=[jax.ShapeDtypeStruct((size,) + value.shape[1:], value.dtype) for size in sizes],
        scratch_shapes=[
            pltpu.VMEM(value.shape, value.dtype),
            pltpu.SemaphoreType.DMA((len(sizes),)),
            pltpu.SemaphoreType.DMA((len(sizes),)),
        ],
        compiler_params=pltpu.CompilerParams(vmem_limit_bytes=LARGE_VMEM_LIMIT),
        cost_estimate=pl.CostEstimate(flops=1024, bytes_accessed=1024, transcendentals=0),
    )(place, value)


def copy_kernel(parts, source, target, sem):
    size = source.shape[0] // parts
    for j in range(parts):
        piece = pl.ds(j * size, size)
        pltpu.make_async_copy(source.at[piece], target.at[piece], sem).start()
    pltpu.make_async_copy(source, target, sem).wait()


def hand_over(value):
    return pl.pallas_call(
        functools.partial(copy_kernel, 16),
        in_specs=[pl.BlockSpec(memory_space=pl.ANY)],
        out_specs=pl.BlockSpec(memory_space=pl.ANY),
        out_shape=jax.ShapeDtypeStruct(value.shape, value.dtype),
        scratch_shapes=[pltpu.SemaphoreType.DMA],
        compiler_params=pltpu.CompilerParams(vmem_limit_bytes=VMEM_LIMIT),
    )(value)


def on_device(a_blocks, a_cols, a_count, b_blocks, b_cols, b_count, c_cols, c_owner):
    devices = lax.axis_size("row") * lax.axis_size("col")
    span = lax.axis_size("col") // 2
    rows, kept = c_cols.shape[1], c_cols.shape[2]
    side = a_blocks.shape[3]
    per_owner = max(2, 3 * rows * kept // (2 * devices))
    first = a_blocks[0].reshape(-1, side, side)
    second = b_blocks[0].reshape(-1, side, side)
    total = second.shape[0]
    large = total * 17 // 40
    spot = lax.axis_index("col") % span
    crossing = (spot == 0).astype(jnp.int32)[None]

    last, middle = span - 1, span - 3

    def near(r, c):
        return r ^ 1, c

    def far(r, c):
        return r ^ 1, c + span

    def at(place, step):
        return lambda r, c: step(r, c) if c % span == place else None

    part_a, part_b, part_c = cut(crossing, second, (large, large, total - 2 * large))
    part_a = move(part_a, at(0, near))
    part_b = move(part_b, at(0, lambda r, c: far(r, c + last)))
    part_c = move(part_c, at(0, lambda r, c: (r, c + middle)))
    early = move(first, lambda r, c: (r - 1, c) if c % span > 1 else None)
    second_next = move(second, lambda r, c: (r, c - 1) if c % span else None)

    own_first_meta = flat_meta(a_cols[0], a_count[0])
    own_second_meta = flat_meta(b_cols[0], b_count[0])
    kept_columns = c_cols[0].reshape(-1)
    owner = c_owner[0, :, 0]
    before, blank = first_stop(
        own_first_meta, own_second_meta, kept_columns, first, second, devices * per_owner
    )

    part_a, part_b, part_c, first, before, blank = lax.optimization_barrier(
        (part_a, part_b, part_c, first, before, blank)
    )
    late = move(first, lambda r, c: (r - 1, c) if c % span < 2 else None)
    part_a = move(part_a, at(0, lambda r, c: far(r, c + last)))
    part_c = move(part_c, at(middle, far))
    part_b, part_c = lax.optimization_barrier((part_b, part_c))
    part_b = move(part_b, at(last, near))

    part_a, part_c, early, second_next, first_meta = lax.optimization_barrier(
        (part_a, part_c, early, second_next, own_first_meta)
    )
    part_c = move(part_c, at(middle, near))
    first_meta = move(first_meta, lambda r, c: (r - 1, c))

    part_c, second_meta = lax.optimization_barrier((part_c, own_second_meta))
    part_c = move(part_c, at(middle, lambda r, c: (r, c + last - middle)))
    second_meta = move(second_meta, lambda r, c: (r, c - 1))

    place = jnp.stack([spot == span - 1, spot < 2]).astype(jnp.int32)
    outgoing = last_stop(
        first_meta, second_meta, kept_columns, owner, place,
        early, late, before, second_next, part_a, part_b, part_c, blank, devices,
    )
    arrived = lax.all_to_all(
        outgoing.reshape(devices, per_owner, side, side),
        ("row", "col"),
        split_axis=0,
        concat_axis=0,
        tiled=True,
    )
    return hand_over(arrived).reshape(1, devices, per_owner, side, side)


def solution(mesh):
    return jax.shard_map(
        on_device,
        mesh=mesh,
        in_specs=(
            P("row", "col", None, None, None),
            P("row", "col", None),
            P("row", "col"),
            P("col", "row", None, None, None),
            P("col", "row", None),
            P("col", "row"),
            P("row", "col", None),
            P("row", "col", None),
        ),
        out_specs=P(("row", "col"), None, None, None, None),
        check_vma=False,
    )
```

```python
import functools

import jax
import jax.numpy as jnp
from jax import lax
from jax.experimental import pallas as pl
from jax.experimental.pallas import tpu as pltpu
from jax.sharding import PartitionSpec as P

VMEM_LIMIT = 40 * 1024 * 1024
LARGE_VMEM_LIMIT = 62 * 1024 * 1024
TABLE_ROWS = 20
SHORT = 4
STRIDE = 13
SHIFT = 8
PIECE = 8


def move(value, chosen):
    rows, cols = lax.axis_size("row"), lax.axis_size("col")
    pairs = []
    for r in range(rows):
        for c in range(cols):
            to = chosen(r, c)
            if to is not None:
                pairs.append((r * cols + c, (to[0] % rows) * cols + to[1] % cols))
    return lax.ppermute(value, ("row", "col"), pairs)


def flat_meta(columns, counts):
    return jnp.concatenate([columns.reshape(-1), counts])


def fill_table(table, meta, slots, width):
    panel_rows = meta.shape[0] // (slots + 1)
    blank = panel_rows * slots

    def clear(n, carry):
        table[n] = blank
        return carry

    lax.fori_loop(0, table.shape[0], clear, 0, unroll=width)
    for k in range(panel_rows):
        count = meta[blank + k]
        columns = [meta[k * slots + b] for b in range(slots)]
        for b in range(slots):
            table[k * width + columns[b]] = jnp.where(b < count, k * slots + b, blank)


def list_matches(matches, crowded, table, meta, kept_columns, slots, width):
    row_total = meta.shape[0] // (slots + 1)
    kept = kept_columns.shape[0] // row_total
    blank = TABLE_ROWS * slots

    def one_row(i, carry):
        count = meta[row_total * slots + i]
        starts = [
            jnp.where(a < count, meta[i * slots + a] * width, TABLE_ROWS * width)
            for a in range(slots)
        ]
        firsts = [(i * slots + a) << SHIFT for a in range(slots)]
        most = jnp.int32(0)
        for f in range(0, kept, 2):
            columns = [kept_columns[i * kept + f + g] for g in range(2)]
            blocks = [[table[start + column] for start in starts] for column in columns]
            for g in range(2):
                at = (i * kept + f + g) * STRIDE
                found = jnp.int32(0)
                for block, first in zip(blocks[g], firsts):
                    matches[at + found] = first + block
                    found += (block != blank).astype(jnp.int32)
                for n in range(slots - SHORT):
                    matches[at + found + n] = blank
                matches[at + STRIDE - 1] = found
                most = jnp.maximum(most, found)
        crowded[i] = (most > SHORT).astype(jnp.int32)
        return carry

    lax.fori_loop(0, row_total, one_row, 0)


def load_pieces(source, target, sem):
    total = source.shape[0]
    for at in range(0, total, PIECE):
        piece = pl.ds(at, min(PIECE, total - at))
        pltpu.make_async_copy(source.at[piece], target.at[piece], sem).start()


def matched_product(matches, l, terms, rows, held):
    codes = [matches[l * STRIDE + n] for n in range(terms)]
    left = jnp.concatenate([rows[code >> SHIFT] for code in codes], axis=1)
    right = jnp.concatenate([held[code & ((1 << SHIFT) - 1)] for code in codes], axis=0)
    return jnp.dot(left, right, preferred_element_type=jnp.float32)


def row_products(matches, crowded, i, slots, rows, held, kept, put):
    for f in range(kept):
        l = i * kept + f
        put(l, f, matched_product(matches, l, SHORT, rows, held))

    @pl.when(crowded[i] != 0)
    def _():
        def again(f, carry):
            l = i * kept + f

            @pl.when(matches[l * STRIDE + STRIDE - 1] > SHORT)
            def _():
                put(l, f, matched_product(matches, l, slots, rows, held))

            return carry

        lax.fori_loop(0, kept, again, 0)


def first_stop_kernel(
    first_meta, second_meta, kept_columns, first, second,
    total, blank, table, matches, crowded, held, rows, zeros, held_sem, row_sem, blank_sem,
):
    i = pl.program_id(0)
    kept = total.shape[1]
    row_total = pl.num_programs(0)
    slots = rows.shape[0] // (kept_columns.shape[0] // kept)
    width = table.shape[0] // (TABLE_ROWS + 1)
    part = zeros.shape[0]
    panel = held.at[pl.ds(0, second.shape[0])]

    @pl.when(i == 0)
    def _():
        load_pieces(second, panel, held_sem)
        load_pieces(first, rows, row_sem)
        held[second.shape[0]] = jnp.zeros(held.shape[1:], held.dtype)
        zeros[...] = jnp.zeros(zeros.shape, zeros.dtype)
        fill_table(table, second_meta, slots, width)
        list_matches(matches, crowded, table, first_meta, kept_columns, slots, width)
        pltpu.make_async_copy(rows, rows, row_sem).wait()
        pltpu.make_async_copy(panel, panel, held_sem).wait()
        for j in range(blank.shape[0] // part):
            pltpu.make_async_copy(zeros, blank.at[pl.ds(j * part, part)], blank_sem).start()

    def put(l, f, value):
        total[0, f] = value

    row_products(matches, crowded, i, slots, rows, held, kept, put)

    @pl.when(i == row_total - 1)
    def _():
        pltpu.make_async_copy(blank, blank, blank_sem).wait()


def last_stop_kernel(
    first_meta, second_meta, kept_columns, owner, place,
    early, late, before, second, part_a, part_b, part_c, blank,
    out, table, matches, crowded, used, held, rows, product, held_sem, row_sem, out_sem,
):
    del blank
    i = pl.program_id(0)
    kept = before.shape[1]
    slots = rows.shape[0] // (kept_columns.shape[0] // kept)
    width = table.shape[0] // (TABLE_ROWS + 1)
    per_owner = out.shape[0] // used.shape[0]
    total = held.shape[0] - 1
    panel = held.at[pl.ds(0, total)]

    @pl.when(i == 0)
    def _():
        @pl.when(place[0] == 0)
        def _():
            load_pieces(second, panel, held_sem)

        @pl.when(place[0] != 0)
        def _():
            at = 0
            for part in (part_a, part_b, part_c):
                load_pieces(part, held.at[pl.ds(at, part.shape[0])], held_sem)
                at += part.shape[0]

        @pl.when(place[1] == 0)
        def _():
            load_pieces(early, rows, row_sem)

        @pl.when(place[1] != 0)
        def _():
            load_pieces(late, rows, row_sem)

        held[total] = jnp.zeros(held.shape[1:], held.dtype)

        def clear(n, carry):
            used[n] = 0
            return carry

        lax.fori_loop(0, used.shape[0], clear, 0, unroll=16)
        fill_table(table, second_meta, slots, width)
        list_matches(matches, crowded, table, first_meta, kept_columns, slots, width)
        pltpu.make_async_copy(rows, rows, row_sem).wait()
        pltpu.make_async_copy(panel, panel, held_sem).wait()

    def put(l, f, value):
        product[l] = (value + before[0, f]).astype(product.dtype)

    row_products(matches, crowded, i, slots, rows, held, kept, put)
    owners = [owner[i * kept + f] for f in range(kept)]
    for f in range(kept):
        rank = used[owners[f]]
        used[owners[f]] = rank + 1
        slot = owners[f] * per_owner + rank
        pltpu.make_async_copy(product.at[i * kept + f], out.at[slot], out_sem).start()

    @pl.when(i == pl.num_programs(0) - 1)
    def _():
        pltpu.make_async_copy(product, out.at[pl.ds(0, product.shape[0])], out_sem).wait()


def list_scratch(kept_total, row_total):
    return [
        pltpu.SMEM(((TABLE_ROWS + 1) * TABLE_ROWS,), jnp.int32),
        pltpu.SMEM((kept_total * STRIDE,), jnp.int32),
        pltpu.SMEM((row_total,), jnp.int32),
    ]


def first_stop(first_meta, second_meta, kept_columns, first, second, outgoing):
    first_total, side, _ = first.shape
    rows = first_meta.shape[0] - first_total
    kept = kept_columns.shape[0] // rows
    second_total = second.shape[0]
    part = 16
    return pl.pallas_call(
        first_stop_kernel,
        grid_spec=pltpu.PrefetchScalarGridSpec(
            num_scalar_prefetch=3,
            grid=(rows,),
            in_specs=[pl.BlockSpec(memory_space=pl.ANY)] * 2,
            out_specs=[
                pl.BlockSpec((1, kept, side, side), lambda i, *_: (i, 0, 0, 0)),
                pl.BlockSpec(memory_space=pl.ANY),
            ],
            scratch_shapes=list_scratch(rows * kept, rows) + [
                pltpu.VMEM((second_total + 1, side, side), second.dtype),
                pltpu.VMEM(first.shape, first.dtype),
                pltpu.VMEM((part, side, side), second.dtype),
                pltpu.SemaphoreType.DMA,
                pltpu.SemaphoreType.DMA,
                pltpu.SemaphoreType.DMA,
            ],
        ),
        out_shape=[
            jax.ShapeDtypeStruct((rows, kept, side, side), jnp.float32),
            jax.ShapeDtypeStruct((outgoing, side, side), second.dtype),
        ],
        compiler_params=pltpu.CompilerParams(vmem_limit_bytes=LARGE_VMEM_LIMIT),
        cost_estimate=pl.CostEstimate(
            flops=4 * first_total * kept * side**3,
            bytes_accessed=2 * (first_total * 2 + rows * kept * 4 + 2 * second_total) * side**2,
            transcendentals=0,
        ),
    )(first_meta, second_meta, kept_columns, first, second)


def last_stop(
    first_meta, second_meta, kept_columns, owner, place,
    early, late, before, second, part_a, part_b, part_c, blank, owners,
):
    side = early.shape[1]
    rows, kept = before.shape[:2]
    second_total = second.shape[0]
    return pl.pallas_call(
        last_stop_kernel,
        grid_spec=pltpu.PrefetchScalarGridSpec(
            num_scalar_prefetch=5,
            grid=(rows,),
            in_specs=[
                pl.BlockSpec(memory_space=pl.ANY),
                pl.BlockSpec(memory_space=pl.ANY),
                pl.BlockSpec((1, kept, side, side), lambda i, *_: (i, 0, 0, 0)),
                pl.BlockSpec(memory_space=pl.ANY),
                pl.BlockSpec(memory_space=pl.ANY),
                pl.BlockSpec(memory_space=pl.ANY),
                pl.BlockSpec(memory_space=pl.ANY),
                pl.BlockSpec(memory_space=pl.ANY),
            ],
            out_specs=pl.BlockSpec(memory_space=pl.ANY),
            scratch_shapes=list_scratch(rows * kept, rows) + [
                pltpu.SMEM((owners,), jnp.int32),
                pltpu.VMEM((second_total + 1, side, side), second.dtype),
                pltpu.VMEM(early.shape, early.dtype),
                pltpu.VMEM((rows * kept, side, side), second.dtype),
                pltpu.SemaphoreType.DMA,
                pltpu.SemaphoreType.DMA,
                pltpu.SemaphoreType.DMA,
            ],
        ),
        out_shape=jax.ShapeDtypeStruct(blank.shape, blank.dtype),
        input_output_aliases={12: 0},
        compiler_params=pltpu.CompilerParams(vmem_limit_bytes=LARGE_VMEM_LIMIT),
        cost_estimate=pl.CostEstimate(flops=1024, bytes_accessed=1024, transcendentals=0),
    )(
        first_meta, second_meta, kept_columns, owner, place,
        early, late, before, second, part_a, part_b, part_c, blank,
    )


def cut_kernel(place, source, *rest):
    held, in_sem, out_sem = rest[-3:]
    targets = rest[:-3]

    @pl.when(place[0] != 0)
    def _():
        loads, stores, at = [], [], 0
        for n, target in enumerate(targets):
            piece = pl.ds(at, target.shape[0])
            loads.append(pltpu.make_async_copy(source.at[piece], held.at[piece], in_sem.at[n]))
            stores.append(pltpu.make_async_copy(held.at[piece], target, out_sem.at[n]))
            at += target.shape[0]
        for load in loads:
            load.start()
        for load, store in zip(loads, stores):
            load.wait()
            store.start()
        for store in stores:
            store.wait()


def cut(place, value, sizes):
    return pl.pallas_call(
        cut_kernel,
        in_specs=[pl.BlockSpec(memory_space=pltpu.SMEM), pl.BlockSpec(memory_space=pl.ANY)],
        out_specs=[pl.BlockSpec(memory_space=pl.ANY)] * len(sizes),
        out_shape=[jax.ShapeDtypeStruct((size,) + value.shape[1:], value.dtype) for size in sizes],
        scratch_shapes=[
            pltpu.VMEM(value.shape, value.dtype),
            pltpu.SemaphoreType.DMA((len(sizes),)),
            pltpu.SemaphoreType.DMA((len(sizes),)),
        ],
        compiler_params=pltpu.CompilerParams(vmem_limit_bytes=LARGE_VMEM_LIMIT),
        cost_estimate=pl.CostEstimate(flops=1024, bytes_accessed=1024, transcendentals=0),
    )(place, value)


def copy_kernel(parts, source, target, sem):
    size = source.shape[0] // parts
    for j in range(parts):
        piece = pl.ds(j * size, size)
        pltpu.make_async_copy(source.at[piece], target.at[piece], sem).start()
    pltpu.make_async_copy(source, target, sem).wait()


def hand_over(value):
    return pl.pallas_call(
        functools.partial(copy_kernel, 16),
        in_specs=[pl.BlockSpec(memory_space=pl.ANY)],
        out_specs=pl.BlockSpec(memory_space=pl.ANY),
        out_shape=jax.ShapeDtypeStruct(value.shape, value.dtype),
        scratch_shapes=[pltpu.SemaphoreType.DMA],
        compiler_params=pltpu.CompilerParams(vmem_limit_bytes=VMEM_LIMIT),
    )(value)


def on_device(a_blocks, a_cols, a_count, b_blocks, b_cols, b_count, c_cols, c_owner):
    devices = lax.axis_size("row") * lax.axis_size("col")
    span = lax.axis_size("col") // 2
    rows, kept = c_cols.shape[1], c_cols.shape[2]
    side = a_blocks.shape[3]
    per_owner = max(2, 3 * rows * kept // (2 * devices))
    first = a_blocks[0].reshape(-1, side, side)
    second = b_blocks[0].reshape(-1, side, side)
    total = second.shape[0]
    large = total * 17 // 40
    spot = lax.axis_index("col") % span
    crossing = (spot == 0).astype(jnp.int32)[None]

    last, middle = span - 1, span - 3

    def near(r, c):
        return r ^ 1, c

    def far(r, c):
        return r ^ 1, c + span

    def at(place, step):
        return lambda r, c: step(r, c) if c % span == place else None

    part_a, part_b, part_c = cut(crossing, second, (large, large, total - 2 * large))
    part_a = move(part_a, at(0, near))
    part_b = move(part_b, at(0, lambda r, c: far(r, c + last)))
    part_c = move(part_c, at(0, lambda r, c: (r, c + middle)))
    early = move(first, lambda r, c: (r - 1, c) if c % span > 1 else None)
    second_next = move(second, lambda r, c: (r, c - 1) if c % span else None)

    own_first_meta = flat_meta(a_cols[0], a_count[0])
    own_second_meta = flat_meta(b_cols[0], b_count[0])
    kept_columns = c_cols[0].reshape(-1)
    owner = c_owner[0, :, 0]
    before, blank = first_stop(
        own_first_meta, own_second_meta, kept_columns, first, second, devices * per_owner
    )

    part_a, part_b, part_c, first, before, blank = lax.optimization_barrier(
        (part_a, part_b, part_c, first, before, blank)
    )
    late = move(first, lambda r, c: (r - 1, c) if c % span < 2 else None)
    part_a = move(part_a, at(0, lambda r, c: far(r, c + last)))
    part_c = move(part_c, at(middle, far))
    part_b, part_c = lax.optimization_barrier((part_b, part_c))
    part_b = move(part_b, at(last, near))

    part_a, part_c, early, second_next, first_meta, second_meta = lax.optimization_barrier(
        (part_a, part_c, early, second_next, own_first_meta, own_second_meta)
    )
    part_c = move(part_c, at(middle, near))
    first_meta = move(first_meta, lambda r, c: (r - 1, c))
    second_meta = move(second_meta, lambda r, c: (r, c - 1))
    part_c = move(part_c, at(middle, lambda r, c: (r, c + last - middle)))

    place = jnp.stack([spot == span - 1, spot < 2]).astype(jnp.int32)
    outgoing = last_stop(
        first_meta, second_meta, kept_columns, owner, place,
        early, late, before, second_next, part_a, part_b, part_c, blank, devices,
    )
    arrived = lax.all_to_all(
        outgoing.reshape(devices, per_owner, side, side),
        ("row", "col"),
        split_axis=0,
        concat_axis=0,
        tiled=True,
    )
    return hand_over(arrived).reshape(1, devices, per_owner, side, side)


def solution(mesh):
    return jax.shard_map(
        on_device,
        mesh=mesh,
        in_specs=(
            P("row", "col", None, None, None),
            P("row", "col", None),
            P("row", "col"),
            P("col", "row", None, None, None),
            P("col", "row", None),
            P("col", "row"),
            P("row", "col", None),
            P("row", "col", None),
        ),
        out_specs=P(("row", "col"), None, None, None, None),
        check_vma=False,
    )
```

```python
import functools

import jax
import jax.numpy as jnp
from jax import lax
from jax.experimental import pallas as pl
from jax.experimental.pallas import tpu as pltpu
from jax.sharding import PartitionSpec as P

VMEM_LIMIT = 40 * 1024 * 1024
LARGE_VMEM_LIMIT = 62 * 1024 * 1024
TABLE_ROWS = 20
PIECE = 8


def move(value, chosen):
    rows, cols = lax.axis_size("row"), lax.axis_size("col")
    pairs = []
    for r in range(rows):
        for c in range(cols):
            to = chosen(r, c)
            if to is not None:
                pairs.append((r * cols + c, (to[0] % rows) * cols + to[1] % cols))
    return lax.ppermute(value, ("row", "col"), pairs)


def flat_meta(columns, counts):
    return jnp.concatenate([columns.reshape(-1), counts])


def fill_table(table, meta, slots, width):
    panel_rows = meta.shape[0] // (slots + 1)
    blank = panel_rows * slots

    def clear(n, carry):
        table[n] = blank
        return carry

    lax.fori_loop(0, table.shape[0], clear, 0, unroll=width)
    for k in range(panel_rows):
        count = meta[blank + k]
        columns = [meta[k * slots + b] for b in range(slots)]
        for b in range(slots):
            table[k * width + columns[b]] = jnp.where(b < count, k * slots + b, blank)


def load_pieces(source, target, sem):
    total = source.shape[0]
    for at in range(0, total, PIECE):
        piece = pl.ds(at, min(PIECE, total - at))
        pltpu.make_async_copy(source.at[piece], target.at[piece], sem).start()


def row_products(table, first_meta, kept_columns, i, slots, kept, rows, held, put):
    width = table.shape[0] // (TABLE_ROWS + 1)
    side = held.shape[1]
    row_total = kept_columns.shape[0] // kept
    count = first_meta[row_total * slots + i]

    def over(terms):
        starts = [
            jnp.where(a < count, first_meta[i * slots + a] * width, TABLE_ROWS * width)
            for a in range(terms)
        ]
        left = jnp.concatenate([rows[i * slots + a] for a in range(terms)], axis=1)
        for f in range(0, kept, 2):
            picked = []
            for g in range(2):
                column = kept_columns[i * kept + f + g]
                blocks = [held[table[start + column]] for start in starts]
                picked.append(jnp.concatenate(blocks, axis=0))
            right = jnp.concatenate(picked, axis=1)
            both = jnp.dot(left, right, preferred_element_type=jnp.float32)
            put(f, both[:, :side])
            put(f + 1, both[:, side:])

    fewer = -1
    for terms in (slots // 2, slots * 3 // 4, slots):
        pl.when((count > fewer) & (count <= terms))(functools.partial(over, terms))
        fewer = terms


def first_stop_kernel(
    first_meta, second_meta, kept_columns, first, second,
    total, blank, table, held, rows, zeros, held_sem, row_sem, blank_sem,
):
    i = pl.program_id(0)
    kept = total.shape[1]
    slots = rows.shape[0] * kept // kept_columns.shape[0]
    part = zeros.shape[0]
    panel = held.at[pl.ds(0, second.shape[0])]

    @pl.when(i == 0)
    def _():
        load_pieces(second, panel, held_sem)
        load_pieces(first, rows, row_sem)
        held[second.shape[0]] = jnp.zeros(held.shape[1:], held.dtype)
        zeros[...] = jnp.zeros(zeros.shape, zeros.dtype)
        fill_table(table, second_meta, slots, table.shape[0] // (TABLE_ROWS + 1))
        pltpu.make_async_copy(rows, rows, row_sem).wait()
        pltpu.make_async_copy(panel, panel, held_sem).wait()
        for j in range(blank.shape[0] // part):
            pltpu.make_async_copy(zeros, blank.at[pl.ds(j * part, part)], blank_sem).start()

    def put(f, value):
        total[0, f] = value

    row_products(table, first_meta, kept_columns, i, slots, kept, rows, held, put)

    @pl.when(i == pl.num_programs(0) - 1)
    def _():
        pltpu.make_async_copy(blank, blank, blank_sem).wait()


def last_stop_kernel(
    first_meta, second_meta, kept_columns, owner, place,
    early, late, before, second, part_a, part_b, part_c, blank,
    out, table, used, held, rows, product, held_sem, row_sem, out_sem,
):
    del blank
    i = pl.program_id(0)
    kept = before.shape[1]
    slots = rows.shape[0] * kept // kept_columns.shape[0]
    per_owner = out.shape[0] // used.shape[0]
    total = held.shape[0] - 1
    panel = held.at[pl.ds(0, total)]

    @pl.when(i == 0)
    def _():
        @pl.when(place[0] == 0)
        def _():
            load_pieces(second, panel, held_sem)

        @pl.when(place[0] != 0)
        def _():
            at = 0
            for part in (part_a, part_b, part_c):
                load_pieces(part, held.at[pl.ds(at, part.shape[0])], held_sem)
                at += part.shape[0]

        @pl.when(place[1] == 0)
        def _():
            load_pieces(early, rows, row_sem)

        @pl.when(place[1] != 0)
        def _():
            load_pieces(late, rows, row_sem)

        held[total] = jnp.zeros(held.shape[1:], held.dtype)

        def clear(n, carry):
            used[n] = 0
            return carry

        lax.fori_loop(0, used.shape[0], clear, 0, unroll=16)
        fill_table(table, second_meta, slots, table.shape[0] // (TABLE_ROWS + 1))
        pltpu.make_async_copy(rows, rows, row_sem).wait()
        pltpu.make_async_copy(panel, panel, held_sem).wait()

    def put(f, value):
        l = i * kept + f
        product[l] = (value + before[0, f]).astype(product.dtype)
        rank = used[owner[l]]
        used[owner[l]] = rank + 1
        slot = owner[l] * per_owner + rank
        pltpu.make_async_copy(product.at[l], out.at[slot], out_sem).start()

    row_products(table, first_meta, kept_columns, i, slots, kept, rows, held, put)

    @pl.when(i == pl.num_programs(0) - 1)
    def _():
        pltpu.make_async_copy(product, out.at[pl.ds(0, product.shape[0])], out_sem).wait()


def first_stop(first_meta, second_meta, kept_columns, first, second, outgoing):
    first_total, side, _ = first.shape
    rows = first_meta.shape[0] - first_total
    kept = kept_columns.shape[0] // rows
    second_total = second.shape[0]
    part = 16
    return pl.pallas_call(
        first_stop_kernel,
        grid_spec=pltpu.PrefetchScalarGridSpec(
            num_scalar_prefetch=3,
            grid=(rows,),
            in_specs=[pl.BlockSpec(memory_space=pl.ANY)] * 2,
            out_specs=[
                pl.BlockSpec((1, kept, side, side), lambda i, *_: (i, 0, 0, 0)),
                pl.BlockSpec(memory_space=pl.ANY),
            ],
            scratch_shapes=[
                pltpu.SMEM(((TABLE_ROWS + 1) * TABLE_ROWS,), jnp.int32),
                pltpu.VMEM((second_total + 1, side, side), second.dtype),
                pltpu.VMEM(first.shape, first.dtype),
                pltpu.VMEM((part, side, side), second.dtype),
                pltpu.SemaphoreType.DMA,
                pltpu.SemaphoreType.DMA,
                pltpu.SemaphoreType.DMA,
            ],
        ),
        out_shape=[
            jax.ShapeDtypeStruct((rows, kept, side, side), jnp.float32),
            jax.ShapeDtypeStruct((outgoing, side, side), second.dtype),
        ],
        compiler_params=pltpu.CompilerParams(vmem_limit_bytes=LARGE_VMEM_LIMIT),
        cost_estimate=pl.CostEstimate(
            flops=4 * first_total * kept * side**3,
            bytes_accessed=2 * (first_total * 2 + rows * kept * 4 + 2 * second_total) * side**2,
            transcendentals=0,
        ),
    )(first_meta, second_meta, kept_columns, first, second)


def last_stop(
    first_meta, second_meta, kept_columns, owner, place,
    early, late, before, second, part_a, part_b, part_c, blank, owners,
):
    side = early.shape[1]
    rows, kept = before.shape[:2]
    second_total = second.shape[0]
    anywhere = pl.BlockSpec(memory_space=pl.ANY)
    return pl.pallas_call(
        last_stop_kernel,
        grid_spec=pltpu.PrefetchScalarGridSpec(
            num_scalar_prefetch=5,
            grid=(rows,),
            in_specs=[
                anywhere,
                anywhere,
                pl.BlockSpec((1, kept, side, side), lambda i, *_: (i, 0, 0, 0)),
            ] + [anywhere] * 5,
            out_specs=anywhere,
            scratch_shapes=[
                pltpu.SMEM(((TABLE_ROWS + 1) * TABLE_ROWS,), jnp.int32),
                pltpu.SMEM((owners,), jnp.int32),
                pltpu.VMEM((second_total + 1, side, side), second.dtype),
                pltpu.VMEM(early.shape, early.dtype),
                pltpu.VMEM((rows * kept, side, side), second.dtype),
                pltpu.SemaphoreType.DMA,
                pltpu.SemaphoreType.DMA,
                pltpu.SemaphoreType.DMA,
            ],
        ),
        out_shape=jax.ShapeDtypeStruct(blank.shape, blank.dtype),
        input_output_aliases={12: 0},
        compiler_params=pltpu.CompilerParams(vmem_limit_bytes=LARGE_VMEM_LIMIT),
        cost_estimate=pl.CostEstimate(flops=1024, bytes_accessed=1024, transcendentals=0),
    )(
        first_meta, second_meta, kept_columns, owner, place,
        early, late, before, second, part_a, part_b, part_c, blank,
    )


def cut_kernel(start, place, source, *rest):
    held, in_sem, out_sem = rest[-3:]
    targets = rest[:-3]

    @pl.when(place[0] != 0)
    def _():
        loads, stores, at = [], [], 0
        for n, target in enumerate(targets):
            piece, size = pl.ds(start + at, target.shape[0]), pl.ds(at, target.shape[0])
            loads.append(pltpu.make_async_copy(source.at[piece], held.at[size], in_sem.at[n]))
            stores.append(pltpu.make_async_copy(held.at[size], target, out_sem.at[n]))
            at += target.shape[0]
        for load in loads:
            load.start()
        for load, store in zip(loads, stores):
            load.wait()
            store.start()
        for store in stores:
            store.wait()


def cut(place, value, start, sizes):
    return pl.pallas_call(
        functools.partial(cut_kernel, start),
        in_specs=[pl.BlockSpec(memory_space=pltpu.SMEM), pl.BlockSpec(memory_space=pl.ANY)],
        out_specs=[pl.BlockSpec(memory_space=pl.ANY)] * len(sizes),
        out_shape=[jax.ShapeDtypeStruct((size,) + value.shape[1:], value.dtype) for size in sizes],
        scratch_shapes=[
            pltpu.VMEM((sum(sizes),) + value.shape[1:], value.dtype),
            pltpu.SemaphoreType.DMA((len(sizes),)),
            pltpu.SemaphoreType.DMA((len(sizes),)),
        ],
        compiler_params=pltpu.CompilerParams(vmem_limit_bytes=LARGE_VMEM_LIMIT),
        cost_estimate=pl.CostEstimate(flops=1024, bytes_accessed=1024, transcendentals=0),
    )(place, value)


def copy_kernel(parts, source, target, sem):
    size = source.shape[0] // parts
    for j in range(parts):
        piece = pl.ds(j * size, size)
        pltpu.make_async_copy(source.at[piece], target.at[piece], sem).start()
    pltpu.make_async_copy(source, target, sem).wait()


def hand_over(value):
    return pl.pallas_call(
        functools.partial(copy_kernel, 16),
        in_specs=[pl.BlockSpec(memory_space=pl.ANY)],
        out_specs=pl.BlockSpec(memory_space=pl.ANY),
        out_shape=jax.ShapeDtypeStruct(value.shape, value.dtype),
        scratch_shapes=[pltpu.SemaphoreType.DMA],
        compiler_params=pltpu.CompilerParams(vmem_limit_bytes=VMEM_LIMIT),
    )(value)


def on_device(a_blocks, a_cols, a_count, b_blocks, b_cols, b_count, c_cols, c_owner):
    devices = lax.axis_size("row") * lax.axis_size("col")
    span = lax.axis_size("col") // 2
    rows, kept = c_cols.shape[1], c_cols.shape[2]
    side = a_blocks.shape[3]
    per_owner = max(2, 3 * rows * kept // (2 * devices))
    first = a_blocks[0].reshape(-1, side, side)
    second = b_blocks[0].reshape(-1, side, side)
    total = second.shape[0]
    large = total * 17 // 40
    spot = lax.axis_index("col") % span
    crossing = (spot == 0).astype(jnp.int32)[None]

    last, middle = span - 1, span - 3

    def near(r, c):
        return r ^ 1, c

    def far(r, c):
        return r ^ 1, c + span

    def at(place, step):
        return lambda r, c: step(r, c) if c % span == place else None

    (part_a,) = cut(crossing, second, 0, (large,))
    part_a = move(part_a, at(0, near))
    part_b, part_c = cut(crossing, second, large, (large, total - 2 * large))
    part_b = move(part_b, at(0, lambda r, c: far(r, c + last)))
    part_c = move(part_c, at(0, lambda r, c: (r, c + middle)))
    early = move(first, lambda r, c: (r - 1, c) if c % span > 1 else None)
    second_next = move(second, lambda r, c: (r, c - 1) if c % span else None)

    own_first_meta = flat_meta(a_cols[0], a_count[0])
    own_second_meta = flat_meta(b_cols[0], b_count[0])
    kept_columns = c_cols[0].reshape(-1)
    owner = c_owner[0, :, 0]
    before, blank = first_stop(
        own_first_meta, own_second_meta, kept_columns, first, second, devices * per_owner
    )

    part_a, part_b, part_c, first, before, blank = lax.optimization_barrier(
        (part_a, part_b, part_c, first, before, blank)
    )
    late = move(first, lambda r, c: (r - 1, c) if c % span < 2 else None)
    part_a = move(part_a, at(0, lambda r, c: far(r, c + last)))
    part_c = move(part_c, at(middle, far))
    part_b, part_c = lax.optimization_barrier((part_b, part_c))
    part_b = move(part_b, at(last, near))

    part_a, part_c, early, second_next, first_meta, second_meta = lax.optimization_barrier(
        (part_a, part_c, early, second_next, own_first_meta, own_second_meta)
    )
    part_c = move(part_c, at(middle, near))
    first_meta = move(first_meta, lambda r, c: (r - 1, c))
    second_meta = move(second_meta, lambda r, c: (r, c - 1))
    part_c = move(part_c, at(middle, lambda r, c: (r, c + last - middle)))

    place = jnp.stack([spot == span - 1, spot < 2]).astype(jnp.int32)
    outgoing = last_stop(
        first_meta, second_meta, kept_columns, owner, place,
        early, late, before, second_next, part_a, part_b, part_c, blank, devices,
    )
    arrived = lax.all_to_all(
        outgoing.reshape(devices, per_owner, side, side),
        ("row", "col"),
        split_axis=0,
        concat_axis=0,
        tiled=True,
    )
    return hand_over(arrived).reshape(1, devices, per_owner, side, side)


def solution(mesh):
    return jax.shard_map(
        on_device,
        mesh=mesh,
        in_specs=(
            P("row", "col", None, None, None),
            P("row", "col", None),
            P("row", "col"),
            P("col", "row", None, None, None),
            P("col", "row", None),
            P("col", "row"),
            P("row", "col", None),
            P("row", "col", None),
        ),
        out_specs=P(("row", "col"), None, None, None, None),
        check_vma=False,
    )
```

```python
import functools

import jax
import jax.numpy as jnp
from jax import lax
from jax.experimental import pallas as pl
from jax.experimental.pallas import tpu as pltpu
from jax.sharding import PartitionSpec as P

VMEM_LIMIT = 40 * 1024 * 1024
LARGE_VMEM_LIMIT = 62 * 1024 * 1024
TABLE_ROWS = 20
PIECE = 4


def move(value, chosen):
    rows, cols = lax.axis_size("row"), lax.axis_size("col")
    pairs = []
    for r in range(rows):
        for c in range(cols):
            to = chosen(r, c)
            if to is not None:
                pairs.append((r * cols + c, (to[0] % rows) * cols + to[1] % cols))
    return lax.ppermute(value, ("row", "col"), pairs)


def flat_meta(columns, counts):
    return jnp.concatenate([columns.reshape(-1), counts])


def fill_table(table, meta, slots, width):
    panel_rows = meta.shape[0] // (slots + 1)
    blank = panel_rows * slots

    def clear(n, carry):
        table[n] = blank
        return carry

    lax.fori_loop(0, table.shape[0], clear, 0, unroll=width)
    for k in range(panel_rows):
        count = meta[blank + k]
        columns = [meta[k * slots + b] for b in range(slots)]
        for b in range(slots):
            table[k * width + columns[b]] = jnp.where(b < count, k * slots + b, blank)


def load_pieces(source, target, sem):
    total = source.shape[0]
    for at in range(0, total, PIECE):
        piece = pl.ds(at, min(PIECE, total - at))
        pltpu.make_async_copy(source.at[piece], target.at[piece], sem).start()


def row_products(table, first_meta, kept_columns, i, slots, kept, rows, held, put):
    width = table.shape[0] // (TABLE_ROWS + 1)
    side = held.shape[1]
    row_total = kept_columns.shape[0] // kept
    count = first_meta[row_total * slots + i]

    def over(terms):
        starts = [
            jnp.where(a < count, first_meta[i * slots + a] * width, TABLE_ROWS * width)
            for a in range(terms)
        ]
        left = jnp.concatenate([rows[i * slots + a] for a in range(terms)], axis=1)
        for f in range(0, kept, 2):
            picked = []
            for g in range(2):
                column = kept_columns[i * kept + f + g]
                blocks = [held[table[start + column]] for start in starts]
                picked.append(jnp.concatenate(blocks, axis=0))
            right = jnp.concatenate(picked, axis=1)
            both = jnp.dot(left, right, preferred_element_type=jnp.float32)
            put(f, both[:, :side])
            put(f + 1, both[:, side:])

    fewer = -1
    for terms in (slots // 2, slots * 3 // 4, slots):
        pl.when((count > fewer) & (count <= terms))(functools.partial(over, terms))
        fewer = terms


def first_stop_kernel(
    first_meta, second_meta, kept_columns, first, second,
    total, blank, table, held, rows, sums, zeros, held_sem, row_sem, sum_sem, blank_sem,
):
    i = pl.program_id(0)
    kept = total.shape[0] // pl.num_programs(0)
    slots = rows.shape[0] * kept // kept_columns.shape[0]
    part = zeros.shape[0]
    panel = held.at[pl.ds(0, second.shape[0])]

    @pl.when(i == 0)
    def _():
        load_pieces(second, panel, held_sem)
        load_pieces(first, rows, row_sem)
        held[second.shape[0]] = jnp.zeros(held.shape[1:], held.dtype)
        zeros[...] = jnp.zeros(zeros.shape, zeros.dtype)
        fill_table(table, second_meta, slots, table.shape[0] // (TABLE_ROWS + 1))
        pltpu.make_async_copy(rows, rows, row_sem).wait()
        pltpu.make_async_copy(panel, panel, held_sem).wait()
        for j in range(blank.shape[0] // part):
            pltpu.make_async_copy(zeros, blank.at[pl.ds(j * part, part)], blank_sem).start()

    def put(f, value):
        l = i * kept + f
        sums[l] = value
        pltpu.make_async_copy(sums.at[l], total.at[l], sum_sem).start()

    row_products(table, first_meta, kept_columns, i, slots, kept, rows, held, put)

    @pl.when(i == pl.num_programs(0) - 1)
    def _():
        pltpu.make_async_copy(sums, total, sum_sem).wait()
        pltpu.make_async_copy(blank, blank, blank_sem).wait()


def last_stop_kernel(
    first_meta, second_meta, kept_columns, owner, place,
    early, late, before, second, part_a, part_b, part_c, blank,
    out, table, used, held, rows, sums, product, held_sem, row_sem, sum_sem, out_sem,
):
    del blank
    i = pl.program_id(0)
    row_total = pl.num_programs(0)
    kept = before.shape[0] // row_total
    slots = rows.shape[0] * kept // kept_columns.shape[0]
    per_owner = out.shape[0] // used.shape[0]
    total = held.shape[0] - 1
    panel = held.at[pl.ds(0, total)]

    @pl.when(i == 0)
    def _():
        @pl.when(place[0] == 0)
        def _():
            load_pieces(second, panel, held_sem)

        @pl.when(place[0] != 0)
        def _():
            at = 0
            for part in (part_a, part_b, part_c):
                load_pieces(part, held.at[pl.ds(at, part.shape[0])], held_sem)
                at += part.shape[0]

        @pl.when(place[1] == 0)
        def _():
            load_pieces(early, rows, row_sem)

        @pl.when(place[1] != 0)
        def _():
            load_pieces(late, rows, row_sem)

        for j in range(sum_sem.shape[0]):
            row = pl.ds(j * kept, kept)
            load_pieces(before.at[row], sums.at[row], sum_sem.at[j])

        held[total] = jnp.zeros(held.shape[1:], held.dtype)

        def clear(n, carry):
            used[n] = 0
            return carry

        lax.fori_loop(0, used.shape[0], clear, 0, unroll=16)
        fill_table(table, second_meta, slots, table.shape[0] // (TABLE_ROWS + 1))
        pltpu.make_async_copy(rows, rows, row_sem).wait()
        pltpu.make_async_copy(panel, panel, held_sem).wait()

    row = sums.at[pl.ds(i * kept, kept)]
    pltpu.make_async_copy(row, row, sum_sem.at[i]).wait()

    def put(f, value):
        l = i * kept + f
        product[l] = (value + sums[l]).astype(product.dtype)
        rank = used[owner[l]]
        used[owner[l]] = rank + 1
        slot = owner[l] * per_owner + rank
        pltpu.make_async_copy(product.at[l], out.at[slot], out_sem).start()

    row_products(table, first_meta, kept_columns, i, slots, kept, rows, held, put)

    @pl.when(i == pl.num_programs(0) - 1)
    def _():
        pltpu.make_async_copy(product, out.at[pl.ds(0, product.shape[0])], out_sem).wait()


def first_stop(first_meta, second_meta, kept_columns, first, second, outgoing):
    first_total, side, _ = first.shape
    rows = first_meta.shape[0] - first_total
    kept = kept_columns.shape[0] // rows
    second_total = second.shape[0]
    part = 16
    return pl.pallas_call(
        first_stop_kernel,
        grid_spec=pltpu.PrefetchScalarGridSpec(
            num_scalar_prefetch=3,
            grid=(rows,),
            in_specs=[pl.BlockSpec(memory_space=pl.ANY)] * 2,
            out_specs=[pl.BlockSpec(memory_space=pl.ANY)] * 2,
            scratch_shapes=[
                pltpu.SMEM(((TABLE_ROWS + 1) * TABLE_ROWS,), jnp.int32),
                pltpu.VMEM((second_total + 1, side, side), second.dtype),
                pltpu.VMEM(first.shape, first.dtype),
                pltpu.VMEM((rows * kept, side, side), jnp.float32),
                pltpu.VMEM((part, side, side), second.dtype),
                pltpu.SemaphoreType.DMA,
                pltpu.SemaphoreType.DMA,
                pltpu.SemaphoreType.DMA,
                pltpu.SemaphoreType.DMA,
            ],
        ),
        out_shape=[
            jax.ShapeDtypeStruct((rows * kept, side, side), jnp.float32),
            jax.ShapeDtypeStruct((outgoing, side, side), second.dtype),
        ],
        compiler_params=pltpu.CompilerParams(vmem_limit_bytes=LARGE_VMEM_LIMIT),
        cost_estimate=pl.CostEstimate(
            flops=400 * first_total * kept * side**3,
            bytes_accessed=2 * (first_total * 2 + rows * kept * 4 + 2 * second_total) * side**2,
            transcendentals=0,
        ),
    )(first_meta, second_meta, kept_columns, first, second)


def last_stop(
    first_meta, second_meta, kept_columns, owner, place,
    early, late, before, second, part_a, part_b, part_c, blank, owners,
):
    side = early.shape[1]
    rows = first_meta.shape[0] - early.shape[0]
    second_total = second.shape[0]
    anywhere = pl.BlockSpec(memory_space=pl.ANY)
    return pl.pallas_call(
        last_stop_kernel,
        grid_spec=pltpu.PrefetchScalarGridSpec(
            num_scalar_prefetch=5,
            grid=(rows,),
            in_specs=[anywhere] * 8,
            out_specs=anywhere,
            scratch_shapes=[
                pltpu.SMEM(((TABLE_ROWS + 1) * TABLE_ROWS,), jnp.int32),
                pltpu.SMEM((owners,), jnp.int32),
                pltpu.VMEM((second_total + 1, side, side), second.dtype),
                pltpu.VMEM(early.shape, early.dtype),
                pltpu.VMEM(before.shape, before.dtype),
                pltpu.VMEM(before.shape, second.dtype),
                pltpu.SemaphoreType.DMA,
                pltpu.SemaphoreType.DMA,
                pltpu.SemaphoreType.DMA((rows,)),
                pltpu.SemaphoreType.DMA,
            ],
        ),
        out_shape=jax.ShapeDtypeStruct(blank.shape, blank.dtype),
        input_output_aliases={12: 0},
        compiler_params=pltpu.CompilerParams(vmem_limit_bytes=LARGE_VMEM_LIMIT),
        cost_estimate=pl.CostEstimate(flops=1024, bytes_accessed=1024, transcendentals=0),
    )(
        first_meta, second_meta, kept_columns, owner, place,
        early, late, before, second, part_a, part_b, part_c, blank,
    )


def cut_kernel(start, place, source, *rest):
    held, in_sem, out_sem = rest[-3:]
    targets = rest[:-3]

    @pl.when(place[0] != 0)
    def _():
        loads, stores, at = [], [], 0
        for n, target in enumerate(targets):
            piece, size = pl.ds(start + at, target.shape[0]), pl.ds(at, target.shape[0])
            loads.append(pltpu.make_async_copy(source.at[piece], held.at[size], in_sem.at[n]))
            stores.append(pltpu.make_async_copy(held.at[size], target, out_sem.at[n]))
            at += target.shape[0]
        for load in loads:
            load.start()
        for load, store in zip(loads, stores):
            load.wait()
            store.start()
        for store in stores:
            store.wait()


def cut(place, value, start, sizes):
    return pl.pallas_call(
        functools.partial(cut_kernel, start),
        in_specs=[pl.BlockSpec(memory_space=pltpu.SMEM), pl.BlockSpec(memory_space=pl.ANY)],
        out_specs=[pl.BlockSpec(memory_space=pl.ANY)] * len(sizes),
        out_shape=[jax.ShapeDtypeStruct((size,) + value.shape[1:], value.dtype) for size in sizes],
        scratch_shapes=[
            pltpu.VMEM((sum(sizes),) + value.shape[1:], value.dtype),
            pltpu.SemaphoreType.DMA((len(sizes),)),
            pltpu.SemaphoreType.DMA((len(sizes),)),
        ],
        compiler_params=pltpu.CompilerParams(vmem_limit_bytes=LARGE_VMEM_LIMIT),
        cost_estimate=pl.CostEstimate(flops=1024, bytes_accessed=1024, transcendentals=0),
    )(place, value)


def copy_kernel(parts, source, target, sem):
    size = source.shape[0] // parts
    for j in range(parts):
        piece = pl.ds(j * size, size)
        pltpu.make_async_copy(source.at[piece], target.at[piece], sem).start()
    pltpu.make_async_copy(source, target, sem).wait()


def hand_over(value):
    return pl.pallas_call(
        functools.partial(copy_kernel, 16),
        in_specs=[pl.BlockSpec(memory_space=pl.ANY)],
        out_specs=pl.BlockSpec(memory_space=pl.ANY),
        out_shape=jax.ShapeDtypeStruct(value.shape, value.dtype),
        scratch_shapes=[pltpu.SemaphoreType.DMA],
        compiler_params=pltpu.CompilerParams(vmem_limit_bytes=VMEM_LIMIT),
    )(value)


def on_device(a_blocks, a_cols, a_count, b_blocks, b_cols, b_count, c_cols, c_owner):
    devices = lax.axis_size("row") * lax.axis_size("col")
    span = lax.axis_size("col") // 2
    rows, kept = c_cols.shape[1], c_cols.shape[2]
    side = a_blocks.shape[3]
    per_owner = max(2, 3 * rows * kept // (2 * devices))
    first = a_blocks[0].reshape(-1, side, side)
    second = b_blocks[0].reshape(-1, side, side)
    total = second.shape[0]
    large = total * 17 // 40
    spot = lax.axis_index("col") % span
    crossing = (spot == 0).astype(jnp.int32)[None]

    last, middle = span - 1, span - 3

    def near(r, c):
        return r ^ 1, c

    def far(r, c):
        return r ^ 1, c + span

    def at(place, step):
        return lambda r, c: step(r, c) if c % span == place else None

    (part_a,) = cut(crossing, second, 0, (large,))
    part_a = move(part_a, at(0, near))
    part_b, part_c = cut(crossing, second, large, (large, total - 2 * large))
    part_b = move(part_b, at(0, lambda r, c: far(r, c + last)))
    part_c = move(part_c, at(0, lambda r, c: (r, c + middle)))
    early = move(first, lambda r, c: (r - 1, c) if c % span > 1 else None)
    second_next = move(second, lambda r, c: (r, c - 1) if c % span else None)

    own_first_meta = flat_meta(a_cols[0], a_count[0])
    own_second_meta = flat_meta(b_cols[0], b_count[0])
    kept_columns = c_cols[0].reshape(-1)
    owner = c_owner[0, :, 0]
    before, blank = first_stop(
        own_first_meta, own_second_meta, kept_columns, first, second, devices * per_owner
    )

    part_a, part_b, part_c, first, before, blank = lax.optimization_barrier(
        (part_a, part_b, part_c, first, before, blank)
    )
    late = move(first, lambda r, c: (r - 1, c) if c % span < 2 else None)
    part_a = move(part_a, at(0, lambda r, c: far(r, c + last)))
    part_c = move(part_c, at(middle, far))
    part_b, part_c = lax.optimization_barrier((part_b, part_c))
    part_b = move(part_b, at(last, near))

    part_a, part_c, early, second_next, first_meta, second_meta = lax.optimization_barrier(
        (part_a, part_c, early, second_next, own_first_meta, own_second_meta)
    )
    part_c = move(part_c, at(middle, near))
    first_meta = move(first_meta, lambda r, c: (r - 1, c))
    second_meta = move(second_meta, lambda r, c: (r, c - 1))
    part_c = move(part_c, at(middle, lambda r, c: (r, c + last - middle)))

    place = jnp.stack([spot == span - 1, spot < 2]).astype(jnp.int32)
    outgoing = last_stop(
        first_meta, second_meta, kept_columns, owner, place,
        early, late, before, second_next, part_a, part_b, part_c, blank, devices,
    )
    arrived = lax.all_to_all(
        outgoing.reshape(devices, per_owner, side, side),
        ("row", "col"),
        split_axis=0,
        concat_axis=0,
        tiled=True,
    )
    return hand_over(arrived).reshape(1, devices, per_owner, side, side)


def solution(mesh):
    return jax.shard_map(
        on_device,
        mesh=mesh,
        in_specs=(
            P("row", "col", None, None, None),
            P("row", "col", None),
            P("row", "col"),
            P("col", "row", None, None, None),
            P("col", "row", None),
            P("col", "row"),
            P("row", "col", None),
            P("row", "col", None),
        ),
        out_specs=P(("row", "col"), None, None, None, None),
        check_vma=False,
    )
```

```python
import functools

import jax
import jax.numpy as jnp
from jax import lax
from jax.experimental import pallas as pl
from jax.experimental.pallas import tpu as pltpu
from jax.sharding import PartitionSpec as P

VMEM_LIMIT = 40 * 1024 * 1024
LARGE_VMEM_LIMIT = 62 * 1024 * 1024
TABLE_ROWS = 20
PIECE = 4


def move(value, chosen):
    rows, cols = lax.axis_size("row"), lax.axis_size("col")
    pairs = []
    for r in range(rows):
        for c in range(cols):
            to = chosen(r, c)
            if to is not None:
                pairs.append((r * cols + c, (to[0] % rows) * cols + to[1] % cols))
    return lax.ppermute(value, ("row", "col"), pairs)


def flat_meta(columns, counts):
    return jnp.concatenate([columns.reshape(-1), counts])


def fill_table(table, meta, slots, width):
    panel_rows = meta.shape[0] // (slots + 1)
    blank = panel_rows * slots

    def clear(n, carry):
        table[n] = blank
        return carry

    lax.fori_loop(0, table.shape[0], clear, 0, unroll=width)
    for k in range(panel_rows):
        count = meta[blank + k]
        columns = [meta[k * slots + b] for b in range(slots)]
        for b in range(slots):
            table[k * width + columns[b]] = jnp.where(b < count, k * slots + b, blank)


def load_pieces(source, target, sem):
    total = source.shape[0]
    for at in range(0, total, PIECE):
        piece = pl.ds(at, min(PIECE, total - at))
        pltpu.make_async_copy(source.at[piece], target.at[piece], sem).start()


def row_products(table, first_meta, kept_columns, i, slots, kept, rows, held, put):
    width = table.shape[0] // (TABLE_ROWS + 1)
    side = held.shape[1]
    row_total = kept_columns.shape[0] // kept
    count = first_meta[row_total * slots + i]

    def over(terms):
        starts = [
            jnp.where(a < count, first_meta[i * slots + a] * width, TABLE_ROWS * width)
            for a in range(terms)
        ]
        left = jnp.concatenate([rows[i * slots + a] for a in range(terms)], axis=1)
        for f in range(0, kept, 2):
            picked = []
            for g in range(2):
                column = kept_columns[i * kept + f + g]
                blocks = [held[table[start + column]] for start in starts]
                picked.append(jnp.concatenate(blocks, axis=0))
            right = jnp.concatenate(picked, axis=1)
            both = jnp.dot(left, right, preferred_element_type=jnp.float32)
            put(f, both[:, :side])
            put(f + 1, both[:, side:])

    fewer = -1
    for terms in (slots // 2, slots * 3 // 4, slots):
        pl.when((count > fewer) & (count <= terms))(functools.partial(over, terms))
        fewer = terms


def first_stop_kernel(
    first_meta, second_meta, kept_columns, first, second,
    total, blank, table, held, rows, zeros, held_sem, row_sem, blank_sem,
):
    i = pl.program_id(0)
    kept = total.shape[1]
    slots = rows.shape[0] * kept // kept_columns.shape[0]
    part = zeros.shape[0]
    panel = held.at[pl.ds(0, second.shape[0])]

    @pl.when(i == 0)
    def _():
        load_pieces(second, panel, held_sem)
        load_pieces(first, rows, row_sem)
        held[second.shape[0]] = jnp.zeros(held.shape[1:], held.dtype)
        zeros[...] = jnp.zeros(zeros.shape, zeros.dtype)
        fill_table(table, second_meta, slots, table.shape[0] // (TABLE_ROWS + 1))
        pltpu.make_async_copy(rows, rows, row_sem).wait()
        pltpu.make_async_copy(panel, panel, held_sem).wait()
        for j in range(blank.shape[0] // part):
            pltpu.make_async_copy(zeros, blank.at[pl.ds(j * part, part)], blank_sem).start()

    def put(f, value):
        total[0, f] = value

    row_products(table, first_meta, kept_columns, i, slots, kept, rows, held, put)

    @pl.when(i == pl.num_programs(0) - 1)
    def _():
        pltpu.make_async_copy(blank, blank, blank_sem).wait()


def last_stop_kernel(
    first_meta, second_meta, kept_columns, owner, place,
    early, late, before, second, part_a, part_b, part_c, blank,
    out, table, used, held, rows, sums, product, held_sem, row_sem, sum_sem, out_sem,
):
    del blank
    i = pl.program_id(0)
    row_total = pl.num_programs(0)
    kept = before.shape[0] // row_total
    slots = rows.shape[0] * kept // kept_columns.shape[0]
    per_owner = out.shape[0] // used.shape[0]
    total = held.shape[0] - 1
    panel = held.at[pl.ds(0, total)]

    @pl.when(i == 0)
    def _():
        @pl.when(place[0] == 0)
        def _():
            load_pieces(second, panel, held_sem)

        @pl.when(place[0] != 0)
        def _():
            at = 0
            for part in (part_a, part_b, part_c):
                load_pieces(part, held.at[pl.ds(at, part.shape[0])], held_sem)
                at += part.shape[0]

        @pl.when(place[1] == 0)
        def _():
            load_pieces(early, rows, row_sem)

        @pl.when(place[1] != 0)
        def _():
            load_pieces(late, rows, row_sem)

        for j in range(sum_sem.shape[0]):
            row = pl.ds(j * kept, kept)
            load_pieces(before.at[row], sums.at[row], sum_sem.at[j])

        held[total] = jnp.zeros(held.shape[1:], held.dtype)

        def clear(n, carry):
            used[n] = 0
            return carry

        lax.fori_loop(0, used.shape[0], clear, 0, unroll=16)
        fill_table(table, second_meta, slots, table.shape[0] // (TABLE_ROWS + 1))
        pltpu.make_async_copy(rows, rows, row_sem).wait()
        pltpu.make_async_copy(panel, panel, held_sem).wait()

    row = sums.at[pl.ds(i * kept, kept)]
    pltpu.make_async_copy(row, row, sum_sem.at[i]).wait()

    def put(f, value):
        l = i * kept + f
        product[l] = (value + sums[l]).astype(product.dtype)
        rank = used[owner[l]]
        used[owner[l]] = rank + 1
        slot = owner[l] * per_owner + rank
        pltpu.make_async_copy(product.at[l], out.at[slot], out_sem).start()

    row_products(table, first_meta, kept_columns, i, slots, kept, rows, held, put)

    @pl.when(i == pl.num_programs(0) - 1)
    def _():
        pltpu.make_async_copy(product, out.at[pl.ds(0, product.shape[0])], out_sem).wait()


def first_stop(first_meta, second_meta, kept_columns, first, second, outgoing):
    first_total, side, _ = first.shape
    rows = first_meta.shape[0] - first_total
    kept = kept_columns.shape[0] // rows
    second_total = second.shape[0]
    part = 16
    return pl.pallas_call(
        first_stop_kernel,
        grid_spec=pltpu.PrefetchScalarGridSpec(
            num_scalar_prefetch=3,
            grid=(rows,),
            in_specs=[pl.BlockSpec(memory_space=pl.ANY)] * 2,
            out_specs=[
                pl.BlockSpec((1, kept, side, side), lambda i, *_: (i, 0, 0, 0)),
                pl.BlockSpec(memory_space=pl.ANY),
            ],
            scratch_shapes=[
                pltpu.SMEM(((TABLE_ROWS + 1) * TABLE_ROWS,), jnp.int32),
                pltpu.VMEM((second_total + 1, side, side), second.dtype),
                pltpu.VMEM(first.shape, first.dtype),
                pltpu.VMEM((part, side, side), second.dtype),
                pltpu.SemaphoreType.DMA,
                pltpu.SemaphoreType.DMA,
                pltpu.SemaphoreType.DMA,
            ],
        ),
        out_shape=[
            jax.ShapeDtypeStruct((rows, kept, side, side), jnp.float32),
            jax.ShapeDtypeStruct((outgoing, side, side), second.dtype),
        ],
        compiler_params=pltpu.CompilerParams(vmem_limit_bytes=LARGE_VMEM_LIMIT),
        cost_estimate=pl.CostEstimate(
            flops=400 * first_total * kept * side**3,
            bytes_accessed=2 * (first_total * 2 + rows * kept * 4 + 2 * second_total) * side**2,
            transcendentals=0,
        ),
    )(first_meta, second_meta, kept_columns, first, second)


def last_stop(
    first_meta, second_meta, kept_columns, owner, place,
    early, late, before, second, part_a, part_b, part_c, blank, owners,
):
    side = early.shape[1]
    rows = first_meta.shape[0] - early.shape[0]
    second_total = second.shape[0]
    anywhere = pl.BlockSpec(memory_space=pl.ANY)
    return pl.pallas_call(
        last_stop_kernel,
        grid_spec=pltpu.PrefetchScalarGridSpec(
            num_scalar_prefetch=5,
            grid=(rows,),
            in_specs=[anywhere] * 8,
            out_specs=anywhere,
            scratch_shapes=[
                pltpu.SMEM(((TABLE_ROWS + 1) * TABLE_ROWS,), jnp.int32),
                pltpu.SMEM((owners,), jnp.int32),
                pltpu.VMEM((second_total + 1, side, side), second.dtype),
                pltpu.VMEM(early.shape, early.dtype),
                pltpu.VMEM(before.shape, before.dtype),
                pltpu.VMEM(before.shape, second.dtype),
                pltpu.SemaphoreType.DMA,
                pltpu.SemaphoreType.DMA,
                pltpu.SemaphoreType.DMA((rows,)),
                pltpu.SemaphoreType.DMA,
            ],
        ),
        out_shape=jax.ShapeDtypeStruct(blank.shape, blank.dtype),
        input_output_aliases={12: 0},
        compiler_params=pltpu.CompilerParams(vmem_limit_bytes=LARGE_VMEM_LIMIT),
        cost_estimate=pl.CostEstimate(flops=1024, bytes_accessed=1024, transcendentals=0),
    )(
        first_meta, second_meta, kept_columns, owner, place,
        early, late, before, second, part_a, part_b, part_c, blank,
    )


def cut_kernel(start, place, source, *rest):
    held, in_sem, out_sem = rest[-3:]
    targets = rest[:-3]

    @pl.when(place[0] != 0)
    def _():
        loads, stores, at = [], [], 0
        for n, target in enumerate(targets):
            piece, size = pl.ds(start + at, target.shape[0]), pl.ds(at, target.shape[0])
            loads.append(pltpu.make_async_copy(source.at[piece], held.at[size], in_sem.at[n]))
            stores.append(pltpu.make_async_copy(held.at[size], target, out_sem.at[n]))
            at += target.shape[0]
        for load in loads:
            load.start()
        for load, store in zip(loads, stores):
            load.wait()
            store.start()
        for store in stores:
            store.wait()


def cut(place, value, start, sizes):
    return pl.pallas_call(
        functools.partial(cut_kernel, start),
        in_specs=[pl.BlockSpec(memory_space=pltpu.SMEM), pl.BlockSpec(memory_space=pl.ANY)],
        out_specs=[pl.BlockSpec(memory_space=pl.ANY)] * len(sizes),
        out_shape=[jax.ShapeDtypeStruct((size,) + value.shape[1:], value.dtype) for size in sizes],
        scratch_shapes=[
            pltpu.VMEM((sum(sizes),) + value.shape[1:], value.dtype),
            pltpu.SemaphoreType.DMA((len(sizes),)),
            pltpu.SemaphoreType.DMA((len(sizes),)),
        ],
        compiler_params=pltpu.CompilerParams(vmem_limit_bytes=LARGE_VMEM_LIMIT),
        cost_estimate=pl.CostEstimate(flops=1024, bytes_accessed=1024, transcendentals=0),
    )(place, value)


def copy_kernel(parts, source, target, sem):
    size = source.shape[0] // parts
    for j in range(parts):
        piece = pl.ds(j * size, size)
        pltpu.make_async_copy(source.at[piece], target.at[piece], sem).start()
    pltpu.make_async_copy(source, target, sem).wait()


def hand_over(value):
    return pl.pallas_call(
        functools.partial(copy_kernel, 16),
        in_specs=[pl.BlockSpec(memory_space=pl.ANY)],
        out_specs=pl.BlockSpec(memory_space=pl.ANY),
        out_shape=jax.ShapeDtypeStruct(value.shape, value.dtype),
        scratch_shapes=[pltpu.SemaphoreType.DMA],
        compiler_params=pltpu.CompilerParams(vmem_limit_bytes=VMEM_LIMIT),
    )(value)


def on_device(a_blocks, a_cols, a_count, b_blocks, b_cols, b_count, c_cols, c_owner):
    devices = lax.axis_size("row") * lax.axis_size("col")
    span = lax.axis_size("col") // 2
    rows, kept = c_cols.shape[1], c_cols.shape[2]
    side = a_blocks.shape[3]
    per_owner = max(2, 3 * rows * kept // (2 * devices))
    first = a_blocks[0].reshape(-1, side, side)
    second = b_blocks[0].reshape(-1, side, side)
    total = second.shape[0]
    large = total * 17 // 40
    spot = lax.axis_index("col") % span
    crossing = (spot == 0).astype(jnp.int32)[None]

    last, middle = span - 1, span - 3

    def near(r, c):
        return r ^ 1, c

    def far(r, c):
        return r ^ 1, c + span

    def at(place, step):
        return lambda r, c: step(r, c) if c % span == place else None

    (part_a,) = cut(crossing, second, 0, (large,))
    part_a = move(part_a, at(0, near))
    part_b, part_c = cut(crossing, second, large, (large, total - 2 * large))
    part_b = move(part_b, at(0, lambda r, c: far(r, c + last)))
    part_c = move(part_c, at(0, lambda r, c: (r, c + middle)))
    early = move(first, lambda r, c: (r - 1, c) if c % span > 1 else None)
    second_next = move(second, lambda r, c: (r, c - 1) if c % span else None)

    own_first_meta = flat_meta(a_cols[0], a_count[0])
    own_second_meta = flat_meta(b_cols[0], b_count[0])
    kept_columns = c_cols[0].reshape(-1)
    owner = c_owner[0, :, 0]
    before, blank = first_stop(
        own_first_meta, own_second_meta, kept_columns, first, second, devices * per_owner
    )

    part_a, part_b, part_c, first, before, blank = lax.optimization_barrier(
        (part_a, part_b, part_c, first, before, blank)
    )
    late = move(first, lambda r, c: (r - 1, c) if c % span < 2 else None)
    part_a = move(part_a, at(0, lambda r, c: far(r, c + last)))
    part_c = move(part_c, at(middle, far))
    part_b, part_c = lax.optimization_barrier((part_b, part_c))
    part_b = move(part_b, at(last, near))

    part_a, part_c, early, second_next, first_meta, second_meta = lax.optimization_barrier(
        (part_a, part_c, early, second_next, own_first_meta, own_second_meta)
    )
    part_c = move(part_c, at(middle, near))
    first_meta = move(first_meta, lambda r, c: (r - 1, c))
    second_meta = move(second_meta, lambda r, c: (r, c - 1))
    part_c = move(part_c, at(middle, lambda r, c: (r, c + last - middle)))

    place = jnp.stack([spot == span - 1, spot < 2]).astype(jnp.int32)
    outgoing = last_stop(
        first_meta, second_meta, kept_columns, owner, place,
        early, late, before.reshape(-1, side, side), second_next, part_a, part_b, part_c, blank, devices,
    )
    arrived = lax.all_to_all(
        outgoing.reshape(devices, per_owner, side, side),
        ("row", "col"),
        split_axis=0,
        concat_axis=0,
        tiled=True,
    )
    return hand_over(arrived).reshape(1, devices, per_owner, side, side)


def solution(mesh):
    return jax.shard_map(
        on_device,
        mesh=mesh,
        in_specs=(
            P("row", "col", None, None, None),
            P("row", "col", None),
            P("row", "col"),
            P("col", "row", None, None, None),
            P("col", "row", None),
            P("col", "row"),
            P("row", "col", None),
            P("row", "col", None),
        ),
        out_specs=P(("row", "col"), None, None, None, None),
        check_vma=False,
    )
```

```python
import functools

import jax
import jax.numpy as jnp
from jax import lax
from jax.experimental import pallas as pl
from jax.experimental.pallas import tpu as pltpu
from jax.sharding import PartitionSpec as P

VMEM_LIMIT = 40 * 1024 * 1024
LARGE_VMEM_LIMIT = 62 * 1024 * 1024
TABLE_ROWS = 20
PIECE = 4
AHEAD = 2


def move(value, chosen):
    rows, cols = lax.axis_size("row"), lax.axis_size("col")
    pairs = []
    for r in range(rows):
        for c in range(cols):
            to = chosen(r, c)
            if to is not None:
                pairs.append((r * cols + c, (to[0] % rows) * cols + to[1] % cols))
    return lax.ppermute(value, ("row", "col"), pairs)


def flat_meta(columns, counts):
    return jnp.concatenate([columns.reshape(-1), counts])


def fill_table(table, meta, slots, width):
    panel_rows = meta.shape[0] // (slots + 1)
    blank = panel_rows * slots

    def clear(n, carry):
        table[n] = blank
        return carry

    lax.fori_loop(0, table.shape[0], clear, 0, unroll=width)
    for k in range(panel_rows):
        count = meta[blank + k]
        columns = [meta[k * slots + b] for b in range(slots)]
        for b in range(slots):
            table[k * width + columns[b]] = jnp.where(b < count, k * slots + b, blank)


def load_pieces(source, target, sem):
    total = source.shape[0]
    for at in range(0, total, PIECE):
        piece = pl.ds(at, min(PIECE, total - at))
        pltpu.make_async_copy(source.at[piece], target.at[piece], sem).start()


def row_products(table, first_meta, kept_columns, i, slots, kept, rows, held, put):
    width = table.shape[0] // (TABLE_ROWS + 1)
    side = held.shape[1]
    row_total = kept_columns.shape[0] // kept
    count = first_meta[row_total * slots + i]

    def over(terms):
        starts = [
            jnp.where(a < count, first_meta[i * slots + a] * width, TABLE_ROWS * width)
            for a in range(terms)
        ]
        left = jnp.concatenate([rows[i * slots + a] for a in range(terms)], axis=1)
        for f in range(0, kept, 2):
            picked = []
            for g in range(2):
                column = kept_columns[i * kept + f + g]
                blocks = [held[table[start + column]] for start in starts]
                picked.append(jnp.concatenate(blocks, axis=0))
            right = jnp.concatenate(picked, axis=1)
            both = jnp.dot(left, right, preferred_element_type=jnp.float32)
            put(f, both[:, :side])
            put(f + 1, both[:, side:])

    fewer = -1
    for terms in (slots // 2, slots * 3 // 4, slots):
        pl.when((count > fewer) & (count <= terms))(functools.partial(over, terms))
        fewer = terms


def first_stop_kernel(
    first_meta, second_meta, kept_columns, first, second,
    total, blank, table, held, rows, zeros, held_sem, row_sem, blank_sem,
):
    i = pl.program_id(0)
    kept = total.shape[1]
    slots = rows.shape[0] * kept // kept_columns.shape[0]
    part = zeros.shape[0]
    panel = held.at[pl.ds(0, second.shape[0])]

    @pl.when(i == 0)
    def _():
        load_pieces(second, panel, held_sem)
        load_pieces(first, rows, row_sem)
        held[second.shape[0]] = jnp.zeros(held.shape[1:], held.dtype)
        zeros[...] = jnp.zeros(zeros.shape, zeros.dtype)
        fill_table(table, second_meta, slots, table.shape[0] // (TABLE_ROWS + 1))
        pltpu.make_async_copy(rows, rows, row_sem).wait()
        pltpu.make_async_copy(panel, panel, held_sem).wait()
        for j in range(blank.shape[0] // part):
            pltpu.make_async_copy(zeros, blank.at[pl.ds(j * part, part)], blank_sem).start()

    def put(f, value):
        total[0, f] = value

    row_products(table, first_meta, kept_columns, i, slots, kept, rows, held, put)

    @pl.when(i == pl.num_programs(0) - 1)
    def _():
        pltpu.make_async_copy(blank, blank, blank_sem).wait()


def last_stop_kernel(
    first_meta, second_meta, kept_columns, owner, place,
    early, late, before, second, part_a, part_b, part_c, blank,
    out, table, used, held, rows, sums, product, held_sem, row_sem, sum_sem, out_sem,
):
    del blank
    i = pl.program_id(0)
    row_total = pl.num_programs(0)
    kept = before.shape[0] // row_total
    slots = rows.shape[0] * kept // kept_columns.shape[0]
    per_owner = out.shape[0] // used.shape[0]
    total = held.shape[0] - 1
    panel = held.at[pl.ds(0, total)]

    def load_row(j):
        row = pl.ds(j * slots, slots)

        @pl.when(place[1] == 0)
        def _():
            load_pieces(early.at[row], rows.at[row], row_sem.at[j])

        @pl.when(place[1] != 0)
        def _():
            load_pieces(late.at[row], rows.at[row], row_sem.at[j])

        row = pl.ds(j * kept, kept)
        load_pieces(before.at[row], sums.at[row], sum_sem.at[j])

    @pl.when(i == 0)
    def _():
        @pl.when(place[0] == 0)
        def _():
            load_pieces(second, panel, held_sem)

        @pl.when(place[0] != 0)
        def _():
            at = 0
            for part in (part_a, part_b, part_c):
                load_pieces(part, held.at[pl.ds(at, part.shape[0])], held_sem)
                at += part.shape[0]

        for j in range(AHEAD):
            load_row(j)

        held[total] = jnp.zeros(held.shape[1:], held.dtype)

        def clear(n, carry):
            used[n] = 0
            return carry

        lax.fori_loop(0, used.shape[0], clear, 0, unroll=16)
        fill_table(table, second_meta, slots, table.shape[0] // (TABLE_ROWS + 1))
        pltpu.make_async_copy(panel, panel, held_sem).wait()

    @pl.when(i + AHEAD < row_total)
    def _():
        load_row(i + AHEAD)

    row = rows.at[pl.ds(i * slots, slots)]
    pltpu.make_async_copy(row, row, row_sem.at[i]).wait()
    row = sums.at[pl.ds(i * kept, kept)]
    pltpu.make_async_copy(row, row, sum_sem.at[i]).wait()

    def put(f, value):
        l = i * kept + f
        product[l] = (value + sums[l]).astype(product.dtype)
        rank = used[owner[l]]
        used[owner[l]] = rank + 1
        slot = owner[l] * per_owner + rank
        pltpu.make_async_copy(product.at[l], out.at[slot], out_sem).start()

    row_products(table, first_meta, kept_columns, i, slots, kept, rows, held, put)

    @pl.when(i == pl.num_programs(0) - 1)
    def _():
        pltpu.make_async_copy(product, out.at[pl.ds(0, product.shape[0])], out_sem).wait()


def first_stop(first_meta, second_meta, kept_columns, first, second, outgoing):
    first_total, side, _ = first.shape
    rows = first_meta.shape[0] - first_total
    kept = kept_columns.shape[0] // rows
    second_total = second.shape[0]
    part = 16
    return pl.pallas_call(
        first_stop_kernel,
        grid_spec=pltpu.PrefetchScalarGridSpec(
            num_scalar_prefetch=3,
            grid=(rows,),
            in_specs=[pl.BlockSpec(memory_space=pl.ANY)] * 2,
            out_specs=[
                pl.BlockSpec((1, kept, side, side), lambda i, *_: (i, 0, 0, 0)),
                pl.BlockSpec(memory_space=pl.ANY),
            ],
            scratch_shapes=[
                pltpu.SMEM(((TABLE_ROWS + 1) * TABLE_ROWS,), jnp.int32),
                pltpu.VMEM((second_total + 1, side, side), second.dtype),
                pltpu.VMEM(first.shape, first.dtype),
                pltpu.VMEM((part, side, side), second.dtype),
                pltpu.SemaphoreType.DMA,
                pltpu.SemaphoreType.DMA,
                pltpu.SemaphoreType.DMA,
            ],
        ),
        out_shape=[
            jax.ShapeDtypeStruct((rows, kept, side, side), jnp.float32),
            jax.ShapeDtypeStruct((outgoing, side, side), second.dtype),
        ],
        compiler_params=pltpu.CompilerParams(vmem_limit_bytes=LARGE_VMEM_LIMIT),
        cost_estimate=pl.CostEstimate(
            flops=400 * first_total * kept * side**3,
            bytes_accessed=2 * (first_total * 2 + rows * kept * 4 + 2 * second_total) * side**2,
            transcendentals=0,
        ),
    )(first_meta, second_meta, kept_columns, first, second)


def last_stop(
    first_meta, second_meta, kept_columns, owner, place,
    early, late, before, second, part_a, part_b, part_c, blank, owners,
):
    side = early.shape[1]
    rows = first_meta.shape[0] - early.shape[0]
    second_total = second.shape[0]
    anywhere = pl.BlockSpec(memory_space=pl.ANY)
    return pl.pallas_call(
        last_stop_kernel,
        grid_spec=pltpu.PrefetchScalarGridSpec(
            num_scalar_prefetch=5,
            grid=(rows,),
            in_specs=[anywhere] * 8,
            out_specs=anywhere,
            scratch_shapes=[
                pltpu.SMEM(((TABLE_ROWS + 1) * TABLE_ROWS,), jnp.int32),
                pltpu.SMEM((owners,), jnp.int32),
                pltpu.VMEM((second_total + 1, side, side), second.dtype),
                pltpu.VMEM(early.shape, early.dtype),
                pltpu.VMEM(before.shape, before.dtype),
                pltpu.VMEM(before.shape, second.dtype),
                pltpu.SemaphoreType.DMA,
                pltpu.SemaphoreType.DMA((rows,)),
                pltpu.SemaphoreType.DMA((rows,)),
                pltpu.SemaphoreType.DMA,
            ],
        ),
        out_shape=jax.ShapeDtypeStruct(blank.shape, blank.dtype),
        input_output_aliases={12: 0},
        compiler_params=pltpu.CompilerParams(vmem_limit_bytes=LARGE_VMEM_LIMIT),
        cost_estimate=pl.CostEstimate(flops=1024, bytes_accessed=1024, transcendentals=0),
    )(
        first_meta, second_meta, kept_columns, owner, place,
        early, late, before, second, part_a, part_b, part_c, blank,
    )


def cut_kernel(start, place, source, *rest):
    held, in_sem, out_sem = rest[-3:]
    targets = rest[:-3]

    @pl.when(place[0] != 0)
    def _():
        loads, stores, at = [], [], 0
        for n, target in enumerate(targets):
            piece, size = pl.ds(start + at, target.shape[0]), pl.ds(at, target.shape[0])
            loads.append(pltpu.make_async_copy(source.at[piece], held.at[size], in_sem.at[n]))
            stores.append(pltpu.make_async_copy(held.at[size], target, out_sem.at[n]))
            at += target.shape[0]
        for load in loads:
            load.start()
        for load, store in zip(loads, stores):
            load.wait()
            store.start()
        for store in stores:
            store.wait()


def cut(place, value, start, sizes):
    return pl.pallas_call(
        functools.partial(cut_kernel, start),
        in_specs=[pl.BlockSpec(memory_space=pltpu.SMEM), pl.BlockSpec(memory_space=pl.ANY)],
        out_specs=[pl.BlockSpec(memory_space=pl.ANY)] * len(sizes),
        out_shape=[jax.ShapeDtypeStruct((size,) + value.shape[1:], value.dtype) for size in sizes],
        scratch_shapes=[
            pltpu.VMEM((sum(sizes),) + value.shape[1:], value.dtype),
            pltpu.SemaphoreType.DMA((len(sizes),)),
            pltpu.SemaphoreType.DMA((len(sizes),)),
        ],
        compiler_params=pltpu.CompilerParams(vmem_limit_bytes=LARGE_VMEM_LIMIT),
        cost_estimate=pl.CostEstimate(flops=1024, bytes_accessed=1024, transcendentals=0),
    )(place, value)


def copy_kernel(parts, source, target, sem):
    size = source.shape[0] // parts
    for j in range(parts):
        piece = pl.ds(j * size, size)
        pltpu.make_async_copy(source.at[piece], target.at[piece], sem).start()
    pltpu.make_async_copy(source, target, sem).wait()


def hand_over(value):
    return pl.pallas_call(
        functools.partial(copy_kernel, 16),
        in_specs=[pl.BlockSpec(memory_space=pl.ANY)],
        out_specs=pl.BlockSpec(memory_space=pl.ANY),
        out_shape=jax.ShapeDtypeStruct(value.shape, value.dtype),
        scratch_shapes=[pltpu.SemaphoreType.DMA],
        compiler_params=pltpu.CompilerParams(vmem_limit_bytes=VMEM_LIMIT),
    )(value)


def on_device(a_blocks, a_cols, a_count, b_blocks, b_cols, b_count, c_cols, c_owner):
    devices = lax.axis_size("row") * lax.axis_size("col")
    span = lax.axis_size("col") // 2
    rows, kept = c_cols.shape[1], c_cols.shape[2]
    side = a_blocks.shape[3]
    per_owner = max(2, 3 * rows * kept // (2 * devices))
    first = a_blocks[0].reshape(-1, side, side)
    second = b_blocks[0].reshape(-1, side, side)
    total = second.shape[0]
    large_a, large_b = total * 17 // 40, total * 7 // 16
    spot = lax.axis_index("col") % span
    crossing = (spot == 0).astype(jnp.int32)[None]

    last, middle = span - 1, span - 3

    def near(r, c):
        return r ^ 1, c

    def far(r, c):
        return r ^ 1, c + span

    def at(place, step):
        return lambda r, c: step(r, c) if c % span == place else None

    (part_a,) = cut(crossing, second, 0, (large_a,))
    part_a = move(part_a, at(0, near))
    part_b, part_c = cut(crossing, second, large_a, (large_b, total - large_a - large_b))
    part_b = move(part_b, at(0, lambda r, c: far(r, c + last)))
    part_c = move(part_c, at(0, lambda r, c: (r, c + middle)))
    early = move(first, lambda r, c: (r - 1, c) if c % span > 1 else None)
    second_next = move(second, lambda r, c: (r, c - 1) if c % span else None)

    own_first_meta = flat_meta(a_cols[0], a_count[0])
    own_second_meta = flat_meta(b_cols[0], b_count[0])
    kept_columns = c_cols[0].reshape(-1)
    owner = c_owner[0, :, 0]
    before, blank = first_stop(
        own_first_meta, own_second_meta, kept_columns, first, second, devices * per_owner
    )

    part_a, part_b, part_c, first, before, blank = lax.optimization_barrier(
        (part_a, part_b, part_c, first, before, blank)
    )
    late = move(first, lambda r, c: (r - 1, c) if c % span < 2 else None)
    part_a = move(part_a, at(0, lambda r, c: far(r, c + last)))
    part_c = move(part_c, at(middle, far))
    part_b, part_c = lax.optimization_barrier((part_b, part_c))
    part_b = move(part_b, at(last, near))

    part_a, part_c, early, second_next, first_meta, second_meta = lax.optimization_barrier(
        (part_a, part_c, early, second_next, own_first_meta, own_second_meta)
    )
    part_c = move(part_c, at(middle, near))
    first_meta = move(first_meta, lambda r, c: (r - 1, c))
    second_meta = move(second_meta, lambda r, c: (r, c - 1))
    part_c = move(part_c, at(middle, lambda r, c: (r, c + last - middle)))

    place = jnp.stack([spot == span - 1, spot < 2]).astype(jnp.int32)
    outgoing = last_stop(
        first_meta, second_meta, kept_columns, owner, place,
        early, late, before.reshape(-1, side, side), second_next, part_a, part_b, part_c, blank, devices,
    )
    arrived = lax.all_to_all(
        outgoing.reshape(devices, per_owner, side, side),
        ("row", "col"),
        split_axis=0,
        concat_axis=0,
        tiled=True,
    )
    return hand_over(arrived).reshape(1, devices, per_owner, side, side)


def solution(mesh):
    return jax.shard_map(
        on_device,
        mesh=mesh,
        in_specs=(
            P("row", "col", None, None, None),
            P("row", "col", None),
            P("row", "col"),
            P("col", "row", None, None, None),
            P("col", "row", None),
            P("col", "row"),
            P("row", "col", None),
            P("row", "col", None),
        ),
        out_specs=P(("row", "col"), None, None, None, None),
        check_vma=False,
    )
```

```python
import functools

import jax
import jax.numpy as jnp
from jax import lax
from jax.experimental import pallas as pl
from jax.experimental.pallas import tpu as pltpu
from jax.sharding import PartitionSpec as P

VMEM_LIMIT = 40 * 1024 * 1024
LARGE_VMEM_LIMIT = 62 * 1024 * 1024
TABLE_ROWS = 20
PIECE = 4
AHEAD = 2


def move(value, chosen):
    rows, cols = lax.axis_size("row"), lax.axis_size("col")
    pairs = []
    for r in range(rows):
        for c in range(cols):
            to = chosen(r, c)
            if to is not None:
                pairs.append((r * cols + c, (to[0] % rows) * cols + to[1] % cols))
    return lax.ppermute(value, ("row", "col"), pairs)


def flat_meta(columns, counts):
    return jnp.concatenate([columns.reshape(-1), counts])


def fill_table(table, meta, slots, width):
    panel_rows = meta.shape[0] // (slots + 1)
    blank = panel_rows * slots

    def clear(n, carry):
        table[n] = blank
        return carry

    lax.fori_loop(0, table.shape[0], clear, 0, unroll=width)
    for k in range(panel_rows):
        count = meta[blank + k]
        columns = [meta[k * slots + b] for b in range(slots)]
        for b in range(slots):
            table[k * width + columns[b]] = jnp.where(b < count, k * slots + b, blank)


def load_pieces(source, target, sem):
    total = source.shape[0]
    for at in range(0, total, PIECE):
        piece = pl.ds(at, min(PIECE, total - at))
        pltpu.make_async_copy(source.at[piece], target.at[piece], sem).start()


def row_products(table, first_meta, kept_columns, i, slots, kept, rows, held, put):
    width = table.shape[0] // (TABLE_ROWS + 1)
    side = held.shape[1]
    row_total = kept_columns.shape[0] // kept
    count = first_meta[row_total * slots + i]

    def over(terms):
        starts = [
            jnp.where(a < count, first_meta[i * slots + a] * width, TABLE_ROWS * width)
            for a in range(terms)
        ]
        left = jnp.concatenate([rows[i * slots + a] for a in range(terms)], axis=1)
        for f in range(0, kept, 2):
            picked = []
            for g in range(2):
                column = kept_columns[i * kept + f + g]
                blocks = [held[table[start + column]] for start in starts]
                picked.append(jnp.concatenate(blocks, axis=0))
            right = jnp.concatenate(picked, axis=1)
            both = jnp.dot(left, right, preferred_element_type=jnp.float32)
            put(f, both[:, :side])
            put(f + 1, both[:, side:])

    fewer = -1
    for terms in (slots // 2, slots * 3 // 4, slots):
        pl.when((count > fewer) & (count <= terms))(functools.partial(over, terms))
        fewer = terms


def first_stop_kernel(
    first_meta, second_meta, kept_columns, first, second,
    total, blank, table, held, rows, zeros, held_sem, row_sem, blank_sem,
):
    i = pl.program_id(0)
    kept = total.shape[1]
    slots = rows.shape[0] * kept // kept_columns.shape[0]
    part = zeros.shape[0]
    panel = held.at[pl.ds(0, second.shape[0])]

    @pl.when(i == 0)
    def _():
        load_pieces(second, panel, held_sem)
        load_pieces(first, rows, row_sem)
        held[second.shape[0]] = jnp.zeros(held.shape[1:], held.dtype)
        zeros[...] = jnp.zeros(zeros.shape, zeros.dtype)
        fill_table(table, second_meta, slots, table.shape[0] // (TABLE_ROWS + 1))
        pltpu.make_async_copy(rows, rows, row_sem).wait()
        pltpu.make_async_copy(panel, panel, held_sem).wait()
        for j in range(blank.shape[0] // part):
            pltpu.make_async_copy(zeros, blank.at[pl.ds(j * part, part)], blank_sem).start()

    def put(f, value):
        total[0, f] = value

    row_products(table, first_meta, kept_columns, i, slots, kept, rows, held, put)

    @pl.when(i == pl.num_programs(0) - 1)
    def _():
        pltpu.make_async_copy(blank, blank, blank_sem).wait()


def last_stop_kernel(
    first_meta, second_meta, kept_columns, owner, place,
    early, late, before, second, part_a, part_b, part_c, blank,
    out, table, used, held, rows, sums, product, held_sem, row_sem, sum_sem, out_sem,
):
    del blank
    i = pl.program_id(0)
    row_total = pl.num_programs(0)
    kept = before.shape[0] // row_total
    slots = rows.shape[0] * kept // kept_columns.shape[0]
    per_owner = out.shape[0] // used.shape[0]
    total = held.shape[0] - 1
    panel = held.at[pl.ds(0, total)]

    def load_row(j):
        row = pl.ds(j * slots, slots)

        @pl.when(place[1] == 0)
        def _():
            load_pieces(early.at[row], rows.at[row], row_sem.at[j])

        @pl.when(place[1] != 0)
        def _():
            load_pieces(late.at[row], rows.at[row], row_sem.at[j])

        row = pl.ds(j * kept, kept)
        load_pieces(before.at[row], sums.at[row], sum_sem.at[j])

    @pl.when(i == 0)
    def _():
        @pl.when(place[0] == 0)
        def _():
            load_pieces(second, panel, held_sem)

        @pl.when(place[0] != 0)
        def _():
            at = 0
            for part in (part_a, part_b, part_c):
                load_pieces(part, held.at[pl.ds(at, part.shape[0])], held_sem)
                at += part.shape[0]

        for j in range(AHEAD):
            load_row(j)

        held[total] = jnp.zeros(held.shape[1:], held.dtype)

        def clear(n, carry):
            used[n] = 0
            return carry

        lax.fori_loop(0, used.shape[0], clear, 0, unroll=16)
        fill_table(table, second_meta, slots, table.shape[0] // (TABLE_ROWS + 1))
        pltpu.make_async_copy(panel, panel, held_sem).wait()

    @pl.when(i + AHEAD < row_total)
    def _():
        load_row(i + AHEAD)

    row = rows.at[pl.ds(i * slots, slots)]
    pltpu.make_async_copy(row, row, row_sem.at[i]).wait()
    row = sums.at[pl.ds(i * kept, kept)]
    pltpu.make_async_copy(row, row, sum_sem.at[i]).wait()

    def put(f, value):
        l = i * kept + f
        product[l] = (value + sums[l]).astype(product.dtype)
        rank = used[owner[l]]
        used[owner[l]] = rank + 1
        slot = owner[l] * per_owner + rank
        pltpu.make_async_copy(product.at[l], out.at[slot], out_sem).start()

    row_products(table, first_meta, kept_columns, i, slots, kept, rows, held, put)

    @pl.when(i == pl.num_programs(0) - 1)
    def _():
        pltpu.make_async_copy(product, out.at[pl.ds(0, product.shape[0])], out_sem).wait()


def first_stop(first_meta, second_meta, kept_columns, first, second, outgoing):
    first_total, side, _ = first.shape
    rows = first_meta.shape[0] - first_total
    kept = kept_columns.shape[0] // rows
    second_total = second.shape[0]
    part = 16
    return pl.pallas_call(
        first_stop_kernel,
        grid_spec=pltpu.PrefetchScalarGridSpec(
            num_scalar_prefetch=3,
            grid=(rows,),
            in_specs=[pl.BlockSpec(memory_space=pl.ANY)] * 2,
            out_specs=[
                pl.BlockSpec((1, kept, side, side), lambda i, *_: (i, 0, 0, 0)),
                pl.BlockSpec(memory_space=pl.ANY),
            ],
            scratch_shapes=[
                pltpu.SMEM(((TABLE_ROWS + 1) * TABLE_ROWS,), jnp.int32),
                pltpu.VMEM((second_total + 1, side, side), second.dtype),
                pltpu.VMEM(first.shape, first.dtype),
                pltpu.VMEM((part, side, side), second.dtype),
                pltpu.SemaphoreType.DMA,
                pltpu.SemaphoreType.DMA,
                pltpu.SemaphoreType.DMA,
            ],
        ),
        out_shape=[
            jax.ShapeDtypeStruct((rows, kept, side, side), jnp.float32),
            jax.ShapeDtypeStruct((outgoing, side, side), second.dtype),
        ],
        compiler_params=pltpu.CompilerParams(vmem_limit_bytes=LARGE_VMEM_LIMIT),
        cost_estimate=pl.CostEstimate(
            flops=400 * first_total * kept * side**3,
            bytes_accessed=2 * (first_total * 2 + rows * kept * 4 + 2 * second_total) * side**2,
            transcendentals=0,
        ),
    )(first_meta, second_meta, kept_columns, first, second)


def last_stop(
    first_meta, second_meta, kept_columns, owner, place,
    early, late, before, second, part_a, part_b, part_c, blank, owners,
):
    side = early.shape[1]
    rows = first_meta.shape[0] - early.shape[0]
    second_total = second.shape[0]
    anywhere = pl.BlockSpec(memory_space=pl.ANY)
    return pl.pallas_call(
        last_stop_kernel,
        grid_spec=pltpu.PrefetchScalarGridSpec(
            num_scalar_prefetch=5,
            grid=(rows,),
            in_specs=[anywhere] * 8,
            out_specs=anywhere,
            scratch_shapes=[
                pltpu.SMEM(((TABLE_ROWS + 1) * TABLE_ROWS,), jnp.int32),
                pltpu.SMEM((owners,), jnp.int32),
                pltpu.VMEM((second_total + 1, side, side), second.dtype),
                pltpu.VMEM(early.shape, early.dtype),
                pltpu.VMEM(before.shape, before.dtype),
                pltpu.VMEM(before.shape, second.dtype),
                pltpu.SemaphoreType.DMA,
                pltpu.SemaphoreType.DMA((rows,)),
                pltpu.SemaphoreType.DMA((rows,)),
                pltpu.SemaphoreType.DMA,
            ],
        ),
        out_shape=jax.ShapeDtypeStruct(blank.shape, blank.dtype),
        input_output_aliases={12: 0},
        compiler_params=pltpu.CompilerParams(vmem_limit_bytes=LARGE_VMEM_LIMIT),
        cost_estimate=pl.CostEstimate(flops=1024, bytes_accessed=1024, transcendentals=0),
    )(
        first_meta, second_meta, kept_columns, owner, place,
        early, late, before, second, part_a, part_b, part_c, blank,
    )


def cut_kernel(start, place, source, *rest):
    held, in_sem, out_sem = rest[-3:]
    targets = rest[:-3]

    @pl.when(place[0] != 0)
    def _():
        loads, stores, at = [], [], 0
        for n, target in enumerate(targets):
            piece, size = pl.ds(start + at, target.shape[0]), pl.ds(at, target.shape[0])
            loads.append(pltpu.make_async_copy(source.at[piece], held.at[size], in_sem.at[n]))
            stores.append(pltpu.make_async_copy(held.at[size], target, out_sem.at[n]))
            at += target.shape[0]
        for load in loads:
            load.start()
        for load, store in zip(loads, stores):
            load.wait()
            store.start()
        for store in stores:
            store.wait()


def cut(place, value, start, sizes):
    return pl.pallas_call(
        functools.partial(cut_kernel, start),
        in_specs=[pl.BlockSpec(memory_space=pltpu.SMEM), pl.BlockSpec(memory_space=pl.ANY)],
        out_specs=[pl.BlockSpec(memory_space=pl.ANY)] * len(sizes),
        out_shape=[jax.ShapeDtypeStruct((size,) + value.shape[1:], value.dtype) for size in sizes],
        scratch_shapes=[
            pltpu.VMEM((sum(sizes),) + value.shape[1:], value.dtype),
            pltpu.SemaphoreType.DMA((len(sizes),)),
            pltpu.SemaphoreType.DMA((len(sizes),)),
        ],
        compiler_params=pltpu.CompilerParams(vmem_limit_bytes=LARGE_VMEM_LIMIT),
        cost_estimate=pl.CostEstimate(flops=1024, bytes_accessed=1024, transcendentals=0),
    )(place, value)


def copy_kernel(parts, source, target, sem):
    size = source.shape[0] // parts
    for j in range(parts):
        piece = pl.ds(j * size, size)
        pltpu.make_async_copy(source.at[piece], target.at[piece], sem).start()
    pltpu.make_async_copy(source, target, sem).wait()


def hand_over(value):
    return pl.pallas_call(
        functools.partial(copy_kernel, 16),
        in_specs=[pl.BlockSpec(memory_space=pl.ANY)],
        out_specs=pl.BlockSpec(memory_space=pl.ANY),
        out_shape=jax.ShapeDtypeStruct(value.shape, value.dtype),
        scratch_shapes=[pltpu.SemaphoreType.DMA],
        compiler_params=pltpu.CompilerParams(vmem_limit_bytes=VMEM_LIMIT),
    )(value)


def on_device(a_blocks, a_cols, a_count, b_blocks, b_cols, b_count, c_cols, c_owner):
    devices = lax.axis_size("row") * lax.axis_size("col")
    span = lax.axis_size("col") // 2
    rows, kept = c_cols.shape[1], c_cols.shape[2]
    side = a_blocks.shape[3]
    per_owner = max(2, 3 * rows * kept // (2 * devices))
    first = a_blocks[0].reshape(-1, side, side)
    second = b_blocks[0].reshape(-1, side, side)
    total = second.shape[0]
    large_a, large_b = total * 17 // 40, total * 7 // 16
    spot = lax.axis_index("col") % span
    crossing = (spot == 0).astype(jnp.int32)[None]

    last, middle = span - 1, span - 3

    def near(r, c):
        return r ^ 1, c

    def far(r, c):
        return r ^ 1, c + span

    def at(place, step):
        return lambda r, c: step(r, c) if c % span == place else None

    (part_a,) = cut(crossing, second, 0, (large_a,))
    part_a = move(part_a, at(0, near))
    part_b, part_c = cut(crossing, second, large_a, (large_b, total - large_a - large_b))
    part_b = move(part_b, at(0, lambda r, c: far(r, c + last)))
    part_c = move(part_c, at(0, lambda r, c: (r, c + middle)))
    early = move(first, lambda r, c: (r - 1, c) if c % span > 1 else None)
    second_next = move(second, lambda r, c: (r, c - 1) if c % span else None)

    own_first_meta = flat_meta(a_cols[0], a_count[0])
    own_second_meta = flat_meta(b_cols[0], b_count[0])
    kept_columns = c_cols[0].reshape(-1)
    owner = c_owner[0, :, 0]
    before, blank = first_stop(
        own_first_meta, own_second_meta, kept_columns, first, second, devices * per_owner
    )

    part_a, part_c, first, before, blank = lax.optimization_barrier(
        (part_a, part_c, first, before, blank)
    )
    late = move(first, lambda r, c: (r - 1, c) if c % span < 2 else None)
    part_a = move(part_a, at(0, lambda r, c: far(r, c + last)))
    part_c = move(part_c, at(middle, far))
    part_b, part_c = lax.optimization_barrier((part_b, part_c))
    part_b = move(part_b, at(last, near))

    part_a, part_c, early, second_next, first_meta, second_meta = lax.optimization_barrier(
        (part_a, part_c, early, second_next, own_first_meta, own_second_meta)
    )
    part_c = move(part_c, at(middle, near))
    first_meta = move(first_meta, lambda r, c: (r - 1, c))
    second_meta = move(second_meta, lambda r, c: (r, c - 1))
    part_c = move(part_c, at(middle, lambda r, c: (r, c + last - middle)))

    place = jnp.stack([spot == span - 1, spot < 2]).astype(jnp.int32)
    outgoing = last_stop(
        first_meta, second_meta, kept_columns, owner, place,
        early, late, before.reshape(-1, side, side), second_next, part_a, part_b, part_c, blank, devices,
    )
    arrived = lax.all_to_all(
        outgoing.reshape(devices, per_owner, side, side),
        ("row", "col"),
        split_axis=0,
        concat_axis=0,
        tiled=True,
    )
    return hand_over(arrived).reshape(1, devices, per_owner, side, side)


def solution(mesh):
    return jax.shard_map(
        on_device,
        mesh=mesh,
        in_specs=(
            P("row", "col", None, None, None),
            P("row", "col", None),
            P("row", "col"),
            P("col", "row", None, None, None),
            P("col", "row", None),
            P("col", "row"),
            P("row", "col", None),
            P("row", "col", None),
        ),
        out_specs=P(("row", "col"), None, None, None, None),
        check_vma=False,
    )
```

```python
import functools

import jax
import jax.numpy as jnp
from jax import lax
from jax.experimental import pallas as pl
from jax.experimental.pallas import tpu as pltpu
from jax.sharding import PartitionSpec as P

VMEM_LIMIT = 40 * 1024 * 1024
LARGE_VMEM_LIMIT = 62 * 1024 * 1024
TABLE_ROWS = 20
PIECE = 4
AHEAD = 2


def move(value, chosen):
    rows, cols = lax.axis_size("row"), lax.axis_size("col")
    pairs = []
    for r in range(rows):
        for c in range(cols):
            to = chosen(r, c)
            if to is not None:
                pairs.append((r * cols + c, (to[0] % rows) * cols + to[1] % cols))
    return lax.ppermute(value, ("row", "col"), pairs)


def flat_meta(columns, counts):
    return jnp.concatenate([columns.reshape(-1), counts])


def fill_table(table, meta, slots, width):
    panel_rows = meta.shape[0] // (slots + 1)
    blank = panel_rows * slots

    def clear(n, carry):
        table[n] = blank
        return carry

    lax.fori_loop(0, table.shape[0], clear, 0, unroll=width)
    for k in range(panel_rows):
        count = meta[blank + k]
        columns = [meta[k * slots + b] for b in range(slots)]
        for b in range(slots):
            table[k * width + columns[b]] = jnp.where(b < count, k * slots + b, blank)


def load_pieces(source, target, sem):
    total = source.shape[0]
    for at in range(0, total, PIECE):
        piece = pl.ds(at, min(PIECE, total - at))
        pltpu.make_async_copy(source.at[piece], target.at[piece], sem).start()


def row_products(table, first_meta, kept_columns, i, slots, kept, rows, held, put):
    width = table.shape[0] // (TABLE_ROWS + 1)
    side = held.shape[1]
    row_total = kept_columns.shape[0] // kept
    count = first_meta[row_total * slots + i]

    def over(terms):
        starts = [
            jnp.where(a < count, first_meta[i * slots + a] * width, TABLE_ROWS * width)
            for a in range(terms)
        ]
        left = jnp.concatenate([rows[i * slots + a] for a in range(terms)], axis=1)
        for f in range(0, kept, 2):
            picked = []
            for g in range(2):
                column = kept_columns[i * kept + f + g]
                blocks = [held[table[start + column]] for start in starts]
                picked.append(jnp.concatenate(blocks, axis=0))
            right = jnp.concatenate(picked, axis=1)
            both = jnp.dot(left, right, preferred_element_type=jnp.float32)
            put(f, both[:, :side])
            put(f + 1, both[:, side:])

    fewer = -1
    for terms in (slots // 2, slots * 3 // 4, slots):
        pl.when((count > fewer) & (count <= terms))(functools.partial(over, terms))
        fewer = terms


def first_stop_kernel(
    first_meta, second_meta, kept_columns, first, second,
    total, blank, table, held, rows, sums, zeros, held_sem, row_sem, sum_sem, blank_sem,
):
    i = pl.program_id(0)
    kept = total.shape[0] // pl.num_programs(0)
    slots = rows.shape[0] * kept // kept_columns.shape[0]
    part = zeros.shape[0]
    panel = held.at[pl.ds(0, second.shape[0])]

    @pl.when(i == 0)
    def _():
        load_pieces(second, panel, held_sem)
        load_pieces(first, rows, row_sem)
        held[second.shape[0]] = jnp.zeros(held.shape[1:], held.dtype)
        zeros[...] = jnp.zeros(zeros.shape, zeros.dtype)
        fill_table(table, second_meta, slots, table.shape[0] // (TABLE_ROWS + 1))
        pltpu.make_async_copy(rows, rows, row_sem).wait()
        pltpu.make_async_copy(panel, panel, held_sem).wait()
        for j in range(blank.shape[0] // part):
            pltpu.make_async_copy(zeros, blank.at[pl.ds(j * part, part)], blank_sem).start()

    def put(f, value):
        l = i * kept + f
        sums[l] = value
        pltpu.make_async_copy(sums.at[l], total.at[l], sum_sem).start()

    row_products(table, first_meta, kept_columns, i, slots, kept, rows, held, put)

    @pl.when(i == pl.num_programs(0) - 1)
    def _():
        pltpu.make_async_copy(sums, total, sum_sem).wait()
        pltpu.make_async_copy(blank, blank, blank_sem).wait()


def last_stop_kernel(
    first_meta, second_meta, kept_columns, owner, place,
    early, late, before, second, part_a, part_b, part_c, blank,
    out, table, used, held, rows, sums, product, held_sem, row_sem, sum_sem, out_sem,
):
    del blank
    i = pl.program_id(0)
    row_total = pl.num_programs(0)
    kept = before.shape[0] // row_total
    slots = rows.shape[0] * kept // kept_columns.shape[0]
    per_owner = out.shape[0] // used.shape[0]
    total = held.shape[0] - 1
    panel = held.at[pl.ds(0, total)]

    def load_row(j):
        row = pl.ds(j * slots, slots)

        @pl.when(place[1] == 0)
        def _():
            load_pieces(early.at[row], rows.at[row], row_sem.at[j])

        @pl.when(place[1] != 0)
        def _():
            load_pieces(late.at[row], rows.at[row], row_sem.at[j])

        row = pl.ds(j * kept, kept)
        load_pieces(before.at[row], sums.at[row], sum_sem.at[j])

    @pl.when(i == 0)
    def _():
        @pl.when(place[0] == 0)
        def _():
            load_pieces(second, panel, held_sem)

        @pl.when(place[0] != 0)
        def _():
            at = 0
            for part in (part_a, part_b, part_c):
                load_pieces(part, held.at[pl.ds(at, part.shape[0])], held_sem)
                at += part.shape[0]

        for j in range(AHEAD):
            load_row(j)

        held[total] = jnp.zeros(held.shape[1:], held.dtype)

        def clear(n, carry):
            used[n] = 0
            return carry

        lax.fori_loop(0, used.shape[0], clear, 0, unroll=16)
        fill_table(table, second_meta, slots, table.shape[0] // (TABLE_ROWS + 1))
        pltpu.make_async_copy(panel, panel, held_sem).wait()

    @pl.when(i + AHEAD < row_total)
    def _():
        load_row(i + AHEAD)

    row = rows.at[pl.ds(i * slots, slots)]
    pltpu.make_async_copy(row, row, row_sem.at[i]).wait()
    row = sums.at[pl.ds(i * kept, kept)]
    pltpu.make_async_copy(row, row, sum_sem.at[i]).wait()

    def put(f, value):
        l = i * kept + f
        product[l] = (value + sums[l]).astype(product.dtype)
        rank = used[owner[l]]
        used[owner[l]] = rank + 1
        slot = owner[l] * per_owner + rank
        pltpu.make_async_copy(product.at[l], out.at[slot], out_sem).start()

    row_products(table, first_meta, kept_columns, i, slots, kept, rows, held, put)

    @pl.when(i == pl.num_programs(0) - 1)
    def _():
        pltpu.make_async_copy(product, out.at[pl.ds(0, product.shape[0])], out_sem).wait()


def first_stop(first_meta, second_meta, kept_columns, first, second, outgoing):
    first_total, side, _ = first.shape
    rows = first_meta.shape[0] - first_total
    kept = kept_columns.shape[0] // rows
    second_total = second.shape[0]
    part = 16
    return pl.pallas_call(
        first_stop_kernel,
        grid_spec=pltpu.PrefetchScalarGridSpec(
            num_scalar_prefetch=3,
            grid=(rows,),
            in_specs=[pl.BlockSpec(memory_space=pl.ANY)] * 2,
            out_specs=[pl.BlockSpec(memory_space=pl.ANY)] * 2,
            scratch_shapes=[
                pltpu.SMEM(((TABLE_ROWS + 1) * TABLE_ROWS,), jnp.int32),
                pltpu.VMEM((second_total + 1, side, side), second.dtype),
                pltpu.VMEM(first.shape, first.dtype),
                pltpu.VMEM((rows * kept, side, side), jnp.float32),
                pltpu.VMEM((part, side, side), second.dtype),
                pltpu.SemaphoreType.DMA,
                pltpu.SemaphoreType.DMA,
                pltpu.SemaphoreType.DMA,
                pltpu.SemaphoreType.DMA,
            ],
        ),
        out_shape=[
            jax.ShapeDtypeStruct((rows * kept, side, side), jnp.float32),
            jax.ShapeDtypeStruct((outgoing, side, side), second.dtype),
        ],
        compiler_params=pltpu.CompilerParams(vmem_limit_bytes=LARGE_VMEM_LIMIT),
        cost_estimate=pl.CostEstimate(
            flops=400 * first_total * kept * side**3,
            bytes_accessed=2 * (first_total * 2 + rows * kept * 4 + 2 * second_total) * side**2,
            transcendentals=0,
        ),
    )(first_meta, second_meta, kept_columns, first, second)


def last_stop(
    first_meta, second_meta, kept_columns, owner, place,
    early, late, before, second, part_a, part_b, part_c, blank, owners,
):
    side = early.shape[1]
    rows = first_meta.shape[0] - early.shape[0]
    second_total = second.shape[0]
    anywhere = pl.BlockSpec(memory_space=pl.ANY)
    return pl.pallas_call(
        last_stop_kernel,
        grid_spec=pltpu.PrefetchScalarGridSpec(
            num_scalar_prefetch=5,
            grid=(rows,),
            in_specs=[anywhere] * 8,
            out_specs=anywhere,
            scratch_shapes=[
                pltpu.SMEM(((TABLE_ROWS + 1) * TABLE_ROWS,), jnp.int32),
                pltpu.SMEM((owners,), jnp.int32),
                pltpu.VMEM((second_total + 1, side, side), second.dtype),
                pltpu.VMEM(early.shape, early.dtype),
                pltpu.VMEM(before.shape, before.dtype),
                pltpu.VMEM(before.shape, second.dtype),
                pltpu.SemaphoreType.DMA,
                pltpu.SemaphoreType.DMA((rows,)),
                pltpu.SemaphoreType.DMA((rows,)),
                pltpu.SemaphoreType.DMA,
            ],
        ),
        out_shape=jax.ShapeDtypeStruct(blank.shape, blank.dtype),
        input_output_aliases={12: 0},
        compiler_params=pltpu.CompilerParams(vmem_limit_bytes=LARGE_VMEM_LIMIT),
        cost_estimate=pl.CostEstimate(flops=1024, bytes_accessed=1024, transcendentals=0),
    )(
        first_meta, second_meta, kept_columns, owner, place,
        early, late, before, second, part_a, part_b, part_c, blank,
    )


def cut_kernel(start, place, source, *rest):
    held, in_sem, out_sem = rest[-3:]
    targets = rest[:-3]

    @pl.when(place[0] != 0)
    def _():
        loads, stores, at = [], [], 0
        for n, target in enumerate(targets):
            piece, size = pl.ds(start + at, target.shape[0]), pl.ds(at, target.shape[0])
            loads.append(pltpu.make_async_copy(source.at[piece], held.at[size], in_sem.at[n]))
            stores.append(pltpu.make_async_copy(held.at[size], target, out_sem.at[n]))
            at += target.shape[0]
        for load in loads:
            load.start()
        for load, store in zip(loads, stores):
            load.wait()
            store.start()
        for store in stores:
            store.wait()


def cut(place, value, start, sizes):
    return pl.pallas_call(
        functools.partial(cut_kernel, start),
        in_specs=[pl.BlockSpec(memory_space=pltpu.SMEM), pl.BlockSpec(memory_space=pl.ANY)],
        out_specs=[pl.BlockSpec(memory_space=pl.ANY)] * len(sizes),
        out_shape=[jax.ShapeDtypeStruct((size,) + value.shape[1:], value.dtype) for size in sizes],
        scratch_shapes=[
            pltpu.VMEM((sum(sizes),) + value.shape[1:], value.dtype),
            pltpu.SemaphoreType.DMA((len(sizes),)),
            pltpu.SemaphoreType.DMA((len(sizes),)),
        ],
        compiler_params=pltpu.CompilerParams(vmem_limit_bytes=LARGE_VMEM_LIMIT),
        cost_estimate=pl.CostEstimate(flops=1024, bytes_accessed=1024, transcendentals=0),
    )(place, value)


def copy_kernel(parts, source, target, sem):
    size = source.shape[0] // parts
    for j in range(parts):
        piece = pl.ds(j * size, size)
        pltpu.make_async_copy(source.at[piece], target.at[piece], sem).start()
    pltpu.make_async_copy(source, target, sem).wait()


def hand_over(value):
    return pl.pallas_call(
        functools.partial(copy_kernel, 16),
        in_specs=[pl.BlockSpec(memory_space=pl.ANY)],
        out_specs=pl.BlockSpec(memory_space=pl.ANY),
        out_shape=jax.ShapeDtypeStruct(value.shape, value.dtype),
        scratch_shapes=[pltpu.SemaphoreType.DMA],
        compiler_params=pltpu.CompilerParams(vmem_limit_bytes=VMEM_LIMIT),
    )(value)


def on_device(a_blocks, a_cols, a_count, b_blocks, b_cols, b_count, c_cols, c_owner):
    devices = lax.axis_size("row") * lax.axis_size("col")
    span = lax.axis_size("col") // 2
    rows, kept = c_cols.shape[1], c_cols.shape[2]
    side = a_blocks.shape[3]
    per_owner = max(2, 3 * rows * kept // (2 * devices))
    first = a_blocks[0].reshape(-1, side, side)
    second = b_blocks[0].reshape(-1, side, side)
    total = second.shape[0]
    large_a, large_b = total * 3 // 8, total * 37 // 80
    spot = lax.axis_index("col") % span
    crossing = (spot == 0).astype(jnp.int32)[None]

    last, middle = span - 1, span - 3

    def near(r, c):
        return r ^ 1, c

    def far(r, c):
        return r ^ 1, c + span

    def at(place, step):
        return lambda r, c: step(r, c) if c % span == place else None

    (cut_first,) = cut(crossing, second, 0, (large_a,))
    part_a = move(cut_first, at(0, near))
    part_b, part_c = cut(crossing, second, large_a, (large_b, total - large_a - large_b))
    part_b = move(part_b, at(0, lambda r, c: far(r, c + last)))
    part_c = move(part_c, at(0, lambda r, c: (r, c + middle)))
    early = move(first, lambda r, c: (r - 1, c) if c % span > 1 else None)
    _, second_sent = lax.optimization_barrier((cut_first, second))
    second_next = move(second_sent, lambda r, c: (r, c - 1) if c % span else None)

    own_first_meta = flat_meta(a_cols[0], a_count[0])
    own_second_meta = flat_meta(b_cols[0], b_count[0])
    kept_columns = c_cols[0].reshape(-1)
    owner = c_owner[0, :, 0]
    before, blank = first_stop(
        own_first_meta, own_second_meta, kept_columns, first, second, devices * per_owner
    )

    part_a, part_c, first, before, blank = lax.optimization_barrier(
        (part_a, part_c, first, before, blank)
    )
    late = move(first, lambda r, c: (r - 1, c) if c % span < 2 else None)
    part_a = move(part_a, at(0, lambda r, c: far(r, c + last)))
    part_c = move(part_c, at(middle, far))
    part_b, part_c = lax.optimization_barrier((part_b, part_c))
    part_b = move(part_b, at(last, near))

    part_a, part_c, early, first_meta = lax.optimization_barrier(
        (part_a, part_c, early, own_first_meta)
    )
    part_c = move(part_c, at(middle, near))
    first_meta = move(first_meta, lambda r, c: (r - 1, c))

    part_c, second_next, second_meta = lax.optimization_barrier(
        (part_c, second_next, own_second_meta)
    )
    second_meta = move(second_meta, lambda r, c: (r, c - 1))
    part_c = move(part_c, at(middle, lambda r, c: (r, c + last - middle)))

    place = jnp.stack([spot == span - 1, spot < 2]).astype(jnp.int32)
    outgoing = last_stop(
        first_meta, second_meta, kept_columns, owner, place,
        early, late, before, second_next, part_a, part_b, part_c, blank, devices,
    )
    arrived = lax.all_to_all(
        outgoing.reshape(devices, per_owner, side, side),
        ("row", "col"),
        split_axis=0,
        concat_axis=0,
        tiled=True,
    )
    return hand_over(arrived).reshape(1, devices, per_owner, side, side)


def solution(mesh):
    return jax.shard_map(
        on_device,
        mesh=mesh,
        in_specs=(
            P("row", "col", None, None, None),
            P("row", "col", None),
            P("row", "col"),
            P("col", "row", None, None, None),
            P("col", "row", None),
            P("col", "row"),
            P("row", "col", None),
            P("row", "col", None),
        ),
        out_specs=P(("row", "col"), None, None, None, None),
        check_vma=False,
    )
```

```python
import functools

import jax
import jax.numpy as jnp
from jax import lax
from jax.experimental import pallas as pl
from jax.experimental.pallas import tpu as pltpu
from jax.sharding import PartitionSpec as P

VMEM_LIMIT = 40 * 1024 * 1024
LARGE_VMEM_LIMIT = 62 * 1024 * 1024
TABLE_ROWS = 20
PIECE = 4
AHEAD = 2


def move(value, chosen):
    rows, cols = lax.axis_size("row"), lax.axis_size("col")
    pairs = []
    for r in range(rows):
        for c in range(cols):
            to = chosen(r, c)
            if to is not None:
                pairs.append((r * cols + c, (to[0] % rows) * cols + to[1] % cols))
    return lax.ppermute(value, ("row", "col"), pairs)


def flat_meta(columns, counts):
    return jnp.concatenate([columns.reshape(-1), counts])


def fill_table(table, meta, slots, width):
    panel_rows = meta.shape[0] // (slots + 1)
    blank = panel_rows * slots

    def clear(n, carry):
        table[n] = blank
        return carry

    lax.fori_loop(0, table.shape[0], clear, 0, unroll=width)
    for k in range(panel_rows):
        count = meta[blank + k]
        columns = [meta[k * slots + b] for b in range(slots)]
        for b in range(slots):
            table[k * width + columns[b]] = jnp.where(b < count, k * slots + b, blank)


def load_pieces(source, target, sem):
    total = source.shape[0]
    for at in range(0, total, PIECE):
        piece = pl.ds(at, min(PIECE, total - at))
        pltpu.make_async_copy(source.at[piece], target.at[piece], sem).start()


def row_products(table, first_meta, kept_columns, i, slots, kept, rows, held, put):
    width = table.shape[0] // (TABLE_ROWS + 1)
    side = held.shape[1]
    row_total = kept_columns.shape[0] // kept
    count = first_meta[row_total * slots + i]

    def over(terms):
        starts = [
            jnp.where(a < count, first_meta[i * slots + a] * width, TABLE_ROWS * width)
            for a in range(terms)
        ]
        left = jnp.concatenate([rows[i * slots + a] for a in range(terms)], axis=1)
        for f in range(0, kept, 2):
            picked = []
            for g in range(2):
                column = kept_columns[i * kept + f + g]
                blocks = [held[table[start + column]] for start in starts]
                picked.append(jnp.concatenate(blocks, axis=0))
            right = jnp.concatenate(picked, axis=1)
            both = jnp.dot(left, right, preferred_element_type=jnp.float32)
            put(f, both[:, :side])
            put(f + 1, both[:, side:])

    fewer = -1
    for terms in (slots // 2, slots * 3 // 4, slots):
        pl.when((count > fewer) & (count <= terms))(functools.partial(over, terms))
        fewer = terms


def first_stop_kernel(
    first_meta, second_meta, kept_columns, first, second,
    total, blank, table, held, rows, zeros, held_sem, row_sem, blank_sem,
):
    i = pl.program_id(0)
    kept = total.shape[1]
    slots = rows.shape[0] * kept // kept_columns.shape[0]
    part = zeros.shape[0]
    panel = held.at[pl.ds(0, second.shape[0])]

    @pl.when(i == 0)
    def _():
        load_pieces(second, panel, held_sem)
        load_pieces(first, rows, row_sem)
        held[second.shape[0]] = jnp.zeros(held.shape[1:], held.dtype)
        zeros[...] = jnp.zeros(zeros.shape, zeros.dtype)
        fill_table(table, second_meta, slots, table.shape[0] // (TABLE_ROWS + 1))
        pltpu.make_async_copy(rows, rows, row_sem).wait()
        pltpu.make_async_copy(panel, panel, held_sem).wait()
        for j in range(blank.shape[0] // part):
            pltpu.make_async_copy(zeros, blank.at[pl.ds(j * part, part)], blank_sem).start()

    def put(f, value):
        total[0, f] = value

    row_products(table, first_meta, kept_columns, i, slots, kept, rows, held, put)

    @pl.when(i == pl.num_programs(0) - 1)
    def _():
        pltpu.make_async_copy(blank, blank, blank_sem).wait()


def last_stop_kernel(
    first_meta, second_meta, kept_columns, owner, place,
    early, late, before, second, part_a, part_b, part_c, blank,
    out, table, used, held, rows, sums, product, held_sem, row_sem, sum_sem, out_sem,
):
    del blank
    i = pl.program_id(0)
    row_total = pl.num_programs(0)
    kept = before.shape[0] // row_total
    slots = rows.shape[0] * kept // kept_columns.shape[0]
    per_owner = out.shape[0] // used.shape[0]
    total = held.shape[0] - 1
    panel = held.at[pl.ds(0, total)]

    def load_row(j):
        row = pl.ds(j * slots, slots)

        @pl.when(place[1] == 0)
        def _():
            load_pieces(early.at[row], rows.at[row], row_sem.at[j])

        @pl.when(place[1] != 0)
        def _():
            load_pieces(late.at[row], rows.at[row], row_sem.at[j])

        row = pl.ds(j * kept, kept)
        load_pieces(before.at[row], sums.at[row], sum_sem.at[j])

    @pl.when(i == 0)
    def _():
        @pl.when(place[0] == 0)
        def _():
            load_pieces(second, panel, held_sem)

        @pl.when(place[0] != 0)
        def _():
            at = 0
            for part in (part_a, part_b, part_c):
                load_pieces(part, held.at[pl.ds(at, part.shape[0])], held_sem)
                at += part.shape[0]

        for j in range(AHEAD):
            load_row(j)

        held[total] = jnp.zeros(held.shape[1:], held.dtype)

        def clear(n, carry):
            used[n] = 0
            return carry

        lax.fori_loop(0, used.shape[0], clear, 0, unroll=16)
        fill_table(table, second_meta, slots, table.shape[0] // (TABLE_ROWS + 1))
        pltpu.make_async_copy(panel, panel, held_sem).wait()

    @pl.when(i + AHEAD < row_total)
    def _():
        load_row(i + AHEAD)

    row = rows.at[pl.ds(i * slots, slots)]
    pltpu.make_async_copy(row, row, row_sem.at[i]).wait()
    row = sums.at[pl.ds(i * kept, kept)]
    pltpu.make_async_copy(row, row, sum_sem.at[i]).wait()

    def put(f, value):
        l = i * kept + f
        product[l] = (value + sums[l]).astype(product.dtype)
        rank = used[owner[l]]
        used[owner[l]] = rank + 1
        slot = owner[l] * per_owner + rank
        pltpu.make_async_copy(product.at[l], out.at[slot], out_sem).start()

    row_products(table, first_meta, kept_columns, i, slots, kept, rows, held, put)

    @pl.when(i == pl.num_programs(0) - 1)
    def _():
        pltpu.make_async_copy(product, out.at[pl.ds(0, product.shape[0])], out_sem).wait()


def first_stop(first_meta, second_meta, kept_columns, first, second, outgoing):
    first_total, side, _ = first.shape
    rows = first_meta.shape[0] - first_total
    kept = kept_columns.shape[0] // rows
    second_total = second.shape[0]
    part = 16
    return pl.pallas_call(
        first_stop_kernel,
        grid_spec=pltpu.PrefetchScalarGridSpec(
            num_scalar_prefetch=3,
            grid=(rows,),
            in_specs=[pl.BlockSpec(memory_space=pl.ANY)] * 2,
            out_specs=[
                pl.BlockSpec((1, kept, side, side), lambda i, *_: (i, 0, 0, 0)),
                pl.BlockSpec(memory_space=pl.ANY),
            ],
            scratch_shapes=[
                pltpu.SMEM(((TABLE_ROWS + 1) * TABLE_ROWS,), jnp.int32),
                pltpu.VMEM((second_total + 1, side, side), second.dtype),
                pltpu.VMEM(first.shape, first.dtype),
                pltpu.VMEM((part, side, side), second.dtype),
                pltpu.SemaphoreType.DMA,
                pltpu.SemaphoreType.DMA,
                pltpu.SemaphoreType.DMA,
            ],
        ),
        out_shape=[
            jax.ShapeDtypeStruct((rows, kept, side, side), jnp.float32),
            jax.ShapeDtypeStruct((outgoing, side, side), second.dtype),
        ],
        compiler_params=pltpu.CompilerParams(vmem_limit_bytes=LARGE_VMEM_LIMIT),
        cost_estimate=pl.CostEstimate(
            flops=400 * first_total * kept * side**3,
            bytes_accessed=2 * (first_total * 2 + rows * kept * 4 + 2 * second_total) * side**2,
            transcendentals=0,
        ),
    )(first_meta, second_meta, kept_columns, first, second)


def last_stop(
    first_meta, second_meta, kept_columns, owner, place,
    early, late, before, second, part_a, part_b, part_c, blank, owners,
):
    side = early.shape[1]
    rows = first_meta.shape[0] - early.shape[0]
    second_total = second.shape[0]
    anywhere = pl.BlockSpec(memory_space=pl.ANY)
    return pl.pallas_call(
        last_stop_kernel,
        grid_spec=pltpu.PrefetchScalarGridSpec(
            num_scalar_prefetch=5,
            grid=(rows,),
            in_specs=[anywhere] * 8,
            out_specs=anywhere,
            scratch_shapes=[
                pltpu.SMEM(((TABLE_ROWS + 1) * TABLE_ROWS,), jnp.int32),
                pltpu.SMEM((owners,), jnp.int32),
                pltpu.VMEM((second_total + 1, side, side), second.dtype),
                pltpu.VMEM(early.shape, early.dtype),
                pltpu.VMEM(before.shape, before.dtype),
                pltpu.VMEM(before.shape, second.dtype),
                pltpu.SemaphoreType.DMA,
                pltpu.SemaphoreType.DMA((rows,)),
                pltpu.SemaphoreType.DMA((rows,)),
                pltpu.SemaphoreType.DMA,
            ],
        ),
        out_shape=jax.ShapeDtypeStruct(blank.shape, blank.dtype),
        input_output_aliases={12: 0},
        compiler_params=pltpu.CompilerParams(vmem_limit_bytes=LARGE_VMEM_LIMIT),
        cost_estimate=pl.CostEstimate(flops=1024, bytes_accessed=1024, transcendentals=0),
    )(
        first_meta, second_meta, kept_columns, owner, place,
        early, late, before, second, part_a, part_b, part_c, blank,
    )


def cut_kernel(start, place, source, *rest):
    held, in_sem, out_sem = rest[-3:]
    targets = rest[:-3]

    @pl.when(place[0] != 0)
    def _():
        loads, stores, at = [], [], 0
        for n, target in enumerate(targets):
            piece, size = pl.ds(start + at, target.shape[0]), pl.ds(at, target.shape[0])
            loads.append(pltpu.make_async_copy(source.at[piece], held.at[size], in_sem.at[n]))
            stores.append(pltpu.make_async_copy(held.at[size], target, out_sem.at[n]))
            at += target.shape[0]
        for load in loads:
            load.start()
        for load, store in zip(loads, stores):
            load.wait()
            store.start()
        for store in stores:
            store.wait()


def cut(place, value, start, sizes):
    return pl.pallas_call(
        functools.partial(cut_kernel, start),
        in_specs=[pl.BlockSpec(memory_space=pltpu.SMEM), pl.BlockSpec(memory_space=pl.ANY)],
        out_specs=[pl.BlockSpec(memory_space=pl.ANY)] * len(sizes),
        out_shape=[jax.ShapeDtypeStruct((size,) + value.shape[1:], value.dtype) for size in sizes],
        scratch_shapes=[
            pltpu.VMEM((sum(sizes),) + value.shape[1:], value.dtype),
            pltpu.SemaphoreType.DMA((len(sizes),)),
            pltpu.SemaphoreType.DMA((len(sizes),)),
        ],
        compiler_params=pltpu.CompilerParams(vmem_limit_bytes=LARGE_VMEM_LIMIT),
        cost_estimate=pl.CostEstimate(flops=1024, bytes_accessed=1024, transcendentals=0),
    )(place, value)


def copy_kernel(parts, source, target, sem):
    size = source.shape[0] // parts
    for j in range(parts):
        piece = pl.ds(j * size, size)
        pltpu.make_async_copy(source.at[piece], target.at[piece], sem).start()
    pltpu.make_async_copy(source, target, sem).wait()


def hand_over(value):
    return pl.pallas_call(
        functools.partial(copy_kernel, 16),
        in_specs=[pl.BlockSpec(memory_space=pl.ANY)],
        out_specs=pl.BlockSpec(memory_space=pl.ANY),
        out_shape=jax.ShapeDtypeStruct(value.shape, value.dtype),
        scratch_shapes=[pltpu.SemaphoreType.DMA],
        compiler_params=pltpu.CompilerParams(vmem_limit_bytes=VMEM_LIMIT),
    )(value)


def on_device(a_blocks, a_cols, a_count, b_blocks, b_cols, b_count, c_cols, c_owner):
    devices = lax.axis_size("row") * lax.axis_size("col")
    span = lax.axis_size("col") // 2
    rows, kept = c_cols.shape[1], c_cols.shape[2]
    side = a_blocks.shape[3]
    per_owner = max(2, 3 * rows * kept // (2 * devices))
    first = a_blocks[0].reshape(-1, side, side)
    second = b_blocks[0].reshape(-1, side, side)
    total = second.shape[0]
    large_a, large_b = total * 17 // 40, total * 13 // 32
    spot = lax.axis_index("col") % span
    crossing = (spot == 0).astype(jnp.int32)[None]

    last, middle = span - 1, span - 3

    def near(r, c):
        return r ^ 1, c

    def far(r, c):
        return r ^ 1, c + span

    def at(place, step):
        return lambda r, c: step(r, c) if c % span == place else None

    (part_a,) = cut(crossing, second, 0, (large_a,))
    part_a = move(part_a, at(0, near))
    part_b, part_c = cut(crossing, second, large_a, (large_b, total - large_a - large_b))
    part_b = move(part_b, at(0, lambda r, c: far(r, c + last)))
    part_c = move(part_c, at(0, lambda r, c: (r, c + middle)))
    early = move(first, lambda r, c: (r - 1, c) if c % span > 1 else None)
    second_next = move(second, lambda r, c: (r, c - 1) if c % span else None)

    own_first_meta = flat_meta(a_cols[0], a_count[0])
    own_second_meta = flat_meta(b_cols[0], b_count[0])
    kept_columns = c_cols[0].reshape(-1)
    owner = c_owner[0, :, 0]
    before, blank = first_stop(
        own_first_meta, own_second_meta, kept_columns, first, second, devices * per_owner
    )

    part_a, part_c, first, before, blank = lax.optimization_barrier(
        (part_a, part_c, first, before, blank)
    )
    late = move(first, lambda r, c: (r - 1, c) if c % span < 2 else None)
    part_a = move(part_a, at(0, lambda r, c: far(r, c + last)))
    part_c = move(part_c, at(middle, far))
    part_b, part_c = lax.optimization_barrier((part_b, part_c))
    part_b = move(part_b, at(last, near))

    part_a, part_c, early, second_next, first_meta, second_meta = lax.optimization_barrier(
        (part_a, part_c, early, second_next, own_first_meta, own_second_meta)
    )
    part_c = move(part_c, at(middle, near))
    first_meta = move(first_meta, lambda r, c: (r - 1, c))
    second_meta = move(second_meta, lambda r, c: (r, c - 1))
    part_c = move(part_c, at(middle, lambda r, c: (r, c + last - middle)))

    place = jnp.stack([spot == span - 1, spot < 2]).astype(jnp.int32)
    outgoing = last_stop(
        first_meta, second_meta, kept_columns, owner, place,
        early, late, before.reshape(-1, side, side), second_next, part_a, part_b, part_c, blank, devices,
    )
    arrived = lax.all_to_all(
        outgoing.reshape(devices, per_owner, side, side),
        ("row", "col"),
        split_axis=0,
        concat_axis=0,
        tiled=True,
    )
    return hand_over(arrived).reshape(1, devices, per_owner, side, side)


def solution(mesh):
    return jax.shard_map(
        on_device,
        mesh=mesh,
        in_specs=(
            P("row", "col", None, None, None),
            P("row", "col", None),
            P("row", "col"),
            P("col", "row", None, None, None),
            P("col", "row", None),
            P("col", "row"),
            P("row", "col", None),
            P("row", "col", None),
        ),
        out_specs=P(("row", "col"), None, None, None, None),
        check_vma=False,
    )
```
